256 devices in a mesh: slab: 16 (over z, core), cross: 16 (over y, x).
Axes of the slice: x: 4, y: 4, z: 8, core: 2. Of those that a mesh axis runs over, the one named last changes fastest.
Arguments:
- forcing: float32 [2, 64, 1024, 512], P(None, 'slab', 'cross'), may hold values from -6 to 6
- viscosity: float32 [64, 1024, 512], P('slab', 'cross'), may hold values from 0.1 to 10
- owner_slot: int32 [512], replicated, may hold values from 0 to 511, each once
Outputs:
- velocity: float32 [2, 64, 1024, 512], P(None, 'slab', 'cross')
- pressure: float32 [64, 512], P('slab', 'cross')
The draws below stay inside these ranges and needn't reach their ends.
All inputs are finite; a program needn't handle non-finite values.
Results may differ from the reference program's by a relative error of at most 0.00013.
Values sent between devices are 32-bit elements; how exact they have to be, the bound alone decides.
No kernel may reach another device: no remote copies, remote signals or barrier semaphores. Data moves between devices by JAX's collectives and lax.ppermute only.
A program may use at most 64 MiB of HBM per device.

```python
import math
import jax
import jax.numpy as jnp

NZ = 512
OUTER = 2
DEGREE = 3
NX = 64
NY = 1024


def draw_forcing(key, part):
    first = jax.random.fold_in(key, 0)
    ramp = 1.0 + 2.0 * jnp.arange(NX, dtype=jnp.float32) / max(NX - 1, 1)
    base = jnp.clip(jax.random.normal(first, (2, NX, NY, NZ), jnp.float32), -2.0, 2.0)
    return base * ramp[None, :, None, None]


def block_scale(key, extent, cuts, low, largest):
    level, own = 1.0, jax.random.fold_in(key, 6)
    for position, parts in cuts:
        heights = jnp.exp(jax.random.uniform(jax.random.fold_in(own, position), (parts,), jnp.float32, low / len(cuts), largest / len(cuts)))
        level = level * jnp.repeat(heights, extent[position] // parts).reshape([-1 if axis == position else 1 for axis in range(len(extent))])
    return level


def setup_inputs(seed: int = 0) -> dict:
    keys = jax.random.split(jax.random.key(seed), 4)
    return {
        "forcing": draw_forcing(jax.random.fold_in(keys[3], 71), 0),
        "viscosity": jnp.clip(jnp.exp(math.log(10.0) - 4.6051702 * jax.random.uniform(keys[1], (NX, NY, NZ), jnp.float32) ** block_scale(keys[1], (NX, NY, NZ), ((0, 16), (1, 16)), -0.2, 0.2)), 0.1, 10.0),
        "owner_slot": jax.random.permutation(keys[2], NZ).astype(jnp.int32),
    }


cheb_theta = 1.025
cheb_delta = 0.975


def face_parts(viscosity):
    rim = jnp.pad(viscosity, 1)
    centre = rim[1:-1, 1:-1, 1:-1]
    neighbours = [rim[2:, 1:-1, 1:-1], rim[:-2, 1:-1, 1:-1], rim[1:-1, 2:, 1:-1], rim[1:-1, :-2, 1:-1], rim[1:-1, 1:-1, 2:], rim[1:-1, 1:-1, :-2]]
    faces = [0.5 * (centre + nb) for nb in neighbours]
    diag = faces[0] + faces[1] + faces[2] + faces[3] + faces[4] + faces[5]
    return faces, diag


def apply_op(field, faces):
    padded = jnp.pad(field, ((0, 0), (1, 1), (1, 1), (1, 1)))
    neighbours = [padded[:, 2:, 1:-1, 1:-1], padded[:, :-2, 1:-1, 1:-1], padded[:, 1:-1, 2:, 1:-1], padded[:, 1:-1, :-2, 1:-1], padded[:, 1:-1, 1:-1, 2:], padded[:, 1:-1, 1:-1, :-2]]
    result = jnp.zeros_like(field)
    for face, nb in zip(faces, neighbours):
        result = result + face[None] * (field - nb)
    return result


def velocity_solve(rhs, faces, diag):
    sigma = cheb_theta / cheb_delta
    solved = rhs / (cheb_theta * diag[None])
    change = solved
    rho_prev = 1.0 / sigma
    for step in range(DEGREE - 1):
        resid = rhs - apply_op(solved, faces)
        rho = 1.0 / (2.0 * sigma - rho_prev)
        change = rho * rho_prev * change + (2.0 * rho / cheb_delta) * resid / diag[None]
        solved = solved + change
        rho_prev = rho
    return solved


def diverge(field, owner_slot):
    col_x = jnp.sum(field[0], axis=1)
    col_z = jnp.sum(field[1], axis=1)
    below = jnp.pad(col_x[:-1], ((1, 0), (0, 0)))
    behind = jnp.pad(col_z[:, :-1], ((0, 0), (1, 0)))
    local = col_x - below + col_z - behind
    return jnp.zeros_like(local).at[:, owner_slot].set(local)


def gradient(press, owner_slot, ny):
    column = press[:, owner_slot]
    grad_x = column - jnp.pad(column[1:], ((0, 1), (0, 0)))
    grad_z = column - jnp.pad(column[:, 1:], ((0, 0), (0, 1)))
    both = jnp.stack([grad_x, grad_z])[:, :, None, :]
    return jnp.broadcast_to(both, (2, column.shape[0], ny, column.shape[1]))


def reference(forcing, viscosity, owner_slot):
    faces, diag = face_parts(viscosity)
    ny = viscosity.shape[1]
    target = diverge(velocity_solve(forcing, faces, diag), owner_slot)
    pressure = jnp.zeros_like(target)
    resid = target
    dirn = target
    rr = jnp.sum(resid * resid)
    for step in range(OUTER):
        image = diverge(velocity_solve(gradient(dirn, owner_slot, ny), faces, diag), owner_slot)
        alpha = rr / jnp.sum(dirn * image)
        pressure = pressure + alpha * dirn
        if step + 1 < OUTER:
            resid = resid - alpha * image
            fresh = jnp.sum(resid * resid)
            dirn = resid + (fresh / rr) * dirn
            rr = fresh
    velocity = velocity_solve(forcing - gradient(pressure, owner_slot, ny), faces, diag)
    return velocity, pressure
```

```python
import functools

import jax
import jax.numpy as jnp
from jax import lax
from jax.experimental import pallas as pl
from jax.experimental.pallas import tpu as pltpu
from jax.sharding import PartitionSpec as P

OUTER = 2
DEGREE = 3
cheb_theta = 1.025
cheb_delta = 0.975


def series():
    sigma = cheb_theta / cheb_delta
    rho0 = 1.0 / sigma
    rho1 = 1.0 / (2.0 * sigma - rho0)
    rho2 = 1.0 / (2.0 * sigma - rho1)
    g1, g2 = 2.0 * rho1 / cheb_delta, 2.0 * rho2 / cheb_delta
    p0, p1 = (1.0 + rho1 * rho0) / cheb_theta + g1, -g1 / cheb_theta
    q = rho2 * rho1
    c0 = (1.0 + q) * p0 - q / cheb_theta + g2
    c1 = (1.0 + q) * p1 - g2 * p0
    c2 = -g2 * p1
    return c0 + c1 + c2, -c1 - 2.0 * c2, c2


E0, E1, E2 = (2.0 * e for e in series())

NY, NZ = 64, 512
ROWS = 4
FRAME = 80
LO, HI = 8, 72
FORWARD = ((0, 0), (0, 1), (0, 2), (1, -1), (1, 0), (1, 1), (2, 0))
PAYLOAD = 40


def up_z(x):
    return pltpu.roll(x, NZ - 1, x.ndim - 1)


def down_z(x):
    return pltpu.roll(x, 1, x.ndim - 1)


def lane(shape):
    return lax.broadcasted_iota(jnp.int32, shape, len(shape) - 1)


def fill_viscosity(par, v, own, od, ev, lo, hi, od_c, ev_c):
    v[...] = jnp.zeros_like(v)
    v[3:7, LO:HI] = own[...]
    v[3:7, LO - 3 : LO] = lo[:, 0:3]
    v[3:7, HI : HI + 3] = hi[:, 0:3]
    od_at = par * 7
    ev_at = 7 - par * 7
    v[pl.ds(od_at, 3), LO:HI] = od[...]
    v[pl.ds(ev_at, 3), LO:HI] = ev[...]
    for at, c in ((od_at, od_c), (ev_at, ev_c)):
        v[pl.ds(at, 3), LO - 3 : LO] = c[:, 0:3]
        v[pl.ds(at, 3), HI : HI + 3] = c[:, 7:10]


def fill_inverse(v, d, fz):
    ids = lane((FRAME, NZ))

    def layer(r, _):
        mid = v[r + 1]
        nxt = jnp.where(ids == NZ - 1, 0.0, up_z(mid))
        prv = jnp.where(ids == 0, 0.0, down_z(mid))
        total = 6.0 * mid + v[r] + v[r + 2] + nxt + prv
        total = total + pltpu.roll(mid, 1, 0) + pltpu.roll(mid, FRAME - 1, 0)
        d[r] = jnp.where(mid > 0.0, 1.0 / total, 0.0)
        fz[r] = jnp.where(ids == NZ - 1, 0.0, mid + nxt)
        return 0

    lax.fori_loop(0, 8, layer, 0)


def stencil_kernel(par_ref, own, od, ev, lo, hi, od_c, ev_c, f, out, v, d, fz, h0, ex, ez, ezm, acc):
    fill_viscosity(par_ref[0], v, own, od, ev, lo, hi, od_c, ev_c)
    fill_inverse(v, d, fz)

    def edges(r, _):
        dm, vm = d[r], v[r + 1]
        ex[r] = E2 * dm * (vm + v[r + 2]) * d[r + 1]
        dy = pltpu.roll(dm, FRAME - 1, 0)
        ey = E2 * dm * (vm + pltpu.roll(vm, FRAME - 1, 0)) * dy
        h0[r] = E1 * dm + ey + pltpu.roll(ey, 1, 0)
        e = E2 * dm * fz[r] * up_z(dm)
        ez[r] = e
        ezm[r] = down_z(e)
        return 0

    lax.fori_loop(0, 7, edges, 0)

    acc[...] = jnp.zeros_like(acc)
    own_rows = slice(LO, HI)
    above = slice(LO + 1, HI + 1)
    under = slice(LO - 1, HI - 1)

    def layer(i, _):
        r = i + 2
        vm = v[r + 1, own_rows]
        fyp = vm + v[r + 1, above]
        fym = vm + v[r + 1, under]
        fxp = vm + v[r + 2, own_rows]
        fxm = vm + v[r, own_rows]
        fzp = fz[r, own_rows]
        fzm = down_z(fzp)
        dm = d[r, own_rows]
        u0, u1 = dm * f[0, i], dm * f[1, i]

        def weigh(di, dk, s):
            for c, u in ((0, u0), (1, u1)):
                row = jnp.sum(u * s, axis=0, keepdims=True)
                if dk:
                    row = pltpu.roll(row, dk % NZ, 1)
                at = pl.ds(16 * c + i + di + 2, 1)
                acc[at] = acc[at] + row[None]
            if (di, dk) in FORWARD:
                out[FORWARD.index((di, dk)), pl.ds(i, 1)] = jnp.sum(dm * s, axis=0, keepdims=True)

        exi, exm = ex[r, own_rows], ex[r - 1, own_rows]
        ezi, ezmi = ez[r, own_rows], ezm[r, own_rows]
        h = h0[r, own_rows]
        weigh(
            0,
            0,
            E0
            + fyp * h0[r, above]
            + fym * h0[r, under]
            + fxp * exi
            + fxm * exm
            + fzp * ezi
            + fzm * ezmi,
        )
        weigh(1, 0, fyp * ex[r, above] + fym * ex[r, under] + fxp * h0[r + 1, own_rows])
        weigh(-1, 0, fyp * ex[r - 1, above] + fym * ex[r - 1, under] + fxm * h0[r - 1, own_rows])
        weigh(0, 1, fyp * ez[r, above] + fym * ez[r, under] + fzp * up_z(h))
        weigh(0, -1, fyp * ezm[r, above] + fym * ezm[r, under] + fzm * down_z(h))
        weigh(2, 0, fxp * ex[r + 1, own_rows])
        weigh(-2, 0, fxm * ex[r - 2, own_rows])
        weigh(0, 2, fzp * up_z(ezi))
        weigh(0, -2, fzm * down_z(ezmi))
        weigh(1, 1, fxp * ez[r + 1, own_rows] + fzp * up_z(exi))
        weigh(1, -1, fxp * ezm[r + 1, own_rows] + fzm * down_z(exi))
        weigh(-1, 1, fxm * ez[r - 1, own_rows] + fzp * up_z(exm))
        weigh(-1, -1, fxm * ezm[r - 1, own_rows] + fzm * down_z(exm))
        return 0

    lax.fori_loop(0, ROWS, layer, 0)

    cx = acc[0:16, 0]
    cz = acc[16:32, 0]
    zero = lane((16, NZ)) == 0
    e = cx - pltpu.roll(cx, 1, 0) + cz - jnp.where(zero, 0.0, down_z(cz))
    out[7:9] = e[0:8].reshape(2, 4, NZ)
    out[9, 0:1] = e[8:9]
    out[9, 1:4] = jnp.zeros((3, NZ), jnp.float32)


def krylov_kernel(par_ref, mine, mate, below_mine, below_mate, above_mine, above_mate, basis, dots, s_ref, g_ref):
    par, chip = par_ref[0], par_ref[1]
    odd = par == 1

    def pair(a, b):
        return lax.select(odd, b, a), lax.select(odd, a, b)

    slabs = []
    for a, b in ((below_mine, below_mate), (mine, mate), (above_mine, above_mate)):
        slabs += pair(a[...], b[...])
    W = 24
    g_ref[...] = jnp.zeros_like(g_ref)
    for n, slab in enumerate(slabs):
        for o in range(7):
            s_ref[o, 4 * n : 4 * n + 4] = slab[o]
        flat = slab[7:10].reshape(12, NZ)[0:9]
        at = 8 + 4 * n - 2
        g_ref[at : at + 9] = g_ref[at : at + 9] + flat
    ids = lane((W, NZ))
    layer = lax.broadcasted_iota(jnp.int32, (W, NZ), 0) - 8 + 8 * chip
    inside = jnp.logical_and(layer >= 0, layer < 64)

    def next_layer(x, n=1):
        return pltpu.roll(x, (W - n) % W, 0)

    def shift(x, di, dk):
        if di:
            x = pltpu.roll(x, (-di) % W, 0)
        if dk:
            x = pltpu.roll(x, (-dk) % NZ, 1)
        return x

    def spread(q):
        qx = q - next_layer(q)
        qz = q - jnp.where(ids == NZ - 1, 0.0, up_z(q))
        return qx, qz

    def times_s(b):
        total = None
        for n, (di, dk) in enumerate(FORWARD):
            s = s_ref[n]
            if n == 0:
                total = s * b
            else:
                total = total + s * shift(b, di, dk) + shift(s * b, -di, -dk)
        return total

    g = jnp.where(inside, g_ref[8 : 8 + W], 0.0)
    gx, gz = spread(g)
    tx, tz = times_s(gx), times_s(gz)
    h = tx - pltpu.roll(tx, 1, 0) + tz - jnp.where(ids == 0, 0.0, down_z(tz))
    h = jnp.where(inside, h, 0.0)
    hx, hz = spread(h)
    energy = hx * times_s(hx) + hz * times_s(hz)

    def own(x):
        return lax.select(odd, pltpu.roll(x, W - 4, 0), x)

    for n, x in enumerate((gx, gz, hx, hz)):
        basis[8 * n : 8 * n + 8] = own(x)[6:14]
    basis[32:40] = own(g)[8:16]
    basis[40:48] = own(h)[8:16]
    rows = []
    for x in (g * g, g * h, h * h, energy):
        part = x[8:16]
        part = part[:, 0:128] + part[:, 128:256] + part[:, 256:384] + part[:, 384:512]
        rows.append(jnp.sum(part, axis=0, keepdims=True))
    dots[...] = jnp.concatenate(rows + [jnp.zeros((4, 128), jnp.float32)], 0)


def velocity_kernel(
    par_ref, own, od, ev, lo, hi, od_c, ev_c, f, od_f, ev_f, basis, dots, onehot, vel, press, v, d, fz, u, t, b
):
    par = par_ref[0]
    fill_viscosity(par, v, own, od, ev, lo, hi, od_c, ev_c)
    fill_inverse(v, d, fz)

    sums = jnp.sum(jnp.sum(dots[...], axis=0), axis=1, keepdims=True)
    gg, gh, hh, hkh = sums[0:1], sums[1:2], sums[2:3], sums[3:4]
    alpha0 = gg / gh
    fresh = gg - 2.0 * alpha0 * gh + alpha0 * alpha0 * hh
    beta = fresh / gg
    grow = 1.0 + beta
    alpha1 = fresh / (grow * grow * gh - 2.0 * grow * alpha0 * hh + alpha0 * alpha0 * hkh)
    on_g = alpha0 + alpha1 * grow
    on_h = alpha1 * alpha0
    b[0:16] = on_g * basis[0:16] - on_h * basis[16:32]
    p = on_g * basis[32:40] - on_h * basis[40:48]
    press[...] = jnp.dot(
        p, onehot[...], precision=lax.Precision.HIGHEST, preferred_element_type=jnp.float32
    )[0:4]

    u[...] = jnp.zeros_like(u)
    od_at, ev_at = par * 6, 6 - par * 6
    for c in range(2):
        u[c, 2:6, LO:HI] = f[c]
        u[c, 2:6, LO - 2 : LO] = lo[:, 3 + 2 * c : 5 + 2 * c]
        u[c, 2:6, HI : HI + 2] = hi[:, 3 + 2 * c : 5 + 2 * c]
        u[c, pl.ds(od_at, 2), LO:HI] = od_f[c]
        u[c, pl.ds(ev_at, 2), LO:HI] = ev_f[c]
        for at, first, corner in ((od_at, 1 - par, od_c), (ev_at, par, ev_c)):
            u[c, pl.ds(at, 2), LO - 2 : LO] = corner[pl.ds(first, 2), 3 + 2 * c : 5 + 2 * c]
            u[c, pl.ds(at, 2), HI : HI + 2] = corner[pl.ds(first, 2), 10 + 2 * c : 12 + 2 * c]

    def scale(r, _):
        dm = d[r]
        u[0, r] = dm * (u[0, r] - b[pl.ds(r, 1)])
        u[1, r] = dm * (u[1, r] - b[pl.ds(8 + r, 1)])
        return 0

    lax.fori_loop(0, 8, scale, 0)

    def first(r, _):
        vm = v[r + 1]
        fy = vm + pltpu.roll(vm, FRAME - 1, 0)
        fxp, fxm = vm + v[r + 2], vm + v[r]
        fzp, dm = fz[r], d[r]
        for c in range(2):
            x = u[c, r]
            y = fy * pltpu.roll(x, FRAME - 1, 0) + pltpu.roll(fy * x, 1, 0)
            y = y + fxp * u[c, r + 1] + fxm * u[c, r - 1]
            y = y + fzp * up_z(x) + down_z(fzp * x)
            t[c, r] = E1 * x + E2 * (dm * y)
        return 0

    lax.fori_loop(1, 7, first, 0)

    own_rows = slice(LO, HI)
    above = slice(LO + 1, HI + 1)
    under = slice(LO - 1, HI - 1)

    def second(i, _):
        r = i + 2
        vm = v[r + 1, own_rows]
        fyp = vm + v[r + 1, above]
        fym = vm + v[r + 1, under]
        fxp, fxm = vm + v[r + 2, own_rows], vm + v[r, own_rows]
        fzp, dm = fz[r, own_rows], d[r, own_rows]
        for c in range(2):
            x = t[c, r, own_rows]
            y = fyp * t[c, r, above] + fym * t[c, r, under]
            y = y + fxp * t[c, r + 1, own_rows] + fxm * t[c, r - 1, own_rows]
            y = y + fzp * up_z(x) + down_z(fzp * x)
            vel[c, i] = E0 * u[c, r, own_rows] + dm * y
        return 0

    lax.fori_loop(0, ROWS, second, 0)


def call(kernel, out_shape, scratch, args, smem=1):
    vmem = pl.BlockSpec(memory_space=pltpu.VMEM)
    specs = [pl.BlockSpec(memory_space=pltpu.SMEM)] * smem + [vmem] * (len(args) - smem)
    return pl.pallas_call(
        kernel,
        out_shape=out_shape,
        in_specs=specs,
        out_specs=jax.tree.map(lambda _: vmem, out_shape),
        scratch_shapes=[pltpu.VMEM(s, jnp.float32) for s in scratch],
        compiler_params=pltpu.CompilerParams(vmem_limit_bytes=48 * 1024 * 1024),
    )(*args)


def f32(*shape):
    return jax.ShapeDtypeStruct(shape, jnp.float32)


def shards(forcing, viscosity, owner_slot):
    slabs, cross = lax.axis_size("slab"), lax.axis_size("cross")
    slab = lax.axis_index("slab")
    par = slab % 2
    where = jnp.stack([par, slab // 2]).astype(jnp.int32)
    mates = [(i, i ^ 1) for i in range(slabs)]
    others = [(i, i + 1) for i in range(1, slabs - 1, 2)]
    others = others + [(b, a) for a, b in others]
    up = [(i, i + 1) for i in range(cross - 1)]
    down = [(b, a) for a, b in up]
    chips = slabs // 2
    chip_up = [(i, (i + 2) % slabs) for i in range(slabs) if i + 2 < slabs]
    chip_down = [(b, a) for a, b in chip_up]

    def sides(x, n):
        last, initial = x[..., x.shape[-3] - n :, :, :], x[..., :n, :, :]
        odd = par == 1
        return jnp.where(odd, last, initial), jnp.where(odd, initial, last)

    to_od, to_ev = sides(viscosity, 3)
    od = lax.ppermute(to_od, "slab", others)
    ev = lax.ppermute(to_ev, "slab", mates)
    edge_hi = jnp.concatenate([viscosity[:, -3:], forcing[0, :, -2:], forcing[1, :, -2:]], 1)
    edge_lo = jnp.concatenate([viscosity[:, :3], forcing[0, :, :2], forcing[1, :, :2]], 1)
    lo = lax.ppermute(edge_hi, "cross", up)
    hi = lax.ppermute(edge_lo, "cross", down)
    to_od, to_ev = sides(jnp.concatenate([lo, hi], 1), 3)
    od_c = lax.ppermute(to_od, "slab", others)
    ev_c = lax.ppermute(to_ev, "slab", mates)

    grid = (viscosity, od, ev, lo, hi, od_c, ev_c)
    part = call(
        stencil_kernel,
        f32(10, 4, NZ),
        [(10, FRAME, NZ)] + [(8, FRAME, NZ)] * 2 + [(7, FRAME, NZ)] * 4 + [(32, 1, NZ)],
        (where, *grid, forcing),
    )

    part, forced = lax.optimization_barrier((part, forcing))
    to_od, to_ev = sides(forced, 2)
    od_f = lax.ppermute(to_od, "slab", others)
    ev_f = lax.ppermute(to_ev, "slab", mates)

    for step in (1, 4):
        part = sum(
            (lax.ppermute(part, "cross", [(i, i ^ (n * step)) for i in range(cross)]) for n in (1, 2, 3)), part
        )

    mate = lax.ppermute(part, "slab", mates)
    both = jnp.stack([part, mate])
    below = lax.ppermute(both, "slab", chip_up)
    above = lax.ppermute(both, "slab", chip_down)
    basis, dots = call(
        krylov_kernel,
        (f32(48, NZ), f32(8, 128)),
        [(7, 24, NZ), (40, NZ)],
        (where, part, mate, below[0], below[1], above[0], above[1]),
    )
    groups = [[2 * z + c for z in range(chips)] for c in range(2)]
    dots = lax.all_to_all(
        jnp.broadcast_to(dots[None], (chips, 8, 128)), "slab", 0, 0, tiled=True, axis_index_groups=groups
    )

    width = owner_slot.shape[0] // cross
    column = lax.axis_index("cross") * width + jnp.arange(width, dtype=jnp.int32)
    onehot = (owner_slot[:, None] == column[None, :]).astype(jnp.float32)
    return call(
        velocity_kernel,
        (f32(2, ROWS, NY, NZ), f32(ROWS, width)),
        [(10, FRAME, NZ)] + [(8, FRAME, NZ)] * 2 + [(2, 8, FRAME, NZ)] * 2 + [(16, NZ)],
        (where, *grid, forcing, od_f, ev_f, basis, dots, onehot),
    )


def solution(mesh):
    in_specs = (P(None, "slab", "cross", None), P("slab", "cross", None), P())
    out_specs = (P(None, "slab", "cross", None), P("slab", "cross"))
    return jax.shard_map(shards, mesh=mesh, in_specs=in_specs, out_specs=out_specs, check_vma=False)
```

```python
import functools

import jax
import jax.numpy as jnp
from jax import lax
from jax.experimental import pallas as pl
from jax.experimental.pallas import tpu as pltpu
from jax.sharding import PartitionSpec as P

OUTER = 2
DEGREE = 3
cheb_theta = 1.025
cheb_delta = 0.975


def series():
    sigma = cheb_theta / cheb_delta
    rho0 = 1.0 / sigma
    rho1 = 1.0 / (2.0 * sigma - rho0)
    rho2 = 1.0 / (2.0 * sigma - rho1)
    g1, g2 = 2.0 * rho1 / cheb_delta, 2.0 * rho2 / cheb_delta
    p0, p1 = (1.0 + rho1 * rho0) / cheb_theta + g1, -g1 / cheb_theta
    q = rho2 * rho1
    c0 = (1.0 + q) * p0 - q / cheb_theta + g2
    c1 = (1.0 + q) * p1 - g2 * p0
    c2 = -g2 * p1
    return c0 + c1 + c2, -c1 - 2.0 * c2, c2


E0, E1, E2 = (2.0 * e for e in series())

NY, NZ = 64, 512
ROWS = 4
FRAME = 80
LO, HI = 8, 72
FORWARD = ((0, 0), (0, 1), (0, 2), (1, -1), (1, 0), (1, 1), (2, 0))
PAYLOAD = 40


def up_z(x):
    return pltpu.roll(x, NZ - 1, x.ndim - 1)


def down_z(x):
    return pltpu.roll(x, 1, x.ndim - 1)


def lane(shape):
    return lax.broadcasted_iota(jnp.int32, shape, len(shape) - 1)


def fill_viscosity(par, v, own, od, ev, lo, hi, od_c, ev_c, sems):
    copies = [pltpu.make_async_copy(own, v.at[3:7, LO:HI], sems.at[0])]
    for n, at, first, x in ((1, par * 7, 1 - par, od), (2, 7 - par * 7, par, ev)):
        copies.append(pltpu.make_async_copy(x.at[pl.ds(first, 3)], v.at[pl.ds(at, 3), LO:HI], sems.at[n]))
    for copy in copies:
        copy.start()
    v[3:7, LO - 3 : LO] = lo[:, 0:3]
    v[3:7, HI : HI + 3] = hi[:, 0:3]
    for at, first, c in ((par * 7, 1 - par, od_c), (7 - par * 7, par, ev_c)):
        v[pl.ds(at, 3), LO - 3 : LO] = c[pl.ds(first, 3), 0:3]
        v[pl.ds(at, 3), HI : HI + 3] = c[pl.ds(first, 3), 7:10]
    for copy in copies:
        copy.wait()


def fill_inverse(v, d, fz):
    ids = lane((FRAME, NZ))

    def layer(r, _):
        mid = v[r + 1]
        nxt = jnp.where(ids == NZ - 1, 0.0, up_z(mid))
        prv = jnp.where(ids == 0, 0.0, down_z(mid))
        total = 6.0 * mid + v[r] + v[r + 2] + nxt + prv
        total = total + pltpu.roll(mid, 1, 0) + pltpu.roll(mid, FRAME - 1, 0)
        d[r] = jnp.where(mid > 0.0, 1.0 / total, 0.0)
        fz[r] = jnp.where(ids == NZ - 1, 0.0, mid + nxt)
        return 0

    lax.fori_loop(0, 8, layer, 0)


def stencil_kernel(
    par_ref, own, od, ev, lo, hi, od_c, ev_c, f_hbm, out, to_od, to_ev, *rest
):
    kept_hbm, (v, d, fz, h0, ex, ez, ezm, acc, f, sems) = rest[:6], rest[6:]
    par = par_ref[0]
    moves = [
        pltpu.make_async_copy(f_hbm, f, sems.at[3]),
        pltpu.make_async_copy(f_hbm.at[:, pl.ds(2 * par, 2)], to_od, sems.at[4]),
        pltpu.make_async_copy(f_hbm.at[:, pl.ds(2 - 2 * par, 2)], to_ev, sems.at[5]),
    ]
    moves[0].start()
    fill_viscosity(par, v, own, od, ev, lo, hi, od_c, ev_c, sems)
    moves[1].start()
    moves[2].start()
    fill_inverse(v, d, fz)

    def edges(r, _):
        dm, vm = d[r], v[r + 1]
        ex[r] = E2 * dm * (vm + v[r + 2]) * d[r + 1]
        dy = pltpu.roll(dm, FRAME - 1, 0)
        ey = E2 * dm * (vm + pltpu.roll(vm, FRAME - 1, 0)) * dy
        h0[r] = E1 * dm + ey + pltpu.roll(ey, 1, 0)
        e = E2 * dm * fz[r] * up_z(dm)
        ez[r] = e
        ezm[r] = down_z(e)
        return 0

    lax.fori_loop(0, 7, edges, 0)

    saves = [pltpu.make_async_copy(x, y, sems.at[6 + n]) for n, (x, y) in enumerate(zip((v, d, fz, h0, ex, ez), kept_hbm))]
    for copy in saves:
        copy.start()
    moves[0].wait()
    acc[...] = jnp.zeros_like(acc)
    own_rows = slice(LO, HI)
    above = slice(LO + 1, HI + 1)
    under = slice(LO - 1, HI - 1)

    def layer(i, _):
        r = i + 2
        vm = v[r + 1, own_rows]
        fyp = vm + v[r + 1, above]
        fym = vm + v[r + 1, under]
        fxp = vm + v[r + 2, own_rows]
        fxm = vm + v[r, own_rows]
        fzp = fz[r, own_rows]
        fzm = down_z(fzp)
        dm = d[r, own_rows]
        u0, u1 = dm * f[0, i], dm * f[1, i]

        def weigh(di, dk, s):
            for c, u in ((0, u0), (1, u1)):
                row = jnp.sum(u * s, axis=0, keepdims=True)
                if dk:
                    row = pltpu.roll(row, dk % NZ, 1)
                at = pl.ds(16 * c + i + di + 2, 1)
                acc[at] = acc[at] + row[None]
            if (di, dk) in FORWARD:
                out[FORWARD.index((di, dk)), pl.ds(i, 1)] = jnp.sum(dm * s, axis=0, keepdims=True)

        exi, exm = ex[r, own_rows], ex[r - 1, own_rows]
        ezi, ezmi = ez[r, own_rows], ezm[r, own_rows]
        h = h0[r, own_rows]
        weigh(
            0,
            0,
            E0
            + fyp * h0[r, above]
            + fym * h0[r, under]
            + fxp * exi
            + fxm * exm
            + fzp * ezi
            + fzm * ezmi,
        )
        weigh(1, 0, fyp * ex[r, above] + fym * ex[r, under] + fxp * h0[r + 1, own_rows])
        weigh(-1, 0, fyp * ex[r - 1, above] + fym * ex[r - 1, under] + fxm * h0[r - 1, own_rows])
        weigh(0, 1, fyp * ez[r, above] + fym * ez[r, under] + fzp * up_z(h))
        weigh(0, -1, fyp * ezm[r, above] + fym * ezm[r, under] + fzm * down_z(h))
        weigh(2, 0, fxp * ex[r + 1, own_rows])
        weigh(-2, 0, fxm * ex[r - 2, own_rows])
        weigh(0, 2, fzp * up_z(ezi))
        weigh(0, -2, fzm * down_z(ezmi))
        weigh(1, 1, fxp * ez[r + 1, own_rows] + fzp * up_z(exi))
        weigh(1, -1, fxp * ezm[r + 1, own_rows] + fzm * down_z(exi))
        weigh(-1, 1, fxm * ez[r - 1, own_rows] + fzp * up_z(exm))
        weigh(-1, -1, fxm * ezm[r - 1, own_rows] + fzm * down_z(exm))
        return 0

    lax.fori_loop(0, ROWS, layer, 0)

    cx = acc[0:16, 0]
    cz = acc[16:32, 0]
    zero = lane((16, NZ)) == 0
    e = cx - pltpu.roll(cx, 1, 0) + cz - jnp.where(zero, 0.0, down_z(cz))
    out[7:9] = e[0:8].reshape(2, 4, NZ)
    out[9, 0:1] = e[8:9]
    out[9, 1:4] = jnp.zeros((3, NZ), jnp.float32)
    for copy in moves[1:] + saves:
        copy.wait()


def krylov_kernel(par_ref, mine, mate, below_mine, below_mate, above_mine, above_mate, basis, dots, s_ref, g_ref):
    par, chip = par_ref[0], par_ref[1]
    odd = par == 1

    def pair(a, b):
        return lax.select(odd, b, a), lax.select(odd, a, b)

    slabs = []
    for a, b in ((below_mine, below_mate), (mine, mate), (above_mine, above_mate)):
        slabs += pair(a[...], b[...])
    W = 24
    g_ref[...] = jnp.zeros_like(g_ref)
    for n, slab in enumerate(slabs):
        for o in range(7):
            s_ref[o, 4 * n : 4 * n + 4] = slab[o]
        flat = slab[7:10].reshape(12, NZ)[0:9]
        at = 8 + 4 * n - 2
        g_ref[at : at + 9] = g_ref[at : at + 9] + flat
    ids = lane((W, NZ))
    layer = lax.broadcasted_iota(jnp.int32, (W, NZ), 0) - 8 + 8 * chip
    inside = jnp.logical_and(layer >= 0, layer < 64)

    def next_layer(x, n=1):
        return pltpu.roll(x, (W - n) % W, 0)

    def shift(x, di, dk):
        if di:
            x = pltpu.roll(x, (-di) % W, 0)
        if dk:
            x = pltpu.roll(x, (-dk) % NZ, 1)
        return x

    def spread(q):
        qx = q - next_layer(q)
        qz = q - jnp.where(ids == NZ - 1, 0.0, up_z(q))
        return qx, qz

    def times_s(b):
        total = None
        for n, (di, dk) in enumerate(FORWARD):
            s = s_ref[n]
            if n == 0:
                total = s * b
            else:
                total = total + s * shift(b, di, dk) + shift(s * b, -di, -dk)
        return total

    g = jnp.where(inside, g_ref[8 : 8 + W], 0.0)
    gx, gz = spread(g)
    tx, tz = times_s(gx), times_s(gz)
    h = tx - pltpu.roll(tx, 1, 0) + tz - jnp.where(ids == 0, 0.0, down_z(tz))
    h = jnp.where(inside, h, 0.0)
    hx, hz = spread(h)
    energy = hx * times_s(hx) + hz * times_s(hz)

    def own(x):
        return lax.select(odd, pltpu.roll(x, W - 4, 0), x)

    for n, x in enumerate((gx, gz, hx, hz)):
        basis[8 * n : 8 * n + 8] = own(x)[6:14]
    basis[32:40] = own(g)[8:16]
    basis[40:48] = own(h)[8:16]
    rows = []
    for x in (g * g, g * h, h * h, energy):
        part = x[8:16]
        part = part[:, 0:128] + part[:, 128:256] + part[:, 256:384] + part[:, 384:512]
        rows.append(jnp.sum(part, axis=0, keepdims=True))
    packed = jnp.concatenate(rows + [jnp.zeros((4, 128), jnp.float32)], 0)
    dots[...] = jnp.broadcast_to(packed[None], dots.shape)


def forced_kernel(
    par_ref, f, od_f, ev_f, lo, hi, od_c, ev_c, v_hbm, d_hbm, fz_hbm, out, v, d, fz, u, t, sems
):
    par = par_ref[0]
    copies = [pltpu.make_async_copy(x, y, sems.at[n]) for n, (x, y) in enumerate(((d_hbm, d), (v_hbm, v), (fz_hbm, fz)))]
    for c in range(2):
        copies.append(pltpu.make_async_copy(f.at[c], u.at[c, 2:6, LO:HI], sems.at[3 + c]))
    copies.append(pltpu.make_async_copy(od_f, u.at[:, pl.ds(par * 6, 2), LO:HI], sems.at[5]))
    copies.append(pltpu.make_async_copy(ev_f, u.at[:, pl.ds(6 - par * 6, 2), LO:HI], sems.at[6]))
    for copy in copies:
        copy.start()
    for c in range(2):
        u[c, 2:6, LO - 2 : LO] = lo[:, 3 + 2 * c : 5 + 2 * c]
        u[c, 2:6, HI : HI + 2] = hi[:, 3 + 2 * c : 5 + 2 * c]
        for at, first, corner in ((par * 6, 2 - 2 * par, od_c), (6 - par * 6, 2 * par, ev_c)):
            u[c, pl.ds(at, 2), LO - 2 : LO] = corner[pl.ds(first, 2), 3 + 2 * c : 5 + 2 * c]
            u[c, pl.ds(at, 2), HI : HI + 2] = corner[pl.ds(first, 2), 10 + 2 * c : 12 + 2 * c]
    for copy in copies:
        copy.wait()

    def scale(r, _):
        dm = d[r]
        u[0, r] = dm * u[0, r]
        u[1, r] = dm * u[1, r]
        return 0

    lax.fori_loop(0, 8, scale, 0)

    def first(r, _):
        vm = v[r + 1]
        fy = vm + pltpu.roll(vm, FRAME - 1, 0)
        fxp, fxm = vm + v[r + 2], vm + v[r]
        fzp, dm = fz[r], d[r]
        for c in range(2):
            x = u[c, r]
            y = fy * pltpu.roll(x, FRAME - 1, 0) + pltpu.roll(fy * x, 1, 0)
            y = y + fxp * u[c, r + 1] + fxm * u[c, r - 1]
            y = y + fzp * up_z(x) + down_z(fzp * x)
            t[c, r] = E1 * x + E2 * (dm * y)
        return 0

    lax.fori_loop(1, 7, first, 0)

    def second(i, _):
        couple(i, v, d, fz, t, lambda c, y: store(c, i, y))
        return 0

    def store(c, i, y):
        out[c, i] = E0 * u[c, i + 2, LO:HI] + y

    lax.fori_loop(0, ROWS, second, 0)


def couple(i, v, d, fz, t, done):
    own_rows = slice(LO, HI)
    above = slice(LO + 1, HI + 1)
    under = slice(LO - 1, HI - 1)
    r = i + 2
    vm = v[r + 1, own_rows]
    fyp = vm + v[r + 1, above]
    fym = vm + v[r + 1, under]
    fxp, fxm = vm + v[r + 2, own_rows], vm + v[r, own_rows]
    fzp, dm = fz[r, own_rows], d[r, own_rows]
    for c in range(2):
        x = t[c, r, own_rows]
        y = fyp * t[c, r, above] + fym * t[c, r, under]
        y = y + fxp * t[c, r + 1, own_rows] + fxm * t[c, r - 1, own_rows]
        y = y + fzp * up_z(x) + down_z(fzp * x)
        done(c, dm * y)


def velocity_kernel(basis, dots, onehot, v, d, fz, h0, ex, ez, forced, vel, press, t, b, bz):
    sums = jnp.sum(jnp.sum(dots[...], axis=0), axis=1, keepdims=True)
    gg, gh, hh, hkh = sums[0:1], sums[1:2], sums[2:3], sums[3:4]
    alpha0 = gg / gh
    fresh = gg - 2.0 * alpha0 * gh + alpha0 * alpha0 * hh
    beta = fresh / gg
    grow = 1.0 + beta
    alpha1 = fresh / (grow * grow * gh - 2.0 * grow * alpha0 * hh + alpha0 * alpha0 * hkh)
    on_g = alpha0 + alpha1 * grow
    on_h = alpha1 * alpha0
    grad = on_g * basis[0:16] - on_h * basis[16:32]
    b[...] = grad
    bz[0:16] = up_z(grad)
    bz[16:32] = down_z(grad)
    p = on_g * basis[32:40] - on_h * basis[40:48]
    press[...] = jnp.dot(
        p, onehot[...], precision=lax.Precision.HIGHEST, preferred_element_type=jnp.float32
    )[0:4]

    def first(r, _):
        h, exi, exm, ezi = h0[r], ex[r], ex[r - 1], ez[r]
        ezm = down_z(ezi)
        for c in range(2):
            at = 8 * c + r
            y = h * b[pl.ds(at, 1)] + exi * b[pl.ds(at + 1, 1)] + exm * b[pl.ds(at - 1, 1)]
            t[c, r] = y + ezi * bz[pl.ds(at, 1)] + ezm * bz[pl.ds(16 + at, 1)]
        return 0

    lax.fori_loop(1, 7, first, 0)

    def second(i, _):
        couple(i, v, d, fz, t, lambda c, y: store(c, i, y))
        return 0

    def store(c, i, y):
        own = E0 * (d[i + 2, LO:HI] * b[pl.ds(8 * c + i + 2, 1)])
        vel[c, i] = forced[c, i] - (own + y)

    lax.fori_loop(0, ROWS, second, 0)


VMEM = pl.BlockSpec(memory_space=pltpu.VMEM)
SMEM = pl.BlockSpec(memory_space=pltpu.SMEM)
ANY = pl.BlockSpec(memory_space=pl.ANY)
HBM = pl.BlockSpec(memory_space=pltpu.HBM)


def call(kernel, out_shape, scratch, args, in_specs, out_specs=None, micros=1.0, sems=0, mib=16):
    return pl.pallas_call(
        kernel,
        out_shape=out_shape,
        in_specs=in_specs,
        out_specs=out_specs or jax.tree.map(lambda _: VMEM, out_shape),
        scratch_shapes=[pltpu.VMEM(s, jnp.float32) for s in scratch]
        + ([pltpu.SemaphoreType.DMA((sems,))] if sems else []),
        compiler_params=pltpu.CompilerParams(vmem_limit_bytes=mib * 1024 * 1024),
        cost_estimate=pl.CostEstimate(flops=0, transcendentals=0, bytes_accessed=int(micros * 3.6e6)),
    )(*args)


def in_hbm(x):
    return pltpu.with_memory_space_constraint(x, pltpu.HBM)


def f32(*shape):
    return jax.ShapeDtypeStruct(shape, jnp.float32)


def shards(forcing, viscosity, owner_slot):
    slabs, cross = lax.axis_size("slab"), lax.axis_size("cross")
    slab = lax.axis_index("slab")
    par = slab % 2
    where = jnp.stack([par, slab // 2]).astype(jnp.int32)
    mates = [(i, i ^ 1) for i in range(slabs)]
    others = [(i, i + 1) for i in range(1, slabs - 1, 2)]
    others = others + [(b, a) for a, b in others]
    up = [(i, i + 1) for i in range(cross - 1)]
    down = [(b, a) for a, b in up]
    chips = slabs // 2
    chip_up = [(i, (i + 2) % slabs) for i in range(slabs) if i + 2 < slabs]
    chip_down = [(b, a) for a, b in chip_up]

    od = lax.ppermute(viscosity, "slab", others)
    ev = lax.ppermute(viscosity, "slab", mates)
    edge_hi = jnp.concatenate([viscosity[:, -3:], forcing[0, :, -2:], forcing[1, :, -2:]], 1)
    edge_lo = jnp.concatenate([viscosity[:, :3], forcing[0, :, :2], forcing[1, :, :2]], 1)
    lo = lax.ppermute(edge_hi, "cross", up)
    hi = lax.ppermute(edge_lo, "cross", down)
    edges = jnp.concatenate([lo, hi], 1)
    od_c = lax.ppermute(edges, "slab", others)
    ev_c = lax.ppermute(edges, "slab", mates)

    margins = (lo, hi, od_c, ev_c)
    kept = (f32(10, FRAME, NZ), f32(8, FRAME, NZ), f32(8, FRAME, NZ)) + (f32(7, FRAME, NZ),) * 3
    part, to_od, to_ev, v, d, fz, h0, ex, ez = call(
        stencil_kernel,
        (f32(10, 4, NZ), f32(2, 2, NY, NZ), f32(2, 2, NY, NZ), *[pltpu.HBM(x.shape, x.dtype) for x in kept]),
        [x.shape for x in kept] + [(7, FRAME, NZ), (32, 1, NZ), (2, ROWS, NY, NZ)],
        (where, in_hbm(viscosity), od, ev, *margins, in_hbm(forcing)),
        in_specs=[SMEM, ANY, ANY, ANY] + [VMEM] * 4 + [ANY],
        out_specs=(VMEM,) + (HBM,) * 8,
        micros=6,
        sems=12,
    )

    width = owner_slot.shape[0] // cross
    column = lax.axis_index("cross") * width + jnp.arange(width, dtype=jnp.int32)
    onehot = (owner_slot[:, None] == column[None, :]).astype(jnp.float32)

    def among(x, step):
        return [lax.ppermute(x, "cross", [(i, i ^ (n * step)) for i in range(cross)]) for n in (1, 2, 3)]

    got = among(part, 1)
    od_f = lax.ppermute(to_od, "slab", others)
    ev_f = lax.ppermute(to_ev, "slab", mates)
    got, od_f, ev_f, onehot = lax.optimization_barrier((got, od_f, ev_f, onehot))
    part = part + got[0] + got[1] + got[2]
    got = among(part, 4)
    forced = call(
        forced_kernel,
        f32(2, ROWS, NY, NZ),
        [x.shape for x in kept[:3]] + [(2, 8, FRAME, NZ)] * 2,
        (where, in_hbm(forcing), od_f, ev_f, *margins, in_hbm(v), in_hbm(d), in_hbm(fz)),
        in_specs=[SMEM] + [ANY] * 3 + [VMEM] * 4 + [ANY] * 3,
        micros=5,
        sems=7,
    )
    got, forced = lax.optimization_barrier((got, forced))
    part = part + got[0] + got[1] + got[2]

    mate = lax.ppermute(part, "slab", mates)
    both = jnp.stack([part, mate])
    below = lax.ppermute(both, "slab", chip_up)
    above = lax.ppermute(both, "slab", chip_down)
    basis, dots = call(
        krylov_kernel,
        (f32(48, NZ), f32(chips, 8, 128)),
        [(7, 24, NZ), (40, NZ)],
        (where, part, mate, below[0], below[1], above[0], above[1]),
        in_specs=[SMEM] + [VMEM] * 6,
        mib=4,
    )
    groups = [[2 * z + c for z in range(chips)] for c in range(2)]
    dots = lax.all_to_all(dots, "slab", 0, 0, tiled=True, axis_index_groups=groups)

    return call(
        velocity_kernel,
        (f32(2, ROWS, NY, NZ), f32(ROWS, width)),
        [(2, 8, FRAME, NZ), (16, NZ), (32, NZ)],
        (basis, dots, onehot, v, d, fz, h0, ex, ez, forced),
        in_specs=[VMEM] * 10,
        micros=4,
    )


def solution(mesh):
    in_specs = (P(None, "slab", "cross", None), P("slab", "cross", None), P())
    out_specs = (P(None, "slab", "cross", None), P("slab", "cross"))
    return jax.shard_map(shards, mesh=mesh, in_specs=in_specs, out_specs=out_specs, check_vma=False)
```

```python
import functools

import jax
import jax.numpy as jnp
from jax import lax
from jax.experimental import pallas as pl
from jax.experimental.pallas import tpu as pltpu
from jax.sharding import PartitionSpec as P

OUTER = 2
DEGREE = 3
cheb_theta = 1.025
cheb_delta = 0.975


def series():
    sigma = cheb_theta / cheb_delta
    rho0 = 1.0 / sigma
    rho1 = 1.0 / (2.0 * sigma - rho0)
    rho2 = 1.0 / (2.0 * sigma - rho1)
    g1, g2 = 2.0 * rho1 / cheb_delta, 2.0 * rho2 / cheb_delta
    p0, p1 = (1.0 + rho1 * rho0) / cheb_theta + g1, -g1 / cheb_theta
    q = rho2 * rho1
    c0 = (1.0 + q) * p0 - q / cheb_theta + g2
    c1 = (1.0 + q) * p1 - g2 * p0
    c2 = -g2 * p1
    return c0 + c1 + c2, -c1 - 2.0 * c2, c2


E0, E1, E2 = (2.0 * e for e in series())

NY, NZ = 64, 512
ROWS = 4
FRAME = 80
LO, HI = 8, 72
FORWARD = ((0, 0), (0, 1), (0, 2), (1, -1), (1, 0), (1, 1), (2, 0))
PAYLOAD = 40


def up_z(x):
    return pltpu.roll(x, NZ - 1, x.ndim - 1)


def down_z(x):
    return pltpu.roll(x, 1, x.ndim - 1)


def lane(shape):
    return lax.broadcasted_iota(jnp.int32, shape, len(shape) - 1)


def edge_kernel(par_ref, own, f, out, low_v, high_v, low_f, high_f, sems):
    copies = [
        pltpu.make_async_copy(own.at[:, 0:8], low_v, sems.at[0]),
        pltpu.make_async_copy(own.at[:, NY - 8 : NY], high_v, sems.at[1]),
        pltpu.make_async_copy(f.at[:, :, 0:8], low_f, sems.at[2]),
        pltpu.make_async_copy(f.at[:, :, NY - 8 : NY], high_f, sems.at[3]),
    ]
    for copy in copies:
        copy.start()
    for copy in copies:
        copy.wait()
    out[:, 0:3] = low_v[:, 0:3]
    out[:, 7:10] = high_v[:, 5:8]
    for c in range(2):
        out[:, 3 + 2 * c : 5 + 2 * c] = low_f[c, :, 0:2]
        out[:, 10 + 2 * c : 12 + 2 * c] = high_f[c, :, 6:8]


def corner_kernel(par_ref, own, od, ev, low, high):
    odd = par_ref[0] == 1
    below = lax.select(odd, ev[2:4], od[2:4])
    above = lax.select(odd, od[0:2], ev[0:2])
    for out, near, forced, base in ((low, (0, 2), 0, 0), (high, (1, 3), 1, 7)):
        for n in range(4):
            out[7 * n : 7 * n + 7] = own[n, base : base + 7]
        for at, x, far, far_at in ((28, below[1], below[0], 36), (32, above[0], above[1], 37)):
            out[at : at + 2] = x[base + near[0] : base + near[1]]
            for c in range(2):
                row = base + 3 + 2 * c + forced
                out[at + 2 + c : at + 3 + c] = x[row : row + 1]
            row = base + 2 * forced
            out[far_at : far_at + 1] = far[row : row + 1]
        out[38:40] = jnp.zeros((2, NZ), jnp.float32)


def fill_viscosity(par, v, own, od, ev, lo, hi, sems):
    copies = [pltpu.make_async_copy(own, v.at[3:7, LO:HI], sems.at[0])]
    for n, at, first, x in ((1, par * 7, 1 - par, od), (2, 7 - par * 7, par, ev)):
        copies.append(pltpu.make_async_copy(x.at[pl.ds(first, 3)], v.at[pl.ds(at, 3), LO:HI], sems.at[n]))
    for copy in copies:
        copy.start()
    for n in range(4):
        v[3 + n, LO - 3 : LO] = lo[7 * n : 7 * n + 3]
        v[3 + n, HI : HI + 3] = hi[7 * n : 7 * n + 3]
    for r, at in ((2, 28), (7, 32)):
        v[r, LO - 2 : LO] = lo[at : at + 2]
        v[r, HI : HI + 2] = hi[at : at + 2]
    for r, at in ((1, 36), (8, 37)):
        v[r, LO - 1 : LO] = lo[at : at + 1]
        v[r, HI : HI + 1] = hi[at : at + 1]
    for copy in copies:
        copy.wait()


def fill_inverse(v, d, fz):
    ids = lane((FRAME, NZ))

    def layer(r, _):
        mid = v[r + 1]
        nxt = jnp.where(ids == NZ - 1, 0.0, up_z(mid))
        prv = jnp.where(ids == 0, 0.0, down_z(mid))
        total = 6.0 * mid + v[r] + v[r + 2] + nxt + prv
        total = total + pltpu.roll(mid, 1, 0) + pltpu.roll(mid, FRAME - 1, 0)
        d[r] = jnp.where(mid > 0.0, 1.0 / total, 0.0)
        fz[r] = jnp.where(ids == NZ - 1, 0.0, mid + nxt)
        return 0

    lax.fori_loop(0, 8, layer, 0)


def stencil_kernel(par_ref, own, od, ev, lo, hi, f_hbm, out, to_od, to_ev, *rest):
    kept_hbm, (v, d, fz, h0, ex, ez, ezm, acc, f, sems) = rest[:6], rest[6:]
    par = par_ref[0]
    load = pltpu.make_async_copy(f_hbm, f, sems.at[3])
    load.start()
    fill_viscosity(par, v, own, od, ev, lo, hi, sems)
    moves = [
        pltpu.make_async_copy(f_hbm.at[:, pl.ds(2 * par, 2)], to_od, sems.at[10]),
        pltpu.make_async_copy(f_hbm.at[:, pl.ds(2 - 2 * par, 2)], to_ev, sems.at[11]),
    ]
    for copy in moves:
        copy.start()
    fill_inverse(v, d, fz)

    def edges(r, _):
        dm, vm = d[r], v[r + 1]
        ex[r] = E2 * dm * (vm + v[r + 2]) * d[r + 1]
        dy = pltpu.roll(dm, FRAME - 1, 0)
        ey = E2 * dm * (vm + pltpu.roll(vm, FRAME - 1, 0)) * dy
        h0[r] = E1 * dm + ey + pltpu.roll(ey, 1, 0)
        e = E2 * dm * fz[r] * up_z(dm)
        ez[r] = e
        ezm[r] = down_z(e)
        return 0

    lax.fori_loop(0, 7, edges, 0)

    saves = [pltpu.make_async_copy(x, y, sems.at[4 + n]) for n, (x, y) in enumerate(zip((v, d, fz, h0, ex, ez), kept_hbm))]
    for copy in saves:
        copy.start()
    load.wait()
    acc[...] = jnp.zeros_like(acc)
    own_rows = slice(LO, HI)
    above = slice(LO + 1, HI + 1)
    under = slice(LO - 1, HI - 1)

    def layer(i, _):
        r = i + 2
        vm = v[r + 1, own_rows]
        fyp = vm + v[r + 1, above]
        fym = vm + v[r + 1, under]
        fxp = vm + v[r + 2, own_rows]
        fxm = vm + v[r, own_rows]
        fzp = fz[r, own_rows]
        fzm = down_z(fzp)
        dm = d[r, own_rows]
        u0, u1 = dm * f[0, i], dm * f[1, i]

        def weigh(di, dk, s):
            for c, u in ((0, u0), (1, u1)):
                row = jnp.sum(u * s, axis=0, keepdims=True)
                if dk:
                    row = pltpu.roll(row, dk % NZ, 1)
                at = pl.ds(16 * c + i + di + 2, 1)
                acc[at] = acc[at] + row[None]
            if (di, dk) in FORWARD:
                out[FORWARD.index((di, dk)), pl.ds(i, 1)] = jnp.sum(dm * s, axis=0, keepdims=True)

        exi, exm = ex[r, own_rows], ex[r - 1, own_rows]
        ezi, ezmi = ez[r, own_rows], ezm[r, own_rows]
        h = h0[r, own_rows]
        weigh(
            0,
            0,
            E0
            + fyp * h0[r, above]
            + fym * h0[r, under]
            + fxp * exi
            + fxm * exm
            + fzp * ezi
            + fzm * ezmi,
        )
        weigh(1, 0, fyp * ex[r, above] + fym * ex[r, under] + fxp * h0[r + 1, own_rows])
        weigh(-1, 0, fyp * ex[r - 1, above] + fym * ex[r - 1, under] + fxm * h0[r - 1, own_rows])
        weigh(0, 1, fyp * ez[r, above] + fym * ez[r, under] + fzp * up_z(h))
        weigh(0, -1, fyp * ezm[r, above] + fym * ezm[r, under] + fzm * down_z(h))
        weigh(2, 0, fxp * ex[r + 1, own_rows])
        weigh(-2, 0, fxm * ex[r - 2, own_rows])
        weigh(0, 2, fzp * up_z(ezi))
        weigh(0, -2, fzm * down_z(ezmi))
        weigh(1, 1, fxp * ez[r + 1, own_rows] + fzp * up_z(exi))
        weigh(1, -1, fxp * ezm[r + 1, own_rows] + fzm * down_z(exi))
        weigh(-1, 1, fxm * ez[r - 1, own_rows] + fzp * up_z(exm))
        weigh(-1, -1, fxm * ezm[r - 1, own_rows] + fzm * down_z(exm))
        return 0

    lax.fori_loop(0, ROWS, layer, 0)

    cx = acc[0:16, 0]
    cz = acc[16:32, 0]
    zero = lane((16, NZ)) == 0
    e = cx - pltpu.roll(cx, 1, 0) + cz - jnp.where(zero, 0.0, down_z(cz))
    out[7:9] = e[0:8].reshape(2, 4, NZ)
    out[9, 0:1] = e[8:9]
    out[9, 1:4] = jnp.zeros((3, NZ), jnp.float32)
    for copy in moves + saves:
        copy.wait()


def krylov_kernel(par_ref, mine, mate, below_mine, below_mate, above_mine, above_mate, basis, dots, s_ref, g_ref):
    par, chip = par_ref[0], par_ref[1]
    odd = par == 1

    def pair(a, b):
        return lax.select(odd, b, a), lax.select(odd, a, b)

    slabs = []
    for a, b in ((below_mine, below_mate), (mine, mate), (above_mine, above_mate)):
        slabs += pair(a[...], b[...])
    W = 24
    g_ref[...] = jnp.zeros_like(g_ref)
    for n, slab in enumerate(slabs):
        for o in range(7):
            s_ref[o, 4 * n : 4 * n + 4] = slab[o]
        flat = slab[7:10].reshape(12, NZ)[0:9]
        at = 8 + 4 * n - 2
        g_ref[at : at + 9] = g_ref[at : at + 9] + flat
    ids = lane((W, NZ))
    layer = lax.broadcasted_iota(jnp.int32, (W, NZ), 0) - 8 + 8 * chip
    inside = jnp.logical_and(layer >= 0, layer < 64)

    def next_layer(x, n=1):
        return pltpu.roll(x, (W - n) % W, 0)

    def shift(x, di, dk):
        if di:
            x = pltpu.roll(x, (-di) % W, 0)
        if dk:
            x = pltpu.roll(x, (-dk) % NZ, 1)
        return x

    def spread(q):
        qx = q - next_layer(q)
        qz = q - jnp.where(ids == NZ - 1, 0.0, up_z(q))
        return qx, qz

    def times_s(b):
        total = None
        for n, (di, dk) in enumerate(FORWARD):
            s = s_ref[n]
            if n == 0:
                total = s * b
            else:
                total = total + s * shift(b, di, dk) + shift(s * b, -di, -dk)
        return total

    g = jnp.where(inside, g_ref[8 : 8 + W], 0.0)
    gx, gz = spread(g)
    tx, tz = times_s(gx), times_s(gz)
    h = tx - pltpu.roll(tx, 1, 0) + tz - jnp.where(ids == 0, 0.0, down_z(tz))
    h = jnp.where(inside, h, 0.0)
    hx, hz = spread(h)
    energy = hx * times_s(hx) + hz * times_s(hz)

    def own(x):
        return lax.select(odd, pltpu.roll(x, W - 4, 0), x)

    for n, x in enumerate((gx, gz, hx, hz)):
        basis[8 * n : 8 * n + 8] = own(x)[6:14]
    basis[32:40] = own(g)[8:16]
    basis[40:48] = own(h)[8:16]
    rows = []
    for x in (g * g, g * h, h * h, energy):
        part = x[8:16]
        part = part[:, 0:128] + part[:, 128:256] + part[:, 256:384] + part[:, 384:512]
        rows.append(jnp.sum(part, axis=0, keepdims=True))
    packed = jnp.concatenate(rows + [jnp.zeros((4, 128), jnp.float32)], 0)
    dots[...] = jnp.broadcast_to(packed[None], dots.shape)


def forced_kernel(par_ref, f, od_f, ev_f, lo, hi, v_hbm, d_hbm, fz_hbm, out_hbm, v, d, fz, u, t, out, sems):
    par = par_ref[0]
    copies = [pltpu.make_async_copy(x, y, sems.at[n]) for n, (x, y) in enumerate(((d_hbm, d), (v_hbm, v), (fz_hbm, fz)))]
    for c in range(2):
        copies.append(pltpu.make_async_copy(f.at[c], u.at[c, 2:6, LO:HI], sems.at[3 + c]))
    for n, at, x in ((5, par * 6, od_f), (6, 6 - par * 6, ev_f)):
        copies.append(pltpu.make_async_copy(x, u.at[:, pl.ds(at, 2), LO:HI], sems.at[n]))
    for copy in copies:
        copy.start()
    for c in range(2):
        for n in range(4):
            u[c, 2 + n, LO - 2 : LO] = lo[7 * n + 3 + 2 * c : 7 * n + 5 + 2 * c]
            u[c, 2 + n, HI : HI + 2] = hi[7 * n + 3 + 2 * c : 7 * n + 5 + 2 * c]
        for r, at in ((1, 30), (6, 34)):
            u[c, r, LO - 1 : LO] = lo[at + c : at + c + 1]
            u[c, r, HI : HI + 1] = hi[at + c : at + c + 1]
    for copy in copies:
        copy.wait()

    def scale(r, _):
        dm = d[r]
        u[0, r] = dm * u[0, r]
        u[1, r] = dm * u[1, r]
        return 0

    lax.fori_loop(0, 8, scale, 0)

    def first(r, _):
        vm = v[r + 1]
        fy = vm + pltpu.roll(vm, FRAME - 1, 0)
        fxp, fxm = vm + v[r + 2], vm + v[r]
        fzp, dm = fz[r], d[r]
        for c in range(2):
            x = u[c, r]
            y = fy * pltpu.roll(x, FRAME - 1, 0) + pltpu.roll(fy * x, 1, 0)
            y = y + fxp * u[c, r + 1] + fxm * u[c, r - 1]
            y = y + fzp * up_z(x) + down_z(fzp * x)
            t[c, r] = E1 * x + E2 * (dm * y)
        return 0

    lax.fori_loop(1, 7, first, 0)

    def store(c, i, y):
        out[c, i] = E0 * u[c, i + 2, LO:HI] + y

    saves = []
    for i in range(ROWS):
        couple(i, v, d, fz, t, lambda c, y: store(c, i, y))
        saves.append(pltpu.make_async_copy(out.at[:, i], out_hbm.at[:, i], sems.at[7 + i]))
        saves[-1].start()
    for copy in saves:
        copy.wait()


def couple(i, v, d, fz, t, done):
    own_rows = slice(LO, HI)
    above = slice(LO + 1, HI + 1)
    under = slice(LO - 1, HI - 1)
    r = i + 2
    vm = v[r + 1, own_rows]
    fyp = vm + v[r + 1, above]
    fym = vm + v[r + 1, under]
    fxp, fxm = vm + v[r + 2, own_rows], vm + v[r, own_rows]
    fzp, dm = fz[r, own_rows], d[r, own_rows]
    for c in range(2):
        x = t[c, r, own_rows]
        y = fyp * t[c, r, above] + fym * t[c, r, under]
        y = y + fxp * t[c, r + 1, own_rows] + fxm * t[c, r - 1, own_rows]
        y = y + fzp * up_z(x) + down_z(fzp * x)
        done(c, dm * y)


def velocity_kernel(basis, dots, onehot, *rest):
    inputs, (vel_hbm, press), scratch, (vel, t, b, bz, sems) = rest[:7], rest[7:9], rest[9:16], rest[16:]
    h0, ex, ez, v, d, fz, forced = scratch
    loads = [pltpu.make_async_copy(x, y, sems.at[n]) for n, (x, y) in enumerate(zip(inputs, scratch))]
    for copy in loads:
        copy.start()
    sums = jnp.sum(jnp.sum(dots[...], axis=0), axis=1, keepdims=True)
    gg, gh, hh, hkh = sums[0:1], sums[1:2], sums[2:3], sums[3:4]
    alpha0 = gg / gh
    fresh = gg - 2.0 * alpha0 * gh + alpha0 * alpha0 * hh
    beta = fresh / gg
    grow = 1.0 + beta
    alpha1 = fresh / (grow * grow * gh - 2.0 * grow * alpha0 * hh + alpha0 * alpha0 * hkh)
    on_g = alpha0 + alpha1 * grow
    on_h = alpha1 * alpha0
    grad = on_g * basis[0:16] - on_h * basis[16:32]
    b[...] = grad
    bz[0:16] = up_z(grad)
    bz[16:32] = down_z(grad)
    p = on_g * basis[32:40] - on_h * basis[40:48]
    press[...] = jnp.dot(
        p, onehot[...], precision=lax.Precision.HIGHEST, preferred_element_type=jnp.float32
    )[0:4]

    for copy in loads[:3]:
        copy.wait()

    def first(r, _):
        h, exi, exm, ezi = h0[r], ex[r], ex[r - 1], ez[r]
        ezm = down_z(ezi)
        for c in range(2):
            at = 8 * c + r
            y = h * b[pl.ds(at, 1)] + exi * b[pl.ds(at + 1, 1)] + exm * b[pl.ds(at - 1, 1)]
            t[c, r] = y + ezi * bz[pl.ds(at, 1)] + ezm * bz[pl.ds(16 + at, 1)]
        return 0

    lax.fori_loop(1, 7, first, 0)

    for copy in loads[3:]:
        copy.wait()

    def store(c, i, y):
        own = E0 * (d[i + 2, LO:HI] * b[pl.ds(8 * c + i + 2, 1)])
        vel[c, i] = forced[c, i] - (own + y)

    saves = []
    for i in range(ROWS):
        couple(i, v, d, fz, t, lambda c, y: store(c, i, y))
        saves.append(pltpu.make_async_copy(vel.at[:, i], vel_hbm.at[:, i], sems.at[7 + i]))
        saves[-1].start()
    for copy in saves:
        copy.wait()


VMEM = pl.BlockSpec(memory_space=pltpu.VMEM)
SMEM = pl.BlockSpec(memory_space=pltpu.SMEM)
ANY = pl.BlockSpec(memory_space=pl.ANY)
HBM = pl.BlockSpec(memory_space=pltpu.HBM)


def call(kernel, out_shape, scratch, args, in_specs, out_specs=None, micros=1.0, sems=0, mib=16):
    return pl.pallas_call(
        kernel,
        out_shape=out_shape,
        in_specs=in_specs,
        out_specs=out_specs or jax.tree.map(lambda _: VMEM, out_shape),
        scratch_shapes=[pltpu.VMEM(s, jnp.float32) for s in scratch]
        + ([pltpu.SemaphoreType.DMA((sems,))] if sems else []),
        compiler_params=pltpu.CompilerParams(vmem_limit_bytes=mib * 1024 * 1024),
        cost_estimate=pl.CostEstimate(flops=0, transcendentals=0, bytes_accessed=int(micros * 3.6e6)),
    )(*args)


def in_hbm(x):
    return pltpu.with_memory_space_constraint(x, pltpu.HBM)


def f32(*shape):
    return jax.ShapeDtypeStruct(shape, jnp.float32)


def shards(forcing, viscosity, owner_slot):
    slabs, cross = lax.axis_size("slab"), lax.axis_size("cross")
    slab = lax.axis_index("slab")
    par = slab % 2
    where = jnp.stack([par, slab // 2]).astype(jnp.int32)
    mates = [(i, i ^ 1) for i in range(slabs)]
    others = [(i, i + 1) for i in range(1, slabs - 1, 2)]
    others = others + [(b, a) for a, b in others]
    up = [(i, i + 1) for i in range(cross - 1)]
    down = [(b, a) for a, b in up]
    chips = slabs // 2
    chip_up = [(i, (i + 2) % slabs) for i in range(slabs) if i + 2 < slabs]
    chip_down = [(b, a) for a, b in chip_up]

    edges = call(
        edge_kernel,
        f32(ROWS, 14, NZ),
        [(ROWS, 8, NZ)] * 2 + [(2, ROWS, 8, NZ)] * 2,
        (where, in_hbm(viscosity), in_hbm(forcing)),
        in_specs=[SMEM, ANY, ANY],
        sems=4,
        mib=4,
    )
    od_e = lax.ppermute(edges, "slab", others)
    ev_e = lax.ppermute(edges, "slab", mates)
    od_e, ev_e, late = lax.optimization_barrier((od_e, ev_e, viscosity))
    od = lax.ppermute(late, "slab", others)
    ev = lax.ppermute(late, "slab", mates)
    low, high = call(
        corner_kernel, (f32(40, NZ), f32(40, NZ)), [], (where, edges, od_e, ev_e), in_specs=[SMEM] + [VMEM] * 3, mib=4
    )
    lo = lax.ppermute(high, "cross", up)
    hi = lax.ppermute(low, "cross", down)

    kept = (f32(10, FRAME, NZ), f32(8, FRAME, NZ), f32(8, FRAME, NZ)) + (f32(7, FRAME, NZ),) * 3
    part, to_od, to_ev, v, d, fz, h0, ex, ez = call(
        stencil_kernel,
        (f32(10, 4, NZ), *[pltpu.HBM((2, 2, NY, NZ), jnp.float32)] * 2, *[pltpu.HBM(x.shape, x.dtype) for x in kept]),
        [x.shape for x in kept] + [(7, FRAME, NZ), (32, 1, NZ), (2, ROWS, NY, NZ)],
        (where, in_hbm(viscosity), od, ev, lo, hi, in_hbm(forcing)),
        in_specs=[SMEM, ANY, ANY, ANY, VMEM, VMEM, ANY],
        out_specs=(VMEM,) + (HBM,) * 8,
        micros=6,
        sems=12,
    )

    width = owner_slot.shape[0] // cross
    column = lax.axis_index("cross") * width + jnp.arange(width, dtype=jnp.int32)
    onehot = (owner_slot[:, None] == column[None, :]).astype(jnp.float32)

    def among(x, step):
        return [lax.ppermute(x, "cross", [(i, i ^ (n * step)) for i in range(cross)]) for n in (1, 2, 3)]

    part, onehot = lax.optimization_barrier((part, onehot))
    got = among(part, 1)
    part = part + got[0] + got[1] + got[2]
    part, to_od, to_ev = lax.optimization_barrier((part, to_od, to_ev))
    od_f = lax.ppermute(to_od, "slab", others)
    ev_f = lax.ppermute(to_ev, "slab", mates)
    got = among(part, 4)
    got, od_f, ev_f = lax.optimization_barrier((got, od_f, ev_f))
    part = part + got[0] + got[1] + got[2]

    mate = lax.ppermute(part, "slab", mates)
    both = jnp.stack([part, mate])
    below = lax.ppermute(both, "slab", chip_up)
    above = lax.ppermute(both, "slab", chip_down)
    basis, dots = call(
        krylov_kernel,
        (f32(48, NZ), f32(chips, 8, 128)),
        [(7, 24, NZ), (40, NZ)],
        (where, part, mate, below[0], below[1], above[0], above[1]),
        in_specs=[SMEM] + [VMEM] * 6,
        mib=4,
    )
    dots, od_f, ev_f = lax.optimization_barrier((dots, od_f, ev_f))
    forced = call(
        forced_kernel,
        pltpu.HBM((2, ROWS, NY, NZ), jnp.float32),
        [x.shape for x in kept[:3]] + [(2, 8, FRAME, NZ)] * 2 + [(2, ROWS, NY, NZ)],
        (where, in_hbm(forcing), in_hbm(od_f), in_hbm(ev_f), lo, hi, in_hbm(v), in_hbm(d), in_hbm(fz)),
        in_specs=[SMEM] + [ANY] * 3 + [VMEM] * 2 + [ANY] * 3,
        out_specs=HBM,
        micros=5,
        sems=11,
    )
    groups = [[2 * z + c for z in range(chips)] for c in range(2)]
    dots = lax.all_to_all(dots, "slab", 0, 0, tiled=True, axis_index_groups=groups)

    big = (h0, ex, ez, v, d, fz, forced)
    return call(
        velocity_kernel,
        (pltpu.HBM((2, ROWS, NY, NZ), jnp.float32), f32(ROWS, width)),
        [x.shape for x in big] + [(2, ROWS, NY, NZ), (2, 8, FRAME, NZ), (16, NZ), (32, NZ)],
        (basis, dots, onehot, *[in_hbm(x) for x in big]),
        in_specs=[VMEM] * 3 + [ANY] * 7,
        out_specs=(HBM, VMEM),
        micros=4,
        sems=11,
        mib=24,
    )


def solution(mesh):
    in_specs = (P(None, "slab", "cross", None), P("slab", "cross", None), P())
    out_specs = (P(None, "slab", "cross", None), P("slab", "cross"))
    return jax.shard_map(shards, mesh=mesh, in_specs=in_specs, out_specs=out_specs, check_vma=False)
```

```python
import functools

import jax
import jax.numpy as jnp
from jax import lax
from jax.experimental import pallas as pl
from jax.experimental.pallas import tpu as pltpu
from jax.sharding import PartitionSpec as P

OUTER = 2
DEGREE = 3
cheb_theta = 1.025
cheb_delta = 0.975


def series():
    sigma = cheb_theta / cheb_delta
    rho0 = 1.0 / sigma
    rho1 = 1.0 / (2.0 * sigma - rho0)
    rho2 = 1.0 / (2.0 * sigma - rho1)
    g1, g2 = 2.0 * rho1 / cheb_delta, 2.0 * rho2 / cheb_delta
    p0, p1 = (1.0 + rho1 * rho0) / cheb_theta + g1, -g1 / cheb_theta
    q = rho2 * rho1
    c0 = (1.0 + q) * p0 - q / cheb_theta + g2
    c1 = (1.0 + q) * p1 - g2 * p0
    c2 = -g2 * p1
    return c0 + c1 + c2, -c1 - 2.0 * c2, c2


E0, E1, E2 = (2.0 * e for e in series())

NY, NZ = 64, 512
ROWS = 4
FRAME = 80
LO, HI = 8, 72
FORWARD = ((0, 0), (0, 1), (0, 2), (1, -1), (1, 0), (1, 1), (2, 0))
PAYLOAD = 40


def up_z(x):
    return pltpu.roll(x, NZ - 1, x.ndim - 1)


def down_z(x):
    return pltpu.roll(x, 1, x.ndim - 1)


def lane(shape):
    return lax.broadcasted_iota(jnp.int32, shape, len(shape) - 1)


def edge_kernel(par_ref, own, f, out, low_v, high_v, low_f, high_f, sems):
    copies = [
        pltpu.make_async_copy(own.at[:, 0:8], low_v, sems.at[0]),
        pltpu.make_async_copy(own.at[:, NY - 8 : NY], high_v, sems.at[1]),
        pltpu.make_async_copy(f.at[:, :, 0:8], low_f, sems.at[2]),
        pltpu.make_async_copy(f.at[:, :, NY - 8 : NY], high_f, sems.at[3]),
    ]
    for copy in copies:
        copy.start()
    for copy in copies:
        copy.wait()
    out[:, 0:3] = low_v[:, 0:3]
    out[:, 7:10] = high_v[:, 5:8]
    for c in range(2):
        out[:, 3 + 2 * c : 5 + 2 * c] = low_f[c, :, 0:2]
        out[:, 10 + 2 * c : 12 + 2 * c] = high_f[c, :, 6:8]


def pack_kernel(par_ref, own_hbm, f_hbm, to_od, to_ev, own, f, sems):
    par = par_ref[0]
    loads = [pltpu.make_async_copy(own_hbm, own, sems.at[0]), pltpu.make_async_copy(f_hbm, f, sems.at[1])]
    for copy in loads:
        copy.start()
    saves = []
    for n, (out, last) in enumerate(((to_od, par), (to_ev, 1 - par))):
        saves.append(pltpu.make_async_copy(own.at[pl.ds(last, 3)], out.at[0:3], sems.at[2 + 3 * n]))
        for c in range(2):
            saves.append(
                pltpu.make_async_copy(
                    f.at[c, pl.ds(2 * last, 2)], out.at[3 + 2 * c : 5 + 2 * c], sems.at[3 + 3 * n + c]
                )
            )
    for copy in loads:
        copy.wait()
    for copy in saves:
        copy.start()
    for copy in saves:
        copy.wait()


def corner_kernel(par_ref, own, od, ev, first, second, low, high):
    odd = par_ref[0] == 1
    below = lax.select(odd, ev[2:4], od[2:4])
    above = lax.select(odd, od[0:2], ev[0:2])
    for out, near, forced, base in ((low, (0, 2), 0, 0), (high, (1, 3), 1, 7)):
        for n in range(4):
            out[7 * n : 7 * n + 7] = own[n, base : base + 7]
        for at, x, far, far_at in ((28, below[1], below[0], 36), (32, above[0], above[1], 37)):
            out[at : at + 2] = x[base + near[0] : base + near[1]]
            for c in range(2):
                row = base + 3 + 2 * c + forced
                out[at + 2 + c : at + 3 + c] = x[row : row + 1]
            row = base + 2 * forced
            out[far_at : far_at + 1] = far[row : row + 1]
        out[38:40] = jnp.zeros((2, NZ), jnp.float32)
    odd = par_ref[2] == 1
    first[...] = lax.select(odd, low[...], high[...])
    second[...] = lax.select(odd, high[...], low[...])


def sides(odd, first, second):
    return lax.select(odd, first[...], second[...]), lax.select(odd, second[...], first[...])


def fill_viscosity(par, v, own, od, ev, lo, hi, sems):
    copies = [pltpu.make_async_copy(own, v.at[3:7, LO:HI], sems.at[0])]
    for n, at, x in ((1, par * 7, od), (2, 7 - par * 7, ev)):
        copies.append(pltpu.make_async_copy(x.at[0:3], v.at[pl.ds(at, 3), LO:HI], sems.at[n]))
    for copy in copies:
        copy.start()
    for n in range(4):
        v[3 + n, LO - 3 : LO] = lo[7 * n : 7 * n + 3]
        v[3 + n, HI : HI + 3] = hi[7 * n : 7 * n + 3]
    for r, at in ((2, 28), (7, 32)):
        v[r, LO - 2 : LO] = lo[at : at + 2]
        v[r, HI : HI + 2] = hi[at : at + 2]
    for r, at in ((1, 36), (8, 37)):
        v[r, LO - 1 : LO] = lo[at : at + 1]
        v[r, HI : HI + 1] = hi[at : at + 1]
    for copy in copies:
        copy.wait()


def fill_inverse(v, d, fz):
    ids = lane((FRAME, NZ))

    def layer(r, _):
        mid = v[r + 1]
        nxt = jnp.where(ids == NZ - 1, 0.0, up_z(mid))
        prv = jnp.where(ids == 0, 0.0, down_z(mid))
        total = 6.0 * mid + v[r] + v[r + 2] + nxt + prv
        total = total + pltpu.roll(mid, 1, 0) + pltpu.roll(mid, FRAME - 1, 0)
        d[r] = jnp.where(mid > 0.0, 1.0 / total, 0.0)
        fz[r] = jnp.where(ids == NZ - 1, 0.0, mid + nxt)
        return 0

    lax.fori_loop(0, 8, layer, 0)


def stencil_kernel(par_ref, own, od, ev, first, second, f_hbm, out, *rest):
    kept_hbm, (v, d, fz, h0, ex, ez, ezm, acc, f, sems) = rest[:6], rest[6:]
    par = par_ref[0]
    load = pltpu.make_async_copy(f_hbm, f, sems.at[3])
    load.start()
    lo, hi = sides(par_ref[2] == 1, first, second)
    fill_viscosity(par, v, own, od, ev, lo, hi, sems)
    fill_inverse(v, d, fz)

    def edges(r, _):
        dm, vm = d[r], v[r + 1]
        ex[r] = E2 * dm * (vm + v[r + 2]) * d[r + 1]
        dy = pltpu.roll(dm, FRAME - 1, 0)
        ey = E2 * dm * (vm + pltpu.roll(vm, FRAME - 1, 0)) * dy
        h0[r] = E1 * dm + ey + pltpu.roll(ey, 1, 0)
        e = E2 * dm * fz[r] * up_z(dm)
        ez[r] = e
        ezm[r] = down_z(e)
        return 0

    lax.fori_loop(0, 7, edges, 0)

    saves = [pltpu.make_async_copy(x, y, sems.at[4 + n]) for n, (x, y) in enumerate(zip((v, d, fz, h0, ex, ez), kept_hbm))]
    for copy in saves:
        copy.start()
    load.wait()
    acc[...] = jnp.zeros_like(acc)
    own_rows = slice(LO, HI)
    above = slice(LO + 1, HI + 1)
    under = slice(LO - 1, HI - 1)

    def layer(i, _):
        r = i + 2
        vm = v[r + 1, own_rows]
        fyp = vm + v[r + 1, above]
        fym = vm + v[r + 1, under]
        fxp = vm + v[r + 2, own_rows]
        fxm = vm + v[r, own_rows]
        fzp = fz[r, own_rows]
        fzm = down_z(fzp)
        dm = d[r, own_rows]
        u0, u1 = dm * f[0, i], dm * f[1, i]

        def weigh(di, dk, s):
            for c, u in ((0, u0), (1, u1)):
                row = jnp.sum(u * s, axis=0, keepdims=True)
                if dk:
                    row = pltpu.roll(row, dk % NZ, 1)
                at = pl.ds(16 * c + i + di + 2, 1)
                acc[at] = acc[at] + row[None]
            if (di, dk) in FORWARD:
                out[FORWARD.index((di, dk)), pl.ds(i, 1)] = jnp.sum(dm * s, axis=0, keepdims=True)

        exi, exm = ex[r, own_rows], ex[r - 1, own_rows]
        ezi, ezmi = ez[r, own_rows], ezm[r, own_rows]
        h = h0[r, own_rows]
        weigh(
            0,
            0,
            E0
            + fyp * h0[r, above]
            + fym * h0[r, under]
            + fxp * exi
            + fxm * exm
            + fzp * ezi
            + fzm * ezmi,
        )
        weigh(1, 0, fyp * ex[r, above] + fym * ex[r, under] + fxp * h0[r + 1, own_rows])
        weigh(-1, 0, fyp * ex[r - 1, above] + fym * ex[r - 1, under] + fxm * h0[r - 1, own_rows])
        weigh(0, 1, fyp * ez[r, above] + fym * ez[r, under] + fzp * up_z(h))
        weigh(0, -1, fyp * ezm[r, above] + fym * ezm[r, under] + fzm * down_z(h))
        weigh(2, 0, fxp * ex[r + 1, own_rows])
        weigh(-2, 0, fxm * ex[r - 2, own_rows])
        weigh(0, 2, fzp * up_z(ezi))
        weigh(0, -2, fzm * down_z(ezmi))
        weigh(1, 1, fxp * ez[r + 1, own_rows] + fzp * up_z(exi))
        weigh(1, -1, fxp * ezm[r + 1, own_rows] + fzm * down_z(exi))
        weigh(-1, 1, fxm * ez[r - 1, own_rows] + fzp * up_z(exm))
        weigh(-1, -1, fxm * ezm[r - 1, own_rows] + fzm * down_z(exm))
        return 0

    lax.fori_loop(0, ROWS, layer, 0)

    cx = acc[0:16, 0]
    cz = acc[16:32, 0]
    zero = lane((16, NZ)) == 0
    e = cx - pltpu.roll(cx, 1, 0) + cz - jnp.where(zero, 0.0, down_z(cz))
    out[7:9] = e[0:8].reshape(2, 4, NZ)
    out[9, 0:1] = e[8:9]
    out[9, 1:4] = jnp.zeros((3, NZ), jnp.float32)
    for copy in saves:
        copy.wait()


def krylov_kernel(par_ref, mine, mate, first, second, basis, dots, s_ref, g_ref):
    par, chip = par_ref[0], par_ref[1]
    odd = par == 1

    def pair(a, b):
        return lax.select(odd, b, a), lax.select(odd, a, b)

    slabs = []
    below, above = sides(par_ref[3] == 1, first, second)
    for a, b in ((below[0], below[1]), (mine[...], mate[...]), (above[0], above[1])):
        slabs += pair(a, b)
    W = 24
    g_ref[...] = jnp.zeros_like(g_ref)
    for n, slab in enumerate(slabs):
        for o in range(7):
            s_ref[o, 4 * n : 4 * n + 4] = slab[o]
        flat = slab[7:10].reshape(12, NZ)[0:9]
        at = 8 + 4 * n - 2
        g_ref[at : at + 9] = g_ref[at : at + 9] + flat
    ids = lane((W, NZ))
    layer = lax.broadcasted_iota(jnp.int32, (W, NZ), 0) - 8 + 8 * chip
    inside = jnp.logical_and(layer >= 0, layer < 64)

    def next_layer(x, n=1):
        return pltpu.roll(x, (W - n) % W, 0)

    def shift(x, di, dk):
        if di:
            x = pltpu.roll(x, (-di) % W, 0)
        if dk:
            x = pltpu.roll(x, (-dk) % NZ, 1)
        return x

    def spread(q):
        qx = q - next_layer(q)
        qz = q - jnp.where(ids == NZ - 1, 0.0, up_z(q))
        return qx, qz

    def times_s(b):
        total = None
        for n, (di, dk) in enumerate(FORWARD):
            s = s_ref[n]
            if n == 0:
                total = s * b
            else:
                total = total + s * shift(b, di, dk) + shift(s * b, -di, -dk)
        return total

    g = jnp.where(inside, g_ref[8 : 8 + W], 0.0)
    gx, gz = spread(g)
    tx, tz = times_s(gx), times_s(gz)
    h = tx - pltpu.roll(tx, 1, 0) + tz - jnp.where(ids == 0, 0.0, down_z(tz))
    h = jnp.where(inside, h, 0.0)
    hx, hz = spread(h)
    energy = hx * times_s(hx) + hz * times_s(hz)

    def own(x):
        return lax.select(odd, pltpu.roll(x, W - 4, 0), x)

    for n, x in enumerate((gx, gz, hx, hz)):
        basis[8 * n : 8 * n + 8] = own(x)[6:14]
    basis[32:40] = own(g)[8:16]
    basis[40:48] = own(h)[8:16]
    rows = []
    for x in (g * g, g * h, h * h, energy):
        part = x[8:16]
        part = part[:, 0:128] + part[:, 128:256] + part[:, 256:384] + part[:, 384:512]
        rows.append(jnp.sum(part, axis=0, keepdims=True))
    packed = jnp.concatenate(rows + [jnp.zeros((4, 128), jnp.float32)], 0)
    dots[...] = jnp.broadcast_to(packed[None], dots.shape)


def forced_kernel(par_ref, f, od, ev, first, second, v_hbm, d_hbm, fz_hbm, out, v, d, fz, u, t, sems):
    par = par_ref[0]
    copies = [pltpu.make_async_copy(x, y, sems.at[n]) for n, (x, y) in enumerate(((d_hbm, d), (v_hbm, v), (fz_hbm, fz)))]
    for c in range(2):
        copies.append(pltpu.make_async_copy(f.at[c], u.at[c, 2:6, LO:HI], sems.at[3 + c]))
        for n, at, x in ((5, par * 6, od), (7, 6 - par * 6, ev)):
            copies.append(
                pltpu.make_async_copy(x.at[3 + 2 * c : 5 + 2 * c], u.at[c, pl.ds(at, 2), LO:HI], sems.at[n + c])
            )
    for copy in copies:
        copy.start()
    lo, hi = sides(par_ref[2] == 1, first, second)
    for c in range(2):
        for n in range(4):
            u[c, 2 + n, LO - 2 : LO] = lo[7 * n + 3 + 2 * c : 7 * n + 5 + 2 * c]
            u[c, 2 + n, HI : HI + 2] = hi[7 * n + 3 + 2 * c : 7 * n + 5 + 2 * c]
        for r, at in ((1, 30), (6, 34)):
            u[c, r, LO - 1 : LO] = lo[at + c : at + c + 1]
            u[c, r, HI : HI + 1] = hi[at + c : at + c + 1]
    for copy in copies:
        copy.wait()

    def scale(r, _):
        dm = d[r]
        u[0, r] = dm * u[0, r]
        u[1, r] = dm * u[1, r]
        return 0

    lax.fori_loop(0, 8, scale, 0)

    def first(r, _):
        vm = v[r + 1]
        fy = vm + pltpu.roll(vm, FRAME - 1, 0)
        fxp, fxm = vm + v[r + 2], vm + v[r]
        fzp, dm = fz[r], d[r]
        for c in range(2):
            x = u[c, r]
            y = fy * pltpu.roll(x, FRAME - 1, 0) + pltpu.roll(fy * x, 1, 0)
            y = y + fxp * u[c, r + 1] + fxm * u[c, r - 1]
            y = y + fzp * up_z(x) + down_z(fzp * x)
            t[c, r] = E1 * x + E2 * (dm * y)
        return 0

    lax.fori_loop(1, 7, first, 0)

    def store(c, i, y):
        out[c, i] = E0 * u[c, i + 2, LO:HI] + y

    for i in range(ROWS):
        couple(i, v, d, fz, t, lambda c, y: store(c, i, y))


def couple(i, v, d, fz, t, done):
    own_rows = slice(LO, HI)
    above = slice(LO + 1, HI + 1)
    under = slice(LO - 1, HI - 1)
    r = i + 2
    vm = v[r + 1, own_rows]
    fyp = vm + v[r + 1, above]
    fym = vm + v[r + 1, under]
    fxp, fxm = vm + v[r + 2, own_rows], vm + v[r, own_rows]
    fzp, dm = fz[r, own_rows], d[r, own_rows]
    for c in range(2):
        x = t[c, r, own_rows]
        y = fyp * t[c, r, above] + fym * t[c, r, under]
        y = y + fxp * t[c, r + 1, own_rows] + fxm * t[c, r - 1, own_rows]
        y = y + fzp * up_z(x) + down_z(fzp * x)
        done(c, dm * y)


def velocity_kernel(basis, dots, onehot, h0, ex, ez, v, d, fz, forced, vel_hbm, press, vel, t, b, bz, sems):
    sums = jnp.sum(jnp.sum(dots[...], axis=0), axis=1, keepdims=True)
    gg, gh, hh, hkh = sums[0:1], sums[1:2], sums[2:3], sums[3:4]
    alpha0 = gg / gh
    fresh = gg - 2.0 * alpha0 * gh + alpha0 * alpha0 * hh
    beta = fresh / gg
    grow = 1.0 + beta
    alpha1 = fresh / (grow * grow * gh - 2.0 * grow * alpha0 * hh + alpha0 * alpha0 * hkh)
    on_g = alpha0 + alpha1 * grow
    on_h = alpha1 * alpha0
    grad = on_g * basis[0:16] - on_h * basis[16:32]
    b[...] = grad
    bz[0:16] = up_z(grad)
    bz[16:32] = down_z(grad)
    p = on_g * basis[32:40] - on_h * basis[40:48]
    press[...] = jnp.dot(
        p, onehot[...], precision=lax.Precision.HIGHEST, preferred_element_type=jnp.float32
    )[0:4]

    def first(r, _):
        h, exi, exm, ezi = h0[r], ex[r], ex[r - 1], ez[r]
        ezm = down_z(ezi)
        for c in range(2):
            at = 8 * c + r
            y = h * b[pl.ds(at, 1)] + exi * b[pl.ds(at + 1, 1)] + exm * b[pl.ds(at - 1, 1)]
            t[c, r] = y + ezi * bz[pl.ds(at, 1)] + ezm * bz[pl.ds(16 + at, 1)]
        return 0

    lax.fori_loop(1, 7, first, 0)

    def store(c, i, y):
        own = E0 * (d[i + 2, LO:HI] * b[pl.ds(8 * c + i + 2, 1)])
        vel[c, i] = forced[c, i] - (own + y)

    saves = []
    for i in range(ROWS):
        couple(i, v, d, fz, t, lambda c, y: store(c, i, y))
        saves.append(pltpu.make_async_copy(vel.at[:, i], vel_hbm.at[:, i], sems.at[i]))
        saves[-1].start()
    for copy in saves:
        copy.wait()


VMEM = pl.BlockSpec(memory_space=pltpu.VMEM)
SMEM = pl.BlockSpec(memory_space=pltpu.SMEM)
ANY = pl.BlockSpec(memory_space=pl.ANY)
HBM = pl.BlockSpec(memory_space=pltpu.HBM)


def call(kernel, out_shape, scratch, args, in_specs, out_specs=None, micros=1.0, sems=0, mib=16):
    return pl.pallas_call(
        kernel,
        out_shape=out_shape,
        in_specs=in_specs,
        out_specs=out_specs or jax.tree.map(lambda _: VMEM, out_shape),
        scratch_shapes=[pltpu.VMEM(s, jnp.float32) for s in scratch]
        + ([pltpu.SemaphoreType.DMA((sems,))] if sems else []),
        compiler_params=pltpu.CompilerParams(vmem_limit_bytes=mib * 1024 * 1024),
        cost_estimate=pl.CostEstimate(flops=0, transcendentals=0, bytes_accessed=int(micros * 3.6e6)),
    )(*args)


def in_hbm(x):
    return pltpu.with_memory_space_constraint(x, pltpu.HBM)


def f32(*shape):
    return jax.ShapeDtypeStruct(shape, jnp.float32)


def pairs(n, first):
    up = [(i, i + 1) for i in range(first, n - 1, 2)]
    return up + [(b, a) for a, b in up]


def shards(forcing, viscosity, owner_slot):
    slabs, cross = lax.axis_size("slab"), lax.axis_size("cross")
    slab = lax.axis_index("slab")
    par = slab % 2
    where = jnp.stack([par, slab // 2, lax.axis_index("cross") % 2, slab // 2 % 2]).astype(jnp.int32)
    mates, others = pairs(slabs, 0), pairs(slabs, 1)
    chips = slabs // 2
    first_chips = [(2 * a + c, 2 * b + c) for a, b in pairs(chips, 0) for c in range(2)]
    second_chips = [(2 * a + c, 2 * b + c) for a, b in pairs(chips, 1) for c in range(2)]

    edges = call(
        edge_kernel,
        f32(ROWS, 14, NZ),
        [(ROWS, 8, NZ)] * 2 + [(2, ROWS, 8, NZ)] * 2,
        (where, in_hbm(viscosity), in_hbm(forcing)),
        in_specs=[SMEM, ANY, ANY],
        sems=4,
        mib=4,
    )
    od_e = lax.ppermute(edges, "slab", others)
    ev_e = lax.ppermute(edges, "slab", mates)
    layers = pltpu.HBM((7, NY, NZ), jnp.float32)
    to_od, to_ev = call(
        pack_kernel,
        (layers, layers),
        [(ROWS, NY, NZ), (2, ROWS, NY, NZ)],
        (where, in_hbm(viscosity), in_hbm(forcing)),
        in_specs=[SMEM, ANY, ANY],
        out_specs=(HBM, HBM),
        micros=2,
        sems=8,
        mib=4,
    )
    od_e, ev_e, to_od, to_ev = lax.optimization_barrier((od_e, ev_e, to_od, to_ev))
    od = lax.ppermute(to_od, "slab", others)
    ev = lax.ppermute(to_ev, "slab", mates)
    first, second = call(
        corner_kernel,
        (f32(40, NZ), f32(40, NZ)),
        [(40, NZ), (40, NZ)],
        (where, edges, od_e, ev_e),
        in_specs=[SMEM] + [VMEM] * 3,
        mib=4,
    )
    first = lax.ppermute(first, "cross", pairs(cross, 0))
    second = lax.ppermute(second, "cross", pairs(cross, 1))

    kept = (f32(10, FRAME, NZ), f32(8, FRAME, NZ), f32(8, FRAME, NZ)) + (f32(7, FRAME, NZ),) * 3
    part, v, d, fz, h0, ex, ez = call(
        stencil_kernel,
        (f32(10, 4, NZ), *[pltpu.HBM(x.shape, x.dtype) for x in kept]),
        [x.shape for x in kept] + [(7, FRAME, NZ), (32, 1, NZ), (2, ROWS, NY, NZ)],
        (where, in_hbm(viscosity), od, ev, first, second, in_hbm(forcing)),
        in_specs=[SMEM, ANY, ANY, ANY, VMEM, VMEM, ANY],
        out_specs=(VMEM,) + (HBM,) * 6,
        micros=6,
        sems=10,
    )

    width = owner_slot.shape[0] // cross
    column = lax.axis_index("cross") * width + jnp.arange(width, dtype=jnp.int32)
    onehot = (owner_slot[:, None] == column[None, :]).astype(jnp.float32)

    def among(x, step):
        return [lax.ppermute(x, "cross", [(i, i ^ (n * step)) for i in range(cross)]) for n in (1, 2, 3)]

    part, onehot = lax.optimization_barrier((part, onehot))
    got = among(part, 1)
    part = part + got[0] + got[1] + got[2]
    got = among(part, 4)
    forced = call(
        forced_kernel,
        f32(2, ROWS, NY, NZ),
        [x.shape for x in kept[:3]] + [(2, 8, FRAME, NZ)] * 2,
        (where, in_hbm(forcing), od, ev, first, second, in_hbm(v), in_hbm(d), in_hbm(fz)),
        in_specs=[SMEM] + [ANY] * 3 + [VMEM] * 2 + [ANY] * 3,
        micros=5,
        sems=9,
    )
    got, forced = lax.optimization_barrier((got, forced))
    part = part + got[0] + got[1] + got[2]

    mate = lax.ppermute(part, "slab", mates)
    both = jnp.stack([part, mate])
    window = (lax.ppermute(both, "slab", first_chips), lax.ppermute(both, "slab", second_chips))
    basis, dots = call(
        krylov_kernel,
        (f32(48, NZ), f32(chips, 8, 128)),
        [(7, 24, NZ), (40, NZ)],
        (where, part, mate, *window),
        in_specs=[SMEM] + [VMEM] * 4,
        mib=4,
    )
    groups = [[2 * z + c for z in range(chips)] for c in range(2)]
    dots = lax.all_to_all(dots, "slab", 0, 0, tiled=True, axis_index_groups=groups)

    return call(
        velocity_kernel,
        (pltpu.HBM((2, ROWS, NY, NZ), jnp.float32), f32(ROWS, width)),
        [(2, ROWS, NY, NZ), (2, 8, FRAME, NZ), (16, NZ), (32, NZ)],
        (basis, dots, onehot, h0, ex, ez, v, d, fz, forced),
        in_specs=[VMEM] * 10,
        out_specs=(HBM, VMEM),
        micros=4,
        sems=4,
    )


def solution(mesh):
    in_specs = (P(None, "slab", "cross", None), P("slab", "cross", None), P())
    out_specs = (P(None, "slab", "cross", None), P("slab", "cross"))
    return jax.shard_map(shards, mesh=mesh, in_specs=in_specs, out_specs=out_specs, check_vma=False)
```

```python
import functools

import jax
import jax.numpy as jnp
from jax import lax
from jax.experimental import pallas as pl
from jax.experimental.pallas import tpu as pltpu
from jax.sharding import PartitionSpec as P

OUTER = 2
DEGREE = 3
cheb_theta = 1.025
cheb_delta = 0.975


def series():
    sigma = cheb_theta / cheb_delta
    rho0 = 1.0 / sigma
    rho1 = 1.0 / (2.0 * sigma - rho0)
    rho2 = 1.0 / (2.0 * sigma - rho1)
    g1, g2 = 2.0 * rho1 / cheb_delta, 2.0 * rho2 / cheb_delta
    p0, p1 = (1.0 + rho1 * rho0) / cheb_theta + g1, -g1 / cheb_theta
    q = rho2 * rho1
    c0 = (1.0 + q) * p0 - q / cheb_theta + g2
    c1 = (1.0 + q) * p1 - g2 * p0
    c2 = -g2 * p1
    return c0 + c1 + c2, -c1 - 2.0 * c2, c2


E0, E1, E2 = (2.0 * e for e in series())

NY, NZ = 64, 512
ROWS = 4
FRAME = 80
LO, HI = 8, 72
FORWARD = ((0, 0), (0, 1), (0, 2), (1, -1), (1, 0), (1, 1), (2, 0))
PAYLOAD = 40


def up_z(x):
    return pltpu.roll(x, NZ - 1, x.ndim - 1)


def down_z(x):
    return pltpu.roll(x, 1, x.ndim - 1)


def lane(shape):
    return lax.broadcasted_iota(jnp.int32, shape, len(shape) - 1)


def edge_kernel(par_ref, own, f, out, low_v, high_v, low_f, high_f, sems):
    copies = [
        pltpu.make_async_copy(own.at[:, 0:8], low_v, sems.at[0]),
        pltpu.make_async_copy(own.at[:, NY - 8 : NY], high_v, sems.at[1]),
        pltpu.make_async_copy(f.at[:, :, 0:8], low_f, sems.at[2]),
        pltpu.make_async_copy(f.at[:, :, NY - 8 : NY], high_f, sems.at[3]),
    ]
    for copy in copies:
        copy.start()
    for copy in copies:
        copy.wait()
    out[:, 0:3] = low_v[:, 0:3]
    out[:, 7:10] = high_v[:, 5:8]
    for c in range(2):
        out[:, 3 + 2 * c : 5 + 2 * c] = low_f[c, :, 0:2]
        out[:, 10 + 2 * c : 12 + 2 * c] = high_f[c, :, 6:8]


def pack_kernel(par_ref, own_hbm, f_hbm, to_od, to_ev, own, f, sems):
    par = par_ref[0]
    copies = []
    for n, (out, last) in enumerate(((to_od, par), (to_ev, 1 - par))):
        copies.append(pltpu.make_async_copy(own_hbm.at[pl.ds(last, 3)], out.at[0:3], sems.at[3 * n]))
        for c in range(2):
            copies.append(
                pltpu.make_async_copy(
                    f_hbm.at[c, pl.ds(2 * last, 2)], out.at[3 + 2 * c : 5 + 2 * c], sems.at[1 + 3 * n + c]
                )
            )
    copies.append(pltpu.make_async_copy(own_hbm, own, sems.at[6]))
    copies.append(pltpu.make_async_copy(f_hbm, f, sems.at[7]))
    for copy in copies:
        copy.start()
    for copy in copies:
        copy.wait()


def corner_kernel(par_ref, own, od, ev, first, second, low, high):
    odd = par_ref[0] == 1
    below = lax.select(odd, ev[2:4], od[2:4])
    above = lax.select(odd, od[0:2], ev[0:2])
    for out, near, forced, base in ((low, (0, 2), 0, 0), (high, (1, 3), 1, 7)):
        for n in range(4):
            out[7 * n : 7 * n + 7] = own[n, base : base + 7]
        for at, x, far, far_at in ((28, below[1], below[0], 36), (32, above[0], above[1], 37)):
            out[at : at + 2] = x[base + near[0] : base + near[1]]
            for c in range(2):
                row = base + 3 + 2 * c + forced
                out[at + 2 + c : at + 3 + c] = x[row : row + 1]
            row = base + 2 * forced
            out[far_at : far_at + 1] = far[row : row + 1]
        out[38:40] = jnp.zeros((2, NZ), jnp.float32)
    odd = par_ref[2] == 1
    first[...] = lax.select(odd, low[...], high[...])
    second[...] = lax.select(odd, high[...], low[...])


def sides(odd, first, second):
    return lax.select(odd, first[...], second[...]), lax.select(odd, second[...], first[...])


def fill_viscosity(par, v, own, od, ev, lo, hi, sems):
    copies = [pltpu.make_async_copy(own, v.at[3:7, LO:HI], sems.at[0])]
    for n, at, x in ((1, par * 7, od), (2, 7 - par * 7, ev)):
        copies.append(pltpu.make_async_copy(x.at[0:3], v.at[pl.ds(at, 3), LO:HI], sems.at[n]))
    for copy in copies:
        copy.start()
    for n in range(4):
        v[3 + n, LO - 3 : LO] = lo[7 * n : 7 * n + 3]
        v[3 + n, HI : HI + 3] = hi[7 * n : 7 * n + 3]
    for r, at in ((2, 28), (7, 32)):
        v[r, LO - 2 : LO] = lo[at : at + 2]
        v[r, HI : HI + 2] = hi[at : at + 2]
    for r, at in ((1, 36), (8, 37)):
        v[r, LO - 1 : LO] = lo[at : at + 1]
        v[r, HI : HI + 1] = hi[at : at + 1]
    for copy in copies:
        copy.wait()


def fill_inverse(v, d, fz):
    ids = lane((FRAME, NZ))

    def layer(r, _):
        mid = v[r + 1]
        nxt = jnp.where(ids == NZ - 1, 0.0, up_z(mid))
        prv = jnp.where(ids == 0, 0.0, down_z(mid))
        total = 6.0 * mid + v[r] + v[r + 2] + nxt + prv
        total = total + pltpu.roll(mid, 1, 0) + pltpu.roll(mid, FRAME - 1, 0)
        d[r] = jnp.where(mid > 0.0, 1.0 / total, 0.0)
        fz[r] = jnp.where(ids == NZ - 1, 0.0, mid + nxt)
        return 0

    lax.fori_loop(0, 8, layer, 0)


def stencil_kernel(par_ref, own, od, ev, first, second, f, out, v, d, fz, h0, ex, ez, ezm, acc, sems):
    par = par_ref[0]
    lo, hi = sides(par_ref[2] == 1, first, second)
    fill_viscosity(par, v, own, od, ev, lo, hi, sems)
    fill_inverse(v, d, fz)

    def edges(r, _):
        dm, vm = d[r], v[r + 1]
        ex[r] = E2 * dm * (vm + v[r + 2]) * d[r + 1]
        dy = pltpu.roll(dm, FRAME - 1, 0)
        ey = E2 * dm * (vm + pltpu.roll(vm, FRAME - 1, 0)) * dy
        h0[r] = E1 * dm + ey + pltpu.roll(ey, 1, 0)
        e = E2 * dm * fz[r] * up_z(dm)
        ez[r] = e
        ezm[r] = down_z(e)
        return 0

    lax.fori_loop(0, 7, edges, 0)

    acc[...] = jnp.zeros_like(acc)
    own_rows = slice(LO, HI)
    above = slice(LO + 1, HI + 1)
    under = slice(LO - 1, HI - 1)

    def layer(i, _):
        r = i + 2
        vm = v[r + 1, own_rows]
        fyp = vm + v[r + 1, above]
        fym = vm + v[r + 1, under]
        fxp = vm + v[r + 2, own_rows]
        fxm = vm + v[r, own_rows]
        fzp = fz[r, own_rows]
        fzm = down_z(fzp)
        dm = d[r, own_rows]
        u0, u1 = dm * f[0, i], dm * f[1, i]

        def weigh(di, dk, s):
            for c, u in ((0, u0), (1, u1)):
                row = jnp.sum(u * s, axis=0, keepdims=True)
                if dk:
                    row = pltpu.roll(row, dk % NZ, 1)
                at = pl.ds(16 * c + i + di + 2, 1)
                acc[at] = acc[at] + row[None]
            if (di, dk) in FORWARD:
                out[FORWARD.index((di, dk)), pl.ds(i, 1)] = jnp.sum(dm * s, axis=0, keepdims=True)

        exi, exm = ex[r, own_rows], ex[r - 1, own_rows]
        ezi, ezmi = ez[r, own_rows], ezm[r, own_rows]
        h = h0[r, own_rows]
        weigh(
            0,
            0,
            E0
            + fyp * h0[r, above]
            + fym * h0[r, under]
            + fxp * exi
            + fxm * exm
            + fzp * ezi
            + fzm * ezmi,
        )
        weigh(1, 0, fyp * ex[r, above] + fym * ex[r, under] + fxp * h0[r + 1, own_rows])
        weigh(-1, 0, fyp * ex[r - 1, above] + fym * ex[r - 1, under] + fxm * h0[r - 1, own_rows])
        weigh(0, 1, fyp * ez[r, above] + fym * ez[r, under] + fzp * up_z(h))
        weigh(0, -1, fyp * ezm[r, above] + fym * ezm[r, under] + fzm * down_z(h))
        weigh(2, 0, fxp * ex[r + 1, own_rows])
        weigh(-2, 0, fxm * ex[r - 2, own_rows])
        weigh(0, 2, fzp * up_z(ezi))
        weigh(0, -2, fzm * down_z(ezmi))
        weigh(1, 1, fxp * ez[r + 1, own_rows] + fzp * up_z(exi))
        weigh(1, -1, fxp * ezm[r + 1, own_rows] + fzm * down_z(exi))
        weigh(-1, 1, fxm * ez[r - 1, own_rows] + fzp * up_z(exm))
        weigh(-1, -1, fxm * ezm[r - 1, own_rows] + fzm * down_z(exm))
        return 0

    lax.fori_loop(0, ROWS, layer, 0)

    cx = acc[0:16, 0]
    cz = acc[16:32, 0]
    zero = lane((16, NZ)) == 0
    e = cx - pltpu.roll(cx, 1, 0) + cz - jnp.where(zero, 0.0, down_z(cz))
    out[7:9] = e[0:8].reshape(2, 4, NZ)
    out[9, 0:1] = e[8:9]
    out[9, 1:4] = jnp.zeros((3, NZ), jnp.float32)


def krylov_kernel(par_ref, mine, mate, first, second, basis, dots, s_ref, g_ref):
    par, chip = par_ref[0], par_ref[1]
    odd = par == 1

    def pair(a, b):
        return lax.select(odd, b, a), lax.select(odd, a, b)

    slabs = []
    below, above = sides(par_ref[3] == 1, first, second)
    for a, b in ((below[0], below[1]), (mine[...], mate[...]), (above[0], above[1])):
        slabs += pair(a, b)
    W = 24
    g_ref[...] = jnp.zeros_like(g_ref)
    for n, slab in enumerate(slabs):
        for o in range(7):
            s_ref[o, 4 * n : 4 * n + 4] = slab[o]
        flat = slab[7:10].reshape(12, NZ)[0:9]
        at = 8 + 4 * n - 2
        g_ref[at : at + 9] = g_ref[at : at + 9] + flat
    ids = lane((W, NZ))
    layer = lax.broadcasted_iota(jnp.int32, (W, NZ), 0) - 8 + 8 * chip
    inside = jnp.logical_and(layer >= 0, layer < 64)

    def next_layer(x, n=1):
        return pltpu.roll(x, (W - n) % W, 0)

    def shift(x, di, dk):
        if di:
            x = pltpu.roll(x, (-di) % W, 0)
        if dk:
            x = pltpu.roll(x, (-dk) % NZ, 1)
        return x

    def spread(q):
        qx = q - next_layer(q)
        qz = q - jnp.where(ids == NZ - 1, 0.0, up_z(q))
        return qx, qz

    def times_s(b):
        total = None
        for n, (di, dk) in enumerate(FORWARD):
            s = s_ref[n]
            if n == 0:
                total = s * b
            else:
                total = total + s * shift(b, di, dk) + shift(s * b, -di, -dk)
        return total

    g = jnp.where(inside, g_ref[8 : 8 + W], 0.0)
    gx, gz = spread(g)
    tx, tz = times_s(gx), times_s(gz)
    h = tx - pltpu.roll(tx, 1, 0) + tz - jnp.where(ids == 0, 0.0, down_z(tz))
    h = jnp.where(inside, h, 0.0)
    hx, hz = spread(h)
    energy = hx * times_s(hx) + hz * times_s(hz)

    def own(x):
        return lax.select(odd, pltpu.roll(x, W - 4, 0), x)

    for n, x in enumerate((gx, gz, hx, hz)):
        basis[8 * n : 8 * n + 8] = own(x)[6:14]
    basis[32:40] = own(g)[8:16]
    basis[40:48] = own(h)[8:16]
    rows = []
    for x in (g * g, g * h, h * h, energy):
        part = x[8:16]
        part = part[:, 0:128] + part[:, 128:256] + part[:, 256:384] + part[:, 384:512]
        rows.append(jnp.sum(part, axis=0, keepdims=True))
    packed = jnp.concatenate(rows + [jnp.zeros((4, 128), jnp.float32)], 0)
    dots[...] = jnp.broadcast_to(packed[None], dots.shape)


def forced_kernel(par_ref, f, od, ev, first, second, v, d, fz, out, u, t):
    par = par_ref[0]
    lo, hi = sides(par_ref[2] == 1, first, second)

    def scale(i, _):
        dm = d[i + 2, LO:HI]
        for c in range(2):
            u[c, i + 2, LO:HI] = dm * f[c, i]
        return 0

    lax.fori_loop(0, ROWS, scale, 0)
    for at, x in ((par * 6, od), (6 - par * 6, ev)):
        dm = d[pl.ds(at, 2), LO:HI]
        for c in range(2):
            u[c, pl.ds(at, 2), LO:HI] = dm * x[3 + 2 * c : 5 + 2 * c]
    for c in range(2):
        for n in range(4):
            u[c, 2 + n, LO - 2 : LO] = d[2 + n, LO - 2 : LO] * lo[7 * n + 3 + 2 * c : 7 * n + 5 + 2 * c]
            u[c, 2 + n, HI : HI + 2] = d[2 + n, HI : HI + 2] * hi[7 * n + 3 + 2 * c : 7 * n + 5 + 2 * c]
        for r, at in ((1, 30), (6, 34)):
            u[c, r, LO - 1 : LO] = d[r, LO - 1 : LO] * lo[at + c : at + c + 1]
            u[c, r, HI : HI + 1] = d[r, HI : HI + 1] * hi[at + c : at + c + 1]

    def first(r, _):
        vm = v[r + 1]
        fy = vm + pltpu.roll(vm, FRAME - 1, 0)
        fxp, fxm = vm + v[r + 2], vm + v[r]
        fzp, dm = fz[r], d[r]
        for c in range(2):
            x = u[c, r]
            y = fy * pltpu.roll(x, FRAME - 1, 0) + pltpu.roll(fy * x, 1, 0)
            y = y + fxp * u[c, r + 1] + fxm * u[c, r - 1]
            y = y + fzp * up_z(x) + down_z(fzp * x)
            t[c, r] = E1 * x + E2 * (dm * y)
        return 0

    lax.fori_loop(1, 7, first, 0)

    def store(c, i, y):
        out[c, i] = E0 * u[c, i + 2, LO:HI] + y

    for i in range(ROWS):
        couple(i, v, d, fz, t, lambda c, y: store(c, i, y))


def couple(i, v, d, fz, t, done):
    own_rows = slice(LO, HI)
    above = slice(LO + 1, HI + 1)
    under = slice(LO - 1, HI - 1)
    r = i + 2
    vm = v[r + 1, own_rows]
    fyp = vm + v[r + 1, above]
    fym = vm + v[r + 1, under]
    fxp, fxm = vm + v[r + 2, own_rows], vm + v[r, own_rows]
    fzp, dm = fz[r, own_rows], d[r, own_rows]
    for c in range(2):
        x = t[c, r, own_rows]
        y = fyp * t[c, r, above] + fym * t[c, r, under]
        y = y + fxp * t[c, r + 1, own_rows] + fxm * t[c, r - 1, own_rows]
        y = y + fzp * up_z(x) + down_z(fzp * x)
        done(c, dm * y)


def velocity_kernel(basis, dots, onehot, h0, ex, ez, v, d, fz, forced, vel_hbm, press, vel, t, b, bz, sems):
    sums = jnp.sum(jnp.sum(dots[...], axis=0), axis=1, keepdims=True)
    gg, gh, hh, hkh = sums[0:1], sums[1:2], sums[2:3], sums[3:4]
    alpha0 = gg / gh
    fresh = gg - 2.0 * alpha0 * gh + alpha0 * alpha0 * hh
    beta = fresh / gg
    grow = 1.0 + beta
    alpha1 = fresh / (grow * grow * gh - 2.0 * grow * alpha0 * hh + alpha0 * alpha0 * hkh)
    on_g = alpha0 + alpha1 * grow
    on_h = alpha1 * alpha0
    grad = on_g * basis[0:16] - on_h * basis[16:32]
    b[...] = grad
    bz[0:16] = up_z(grad)
    bz[16:32] = down_z(grad)
    p = on_g * basis[32:40] - on_h * basis[40:48]
    press[...] = jnp.dot(
        p, onehot[...], precision=lax.Precision.HIGHEST, preferred_element_type=jnp.float32
    )[0:4]

    def first(r, _):
        h, exi, exm, ezi = h0[r], ex[r], ex[r - 1], ez[r]
        ezm = down_z(ezi)
        for c in range(2):
            at = 8 * c + r
            y = h * b[pl.ds(at, 1)] + exi * b[pl.ds(at + 1, 1)] + exm * b[pl.ds(at - 1, 1)]
            t[c, r] = y + ezi * bz[pl.ds(at, 1)] + ezm * bz[pl.ds(16 + at, 1)]
        return 0

    lax.fori_loop(1, 7, first, 0)

    def store(c, i, y):
        own = E0 * (d[i + 2, LO:HI] * b[pl.ds(8 * c + i + 2, 1)])
        vel[c, i] = forced[c, i] - (own + y)

    saves = []
    for i in range(ROWS):
        couple(i, v, d, fz, t, lambda c, y: store(c, i, y))
        saves.append(pltpu.make_async_copy(vel.at[:, i], vel_hbm.at[:, i], sems.at[i]))
        saves[-1].start()
    for copy in saves:
        copy.wait()


VMEM = pl.BlockSpec(memory_space=pltpu.VMEM)
SMEM = pl.BlockSpec(memory_space=pltpu.SMEM)
ANY = pl.BlockSpec(memory_space=pl.ANY)
HBM = pl.BlockSpec(memory_space=pltpu.HBM)


def call(kernel, out_shape, scratch, args, in_specs, out_specs=None, micros=1.0, sems=0, mib=16):
    return pl.pallas_call(
        kernel,
        out_shape=out_shape,
        in_specs=in_specs,
        out_specs=out_specs or jax.tree.map(lambda _: VMEM, out_shape),
        scratch_shapes=[pltpu.VMEM(s, jnp.float32) for s in scratch]
        + ([pltpu.SemaphoreType.DMA((sems,))] if sems else []),
        compiler_params=pltpu.CompilerParams(vmem_limit_bytes=mib * 1024 * 1024),
        cost_estimate=pl.CostEstimate(flops=0, transcendentals=0, bytes_accessed=int(micros * 3.6e6)),
    )(*args)


def in_vmem(x):
    return pltpu.with_memory_space_constraint(x, pltpu.VMEM)


def in_hbm(x):
    return pltpu.with_memory_space_constraint(x, pltpu.HBM)


def f32(*shape):
    return jax.ShapeDtypeStruct(shape, jnp.float32)


def pairs(n, first):
    up = [(i, i + 1) for i in range(first, n - 1, 2)]
    return up + [(b, a) for a, b in up]


def shards(forcing, viscosity, owner_slot):
    slabs, cross = lax.axis_size("slab"), lax.axis_size("cross")
    slab = lax.axis_index("slab")
    par = slab % 2
    where = jnp.stack([par, slab // 2, lax.axis_index("cross") % 2, slab // 2 % 2]).astype(jnp.int32)
    mates, others = pairs(slabs, 0), pairs(slabs, 1)
    chips = slabs // 2
    first_chips = [(2 * a + c, 2 * b + c) for a, b in pairs(chips, 0) for c in range(2)]
    second_chips = [(2 * a + c, 2 * b + c) for a, b in pairs(chips, 1) for c in range(2)]

    edges = call(
        edge_kernel,
        f32(ROWS, 14, NZ),
        [(ROWS, 8, NZ)] * 2 + [(2, ROWS, 8, NZ)] * 2,
        (where, in_hbm(viscosity), in_hbm(forcing)),
        in_specs=[SMEM, ANY, ANY],
        sems=4,
        mib=4,
    )
    od_e = lax.ppermute(edges, "slab", others)
    ev_e = lax.ppermute(edges, "slab", mates)
    layers = pltpu.VMEM((7, NY, NZ), jnp.float32)
    to_od, to_ev, own, f = call(
        pack_kernel,
        (layers, layers, pltpu.VMEM(viscosity.shape, jnp.float32), pltpu.VMEM(forcing.shape, jnp.float32)),
        [],
        (where, in_hbm(viscosity), in_hbm(forcing)),
        in_specs=[SMEM, ANY, ANY],
        micros=2,
        sems=8,
        mib=4,
    )
    od_e, ev_e, to_od, to_ev = lax.optimization_barrier((od_e, ev_e, to_od, to_ev))
    od = lax.ppermute(to_od, "slab", others)
    ev = lax.ppermute(to_ev, "slab", mates)
    first, second = call(
        corner_kernel,
        (f32(40, NZ), f32(40, NZ)),
        [(40, NZ), (40, NZ)],
        (where, in_vmem(edges), in_vmem(od_e), in_vmem(ev_e)),
        in_specs=[SMEM] + [VMEM] * 3,
        mib=4,
    )
    first = lax.ppermute(first, "cross", pairs(cross, 0))
    second = lax.ppermute(second, "cross", pairs(cross, 1))

    kept = (f32(10, FRAME, NZ), f32(8, FRAME, NZ), f32(8, FRAME, NZ)) + (f32(7, FRAME, NZ),) * 3
    part, v, d, fz, h0, ex, ez = call(
        stencil_kernel,
        (f32(10, 4, NZ), *[pltpu.VMEM(x.shape, x.dtype) for x in kept]),
        [(7, FRAME, NZ), (32, 1, NZ)],
        (where, in_vmem(own), in_vmem(od), in_vmem(ev), first, second, in_vmem(f)),
        in_specs=[SMEM] + [VMEM] * 6,
        micros=6,
        sems=4,
        mib=6,
    )

    width = owner_slot.shape[0] // cross
    column = lax.axis_index("cross") * width + jnp.arange(width, dtype=jnp.int32)
    onehot = (owner_slot[:, None] == column[None, :]).astype(jnp.float32)

    def among(x, step):
        return [lax.ppermute(x, "cross", [(i, i ^ (n * step)) for i in range(cross)]) for n in (1, 2, 3)]

    part, onehot = lax.optimization_barrier((part, onehot))
    got = among(part, 1)
    part = part + got[0] + got[1] + got[2]
    got = among(part, 4)
    forced = call(
        forced_kernel,
        pltpu.VMEM((2, ROWS, NY, NZ), jnp.float32),
        [(2, 8, FRAME, NZ)] * 2,
        (where, in_vmem(f), in_vmem(od), in_vmem(ev), first, second, in_vmem(v), in_vmem(d), in_vmem(fz)),
        in_specs=[SMEM] + [VMEM] * 8,
        micros=5,
        mib=8,
    )
    got, forced = lax.optimization_barrier((got, forced))
    part = part + got[0] + got[1] + got[2]

    mate = lax.ppermute(part, "slab", mates)
    both = jnp.stack([part, mate])
    window = (lax.ppermute(both, "slab", first_chips), lax.ppermute(both, "slab", second_chips))
    basis, dots = call(
        krylov_kernel,
        (f32(48, NZ), f32(chips, 8, 128)),
        [(7, 24, NZ), (40, NZ)],
        (where, part, mate, *window),
        in_specs=[SMEM] + [VMEM] * 4,
        mib=4,
    )
    groups = [[2 * z + c for z in range(chips)] for c in range(2)]
    dots = lax.all_to_all(dots, "slab", 0, 0, tiled=True, axis_index_groups=groups)

    return call(
        velocity_kernel,
        (pltpu.HBM((2, ROWS, NY, NZ), jnp.float32), f32(ROWS, width)),
        [(2, ROWS, NY, NZ), (2, 8, FRAME, NZ), (16, NZ), (32, NZ)],
        (basis, dots, onehot, *[in_vmem(x) for x in (h0, ex, ez, v, d, fz, forced)]),
        in_specs=[VMEM] * 10,
        out_specs=(HBM, VMEM),
        micros=4,
        sems=4,
        mib=8,
    )


def solution(mesh):
    in_specs = (P(None, "slab", "cross", None), P("slab", "cross", None), P())
    out_specs = (P(None, "slab", "cross", None), P("slab", "cross"))
    return jax.shard_map(shards, mesh=mesh, in_specs=in_specs, out_specs=out_specs, check_vma=False)
```

```python
import functools

import jax
import jax.numpy as jnp
from jax import lax
from jax.experimental import pallas as pl
from jax.experimental.pallas import tpu as pltpu
from jax.sharding import PartitionSpec as P

OUTER = 2
DEGREE = 3
cheb_theta = 1.025
cheb_delta = 0.975


def series():
    sigma = cheb_theta / cheb_delta
    rho0 = 1.0 / sigma
    rho1 = 1.0 / (2.0 * sigma - rho0)
    rho2 = 1.0 / (2.0 * sigma - rho1)
    g1, g2 = 2.0 * rho1 / cheb_delta, 2.0 * rho2 / cheb_delta
    p0, p1 = (1.0 + rho1 * rho0) / cheb_theta + g1, -g1 / cheb_theta
    q = rho2 * rho1
    c0 = (1.0 + q) * p0 - q / cheb_theta + g2
    c1 = (1.0 + q) * p1 - g2 * p0
    c2 = -g2 * p1
    return c0 + c1 + c2, -c1 - 2.0 * c2, c2


E0, E1, E2 = (2.0 * e for e in series())

NY, NZ = 64, 512
ROWS = 4
FRAME = 80
LO, HI = 8, 72
FORWARD = ((0, 0), (0, 1), (0, 2), (1, -1), (1, 0), (1, 1), (2, 0))
PAYLOAD = 40


def up_z(x):
    return pltpu.roll(x, NZ - 1, x.ndim - 1)


def down_z(x):
    return pltpu.roll(x, 1, x.ndim - 1)


def lane(shape):
    return lax.broadcasted_iota(jnp.int32, shape, len(shape) - 1)


def edge_kernel(own_hbm, f_hbm, out, own, f, sems):
    copies = [pltpu.make_async_copy(own_hbm, own, sems.at[0]), pltpu.make_async_copy(f_hbm, f, sems.at[1])]
    for copy in copies:
        copy.start()
    copies[0].wait()
    out[:, 0:3] = own[:, 0:3]
    out[:, 7:10] = own[:, NY - 3 : NY]
    copies[1].wait()
    for c in range(2):
        out[:, 3 + 2 * c : 5 + 2 * c] = f[c, :, 0:2]
        out[:, 10 + 2 * c : 12 + 2 * c] = f[c, :, NY - 2 : NY]


def pack(par, own, f, to_od, to_ev, sems):
    copies = []
    for n, (out, last) in enumerate(((to_od, par), (to_ev, 1 - par))):
        copies.append(pltpu.make_async_copy(own.at[pl.ds(last, 3)], out.at[0:3], sems.at[3 * n]))
        for c in range(2):
            copies.append(
                pltpu.make_async_copy(
                    f.at[c, pl.ds(2 * last, 2)], out.at[3 + 2 * c : 5 + 2 * c], sems.at[1 + 3 * n + c]
                )
            )
    return copies


def corner_kernel(par_ref, own, od, ev, own_all, f_all, first, second, to_od, to_ev, low, high, sems):
    copies = pack(par_ref[0], own_all, f_all, to_od, to_ev, sems)
    for copy in copies:
        copy.start()
    odd = par_ref[0] == 1
    below = lax.select(odd, ev[2:4], od[2:4])
    above = lax.select(odd, od[0:2], ev[0:2])
    for out, near, forced, base in ((low, (0, 2), 0, 0), (high, (1, 3), 1, 7)):
        for n in range(4):
            out[7 * n : 7 * n + 7] = own[n, base : base + 7]
        for at, x, far, far_at in ((28, below[1], below[0], 36), (32, above[0], above[1], 37)):
            out[at : at + 2] = x[base + near[0] : base + near[1]]
            for c in range(2):
                row = base + 3 + 2 * c + forced
                out[at + 2 + c : at + 3 + c] = x[row : row + 1]
            row = base + 2 * forced
            out[far_at : far_at + 1] = far[row : row + 1]
        out[38:40] = jnp.zeros((2, NZ), jnp.float32)
    odd = par_ref[2] == 1
    first[...] = lax.select(odd, low[...], high[...])
    second[...] = lax.select(odd, high[...], low[...])
    for copy in copies:
        copy.wait()


def sides(odd, first, second):
    return lax.select(odd, first[...], second[...]), lax.select(odd, second[...], first[...])


def fill_viscosity(par, v, own, od, ev, lo, hi, sems):
    copies = [pltpu.make_async_copy(own, v.at[3:7, LO:HI], sems.at[0])]
    for n, at, x in ((1, par * 7, od), (2, 7 - par * 7, ev)):
        copies.append(pltpu.make_async_copy(x.at[0:3], v.at[pl.ds(at, 3), LO:HI], sems.at[n]))
    for copy in copies:
        copy.start()
    for n in range(4):
        v[3 + n, LO - 3 : LO] = lo[7 * n : 7 * n + 3]
        v[3 + n, HI : HI + 3] = hi[7 * n : 7 * n + 3]
    for r, at in ((2, 28), (7, 32)):
        v[r, LO - 2 : LO] = lo[at : at + 2]
        v[r, HI : HI + 2] = hi[at : at + 2]
    for r, at in ((1, 36), (8, 37)):
        v[r, LO - 1 : LO] = lo[at : at + 1]
        v[r, HI : HI + 1] = hi[at : at + 1]
    for copy in copies:
        copy.wait()


def fill_inverse(v, d, fz):
    ids = lane((FRAME, NZ))

    def layer(r, _):
        mid = v[r + 1]
        nxt = jnp.where(ids == NZ - 1, 0.0, up_z(mid))
        prv = jnp.where(ids == 0, 0.0, down_z(mid))
        total = 6.0 * mid + v[r] + v[r + 2] + nxt + prv
        total = total + pltpu.roll(mid, 1, 0) + pltpu.roll(mid, FRAME - 1, 0)
        d[r] = jnp.where(mid > 0.0, 1.0 / total, 0.0)
        fz[r] = jnp.where(ids == NZ - 1, 0.0, mid + nxt)
        return 0

    lax.fori_loop(0, 8, layer, 0)


def stencil_kernel(par_ref, own, od, ev, first, second, f, out, v, d, fz, h0, ex, ez, ezm, acc, s_acc, sems):
    par = par_ref[0]
    lo, hi = sides(par_ref[2] == 1, first, second)
    fill_viscosity(par, v, own, od, ev, lo, hi, sems)
    fill_inverse(v, d, fz)

    ex[0] = E2 * d[0] * (v[1] + v[2]) * d[1]

    def edges(r, _):
        dm, vm = d[r], v[r + 1]
        ex[r] = E2 * dm * (vm + v[r + 2]) * d[r + 1]
        dy = pltpu.roll(dm, FRAME - 1, 0)
        ey = E2 * dm * (vm + pltpu.roll(vm, FRAME - 1, 0)) * dy
        h0[r] = E1 * dm + ey + pltpu.roll(ey, 1, 0)
        e = E2 * dm * fz[r] * up_z(dm)
        ez[r] = e
        ezm[r] = down_z(e)
        return 0

    lax.fori_loop(1, 7, edges, 0)

    acc[...] = jnp.zeros_like(acc)
    own_rows = slice(LO, HI)
    above = slice(LO + 1, HI + 1)
    under = slice(LO - 1, HI - 1)

    def layer(i, _):
        r = i + 2
        vm = v[r + 1, own_rows]
        fyp = vm + v[r + 1, above]
        fym = vm + v[r + 1, under]
        fxp = vm + v[r + 2, own_rows]
        fxm = vm + v[r, own_rows]
        fzp = fz[r, own_rows]
        fzm = down_z(fzp)
        dm = d[r, own_rows]
        u0, u1 = dm * f[0, i], dm * f[1, i]

        def fold(x):
            return jnp.sum(x.reshape(8, 8, NZ), axis=0)

        def weigh(di, dk, s):
            for c, u in ((0, u0), (1, u1)):
                at = i + di + 2
                acc[dk + 2, c, at] = acc[dk + 2, c, at] + fold(u * s)
            if (di, dk) in FORWARD:
                s_acc[FORWARD.index((di, dk)), i] = fold(dm * s)

        exi, exm = ex[r, own_rows], ex[r - 1, own_rows]
        ezi, ezmi = ez[r, own_rows], ezm[r, own_rows]
        h = h0[r, own_rows]
        weigh(
            0,
            0,
            E0
            + fyp * h0[r, above]
            + fym * h0[r, under]
            + fxp * exi
            + fxm * exm
            + fzp * ezi
            + fzm * ezmi,
        )
        weigh(1, 0, fyp * ex[r, above] + fym * ex[r, under] + fxp * h0[r + 1, own_rows])
        weigh(-1, 0, fyp * ex[r - 1, above] + fym * ex[r - 1, under] + fxm * h0[r - 1, own_rows])
        weigh(0, 1, fyp * ez[r, above] + fym * ez[r, under] + fzp * up_z(h))
        weigh(0, -1, fyp * ezm[r, above] + fym * ezm[r, under] + fzm * down_z(h))
        weigh(2, 0, fxp * ex[r + 1, own_rows])
        weigh(-2, 0, fxm * ex[r - 2, own_rows])
        weigh(0, 2, fzp * up_z(ezi))
        weigh(0, -2, fzm * down_z(ezmi))
        weigh(1, 1, fxp * ez[r + 1, own_rows] + fzp * up_z(exi))
        weigh(1, -1, fxp * ezm[r + 1, own_rows] + fzm * down_z(exi))
        weigh(-1, 1, fxm * ez[r - 1, own_rows] + fzp * up_z(exm))
        weigh(-1, -1, fxm * ezm[r - 1, own_rows] + fzm * down_z(exm))
        return 0

    lax.fori_loop(0, ROWS, layer, 0)

    for n in range(7):
        out[n] = jnp.sum(s_acc[n], axis=1)

    def columns(c):
        total = jnp.sum(acc[2, c], axis=1)
        for dk in (-2, -1, 1, 2):
            total = total + pltpu.roll(jnp.sum(acc[dk + 2, c], axis=1), dk % NZ, 1)
        return jnp.concatenate([total, jnp.zeros((8, NZ), jnp.float32)], 0)

    cx, cz = columns(0), columns(1)
    zero = lane((16, NZ)) == 0
    e = cx - pltpu.roll(cx, 1, 0) + cz - jnp.where(zero, 0.0, down_z(cz))
    out[7:9] = e[0:8].reshape(2, 4, NZ)
    out[9, 0:1] = e[8:9]
    out[9, 1:4] = jnp.zeros((3, NZ), jnp.float32)


def krylov_kernel(par_ref, mine, mate, first, second, basis, dots, s_ref, g_ref):
    par, chip = par_ref[0], par_ref[1]
    odd = par == 1

    def pair(a, b):
        return lax.select(odd, b, a), lax.select(odd, a, b)

    slabs = []
    below, above = sides(par_ref[3] == 1, first, second)
    for a, b in ((below[0], below[1]), (mine[...], mate[...]), (above[0], above[1])):
        slabs += pair(a, b)
    W = 24
    g_ref[...] = jnp.zeros_like(g_ref)
    for n, slab in enumerate(slabs):
        for o in range(7):
            s_ref[o, 4 * n : 4 * n + 4] = slab[o]
        flat = slab[7:10].reshape(12, NZ)[0:9]
        at = 8 + 4 * n - 2
        g_ref[at : at + 9] = g_ref[at : at + 9] + flat
    ids = lane((W, NZ))
    layer = lax.broadcasted_iota(jnp.int32, (W, NZ), 0) - 8 + 8 * chip
    inside = jnp.logical_and(layer >= 0, layer < 64)

    def next_layer(x, n=1):
        return pltpu.roll(x, (W - n) % W, 0)

    def shift(x, di, dk):
        if di:
            x = pltpu.roll(x, (-di) % W, 0)
        if dk:
            x = pltpu.roll(x, (-dk) % NZ, 1)
        return x

    def spread(q):
        qx = q - next_layer(q)
        qz = q - jnp.where(ids == NZ - 1, 0.0, up_z(q))
        return qx, qz

    def times_s(b):
        total = None
        for n, (di, dk) in enumerate(FORWARD):
            s = s_ref[n]
            if n == 0:
                total = s * b
            else:
                total = total + s * shift(b, di, dk) + shift(s * b, -di, -dk)
        return total

    g = jnp.where(inside, g_ref[8 : 8 + W], 0.0)
    gx, gz = spread(g)
    tx, tz = times_s(gx), times_s(gz)
    h = tx - pltpu.roll(tx, 1, 0) + tz - jnp.where(ids == 0, 0.0, down_z(tz))
    h = jnp.where(inside, h, 0.0)
    hx, hz = spread(h)
    energy = hx * times_s(hx) + hz * times_s(hz)

    def own(x):
        return lax.select(odd, pltpu.roll(x, W - 4, 0), x)

    for n, x in enumerate((gx, gz, hx, hz)):
        basis[8 * n : 8 * n + 8] = own(x)[6:14]
    basis[32:40] = own(g)[8:16]
    basis[40:48] = own(h)[8:16]
    rows = []
    for x in (g * g, g * h, h * h, energy):
        part = x[8:16]
        part = part[:, 0:128] + part[:, 128:256] + part[:, 256:384] + part[:, 384:512]
        rows.append(jnp.sum(part, axis=0, keepdims=True))
    packed = jnp.concatenate(rows + [jnp.zeros((4, 128), jnp.float32)], 0)
    dots[...] = jnp.broadcast_to(packed[None], dots.shape)


def forced_kernel(par_ref, f, od, ev, first, second, v, d, fz, out, u, t):
    par = par_ref[0]
    lo, hi = sides(par_ref[2] == 1, first, second)

    def scale(i, _):
        dm = d[i + 2, LO:HI]
        for c in range(2):
            u[c, i + 2, LO:HI] = dm * f[c, i]
        return 0

    lax.fori_loop(0, ROWS, scale, 0)
    for at, x in ((par * 6, od), (6 - par * 6, ev)):
        dm = d[pl.ds(at, 2), LO:HI]
        for c in range(2):
            u[c, pl.ds(at, 2), LO:HI] = dm * x[3 + 2 * c : 5 + 2 * c]
    for c in range(2):
        for n in range(4):
            u[c, 2 + n, LO - 2 : LO] = d[2 + n, LO - 2 : LO] * lo[7 * n + 3 + 2 * c : 7 * n + 5 + 2 * c]
            u[c, 2 + n, HI : HI + 2] = d[2 + n, HI : HI + 2] * hi[7 * n + 3 + 2 * c : 7 * n + 5 + 2 * c]
        for r, at in ((1, 30), (6, 34)):
            u[c, r, LO - 1 : LO] = d[r, LO - 1 : LO] * lo[at + c : at + c + 1]
            u[c, r, HI : HI + 1] = d[r, HI : HI + 1] * hi[at + c : at + c + 1]

    def first(r, _):
        vm = v[r + 1]
        fy = vm + pltpu.roll(vm, FRAME - 1, 0)
        fxp, fxm = vm + v[r + 2], vm + v[r]
        fzp, dm = fz[r], d[r]
        for c in range(2):
            x = u[c, r]
            y = fy * pltpu.roll(x, FRAME - 1, 0) + pltpu.roll(fy * x, 1, 0)
            y = y + fxp * u[c, r + 1] + fxm * u[c, r - 1]
            y = y + fzp * up_z(x) + down_z(fzp * x)
            t[c, r] = E1 * x + E2 * (dm * y)
        return 0

    lax.fori_loop(1, 7, first, 0)

    def store(c, i, y):
        out[c, i] = E0 * u[c, i + 2, LO:HI] + y

    for i in range(ROWS):
        couple(i, v, d, fz, t, lambda c, y: store(c, i, y))


def couple(i, v, d, fz, t, done):
    own_rows = slice(LO, HI)
    above = slice(LO + 1, HI + 1)
    under = slice(LO - 1, HI - 1)
    r = i + 2
    vm = v[r + 1, own_rows]
    fyp = vm + v[r + 1, above]
    fym = vm + v[r + 1, under]
    fxp, fxm = vm + v[r + 2, own_rows], vm + v[r, own_rows]
    fzp, dm = fz[r, own_rows], d[r, own_rows]
    for c in range(2):
        x = t[c, r, own_rows]
        y = fyp * t[c, r, above] + fym * t[c, r, under]
        y = y + fxp * t[c, r + 1, own_rows] + fxm * t[c, r - 1, own_rows]
        y = y + fzp * up_z(x) + down_z(fzp * x)
        done(c, dm * y)


def velocity_kernel(basis, dots, onehot, h0, ex, ez, v, d, fz, forced, vel_hbm, press, vel, t, b, bz, sems):
    sums = jnp.sum(jnp.sum(dots[...], axis=0), axis=1, keepdims=True)
    gg, gh, hh, hkh = sums[0:1], sums[1:2], sums[2:3], sums[3:4]
    alpha0 = gg / gh
    fresh = gg - 2.0 * alpha0 * gh + alpha0 * alpha0 * hh
    beta = fresh / gg
    grow = 1.0 + beta
    alpha1 = fresh / (grow * grow * gh - 2.0 * grow * alpha0 * hh + alpha0 * alpha0 * hkh)
    on_g = alpha0 + alpha1 * grow
    on_h = alpha1 * alpha0
    grad = on_g * basis[0:16] - on_h * basis[16:32]
    b[...] = grad
    bz[0:16] = up_z(grad)
    bz[16:32] = down_z(grad)
    p = on_g * basis[32:40] - on_h * basis[40:48]
    press[...] = jnp.dot(
        p, onehot[...], precision=lax.Precision.HIGHEST, preferred_element_type=jnp.float32
    )[0:4]

    def first(r, _):
        h, exi, exm, ezi = h0[r], ex[r], ex[r - 1], ez[r]
        ezm = down_z(ezi)
        for c in range(2):
            at = 8 * c + r
            y = h * b[pl.ds(at, 1)] + exi * b[pl.ds(at + 1, 1)] + exm * b[pl.ds(at - 1, 1)]
            t[c, r] = y + ezi * bz[pl.ds(at, 1)] + ezm * bz[pl.ds(16 + at, 1)]
        return 0

    lax.fori_loop(1, 7, first, 0)

    def store(c, i, y):
        own = E0 * (d[i + 2, LO:HI] * b[pl.ds(8 * c + i + 2, 1)])
        vel[c, i] = forced[c, i] - (own + y)

    saves = []
    for i in range(ROWS):
        couple(i, v, d, fz, t, lambda c, y: store(c, i, y))
        saves.append(pltpu.make_async_copy(vel.at[:, i], vel_hbm.at[:, i], sems.at[i]))
        saves[-1].start()
    for copy in saves:
        copy.wait()


VMEM = pl.BlockSpec(memory_space=pltpu.VMEM)
SMEM = pl.BlockSpec(memory_space=pltpu.SMEM)
ANY = pl.BlockSpec(memory_space=pl.ANY)
HBM = pl.BlockSpec(memory_space=pltpu.HBM)


def call(kernel, out_shape, scratch, args, in_specs, out_specs=None, micros=1.0, sems=0, mib=16):
    return pl.pallas_call(
        kernel,
        out_shape=out_shape,
        in_specs=in_specs,
        out_specs=out_specs or jax.tree.map(lambda _: VMEM, out_shape),
        scratch_shapes=[pltpu.VMEM(s, jnp.float32) for s in scratch]
        + ([pltpu.SemaphoreType.DMA((sems,))] if sems else []),
        compiler_params=pltpu.CompilerParams(vmem_limit_bytes=mib * 1024 * 1024),
        cost_estimate=pl.CostEstimate(flops=0, transcendentals=0, bytes_accessed=int(micros * 3.6e6)),
    )(*args)


def in_vmem(x):
    return pltpu.with_memory_space_constraint(x, pltpu.VMEM)


def in_hbm(x):
    return pltpu.with_memory_space_constraint(x, pltpu.HBM)


def f32(*shape):
    return jax.ShapeDtypeStruct(shape, jnp.float32)


def pairs(n, first):
    up = [(i, i + 1) for i in range(first, n - 1, 2)]
    return up + [(b, a) for a, b in up]


def shards(forcing, viscosity, owner_slot):
    slabs, cross = lax.axis_size("slab"), lax.axis_size("cross")
    slab = lax.axis_index("slab")
    par = slab % 2
    where = jnp.stack([par, slab // 2, lax.axis_index("cross") % 2, slab // 2 % 2]).astype(jnp.int32)
    mates, others = pairs(slabs, 0), pairs(slabs, 1)
    chips = slabs // 2
    first_chips = [(2 * a + c, 2 * b + c) for a, b in pairs(chips, 0) for c in range(2)]
    second_chips = [(2 * a + c, 2 * b + c) for a, b in pairs(chips, 1) for c in range(2)]

    edges, own, f = call(
        edge_kernel,
        (
            pltpu.VMEM((ROWS, 14, NZ), jnp.float32),
            pltpu.VMEM(viscosity.shape, jnp.float32),
            pltpu.VMEM(forcing.shape, jnp.float32),
        ),
        [],
        (in_hbm(viscosity), in_hbm(forcing)),
        in_specs=[ANY, ANY],
        sems=2,
        mib=4,
    )
    od_e = lax.ppermute(edges, "slab", others)
    ev_e = lax.ppermute(edges, "slab", mates)
    layers = pltpu.VMEM((7, NY, NZ), jnp.float32)
    first, second, to_od, to_ev = call(
        corner_kernel,
        (f32(40, NZ), f32(40, NZ), layers, layers),
        [(40, NZ), (40, NZ)],
        (where, in_vmem(edges), in_vmem(od_e), in_vmem(ev_e), in_vmem(own), in_vmem(f)),
        in_specs=[SMEM] + [VMEM] * 5,
        sems=6,
        mib=4,
    )
    od = lax.ppermute(to_od, "slab", others)
    ev = lax.ppermute(to_ev, "slab", mates)
    first = lax.ppermute(first, "cross", pairs(cross, 0))
    second = lax.ppermute(second, "cross", pairs(cross, 1))

    kept = (f32(10, FRAME, NZ), f32(8, FRAME, NZ), f32(8, FRAME, NZ)) + (f32(7, FRAME, NZ),) * 3
    part, v, d, fz, h0, ex, ez = call(
        stencil_kernel,
        (f32(10, 4, NZ), *[pltpu.VMEM(x.shape, x.dtype) for x in kept]),
        [(7, FRAME, NZ), (5, 2, 8, 8, NZ), (7, ROWS, 8, NZ)],
        (where, in_vmem(own), in_vmem(od), in_vmem(ev), first, second, in_vmem(f)),
        in_specs=[SMEM] + [VMEM] * 6,
        micros=6,
        sems=4,
        mib=8,
    )

    width = owner_slot.shape[0] // cross
    column = lax.axis_index("cross") * width + jnp.arange(width, dtype=jnp.int32)
    onehot = (owner_slot[:, None] == column[None, :]).astype(jnp.float32)

    def among(x, step):
        return [lax.ppermute(x, "cross", [(i, i ^ (n * step)) for i in range(cross)]) for n in (1, 2, 3)]

    part, onehot = lax.optimization_barrier((part, onehot))
    got = among(part, 1)
    part = part + got[0] + got[1] + got[2]
    got = among(part, 4)
    forced = call(
        forced_kernel,
        pltpu.VMEM((2, ROWS, NY, NZ), jnp.float32),
        [(2, 8, FRAME, NZ)] * 2,
        (where, in_vmem(f), in_vmem(od), in_vmem(ev), first, second, in_vmem(v), in_vmem(d), in_vmem(fz)),
        in_specs=[SMEM] + [VMEM] * 8,
        micros=5,
        mib=8,
    )
    got, forced = lax.optimization_barrier((got, forced))
    part = part + got[0] + got[1] + got[2]

    mate = lax.ppermute(part, "slab", mates)
    both = jnp.stack([part, mate])
    window = (lax.ppermute(both, "slab", first_chips), lax.ppermute(both, "slab", second_chips))
    basis, dots = call(
        krylov_kernel,
        (f32(48, NZ), f32(chips, 8, 128)),
        [(7, 24, NZ), (40, NZ)],
        (where, part, mate, *window),
        in_specs=[SMEM] + [VMEM] * 4,
        mib=4,
    )
    groups = [[2 * z + c for z in range(chips)] for c in range(2)]
    dots = lax.all_to_all(dots, "slab", 0, 0, tiled=True, axis_index_groups=groups)

    return call(
        velocity_kernel,
        (pltpu.HBM((2, ROWS, NY, NZ), jnp.float32), f32(ROWS, width)),
        [(2, ROWS, NY, NZ), (2, 8, FRAME, NZ), (16, NZ), (32, NZ)],
        (basis, dots, onehot, *[in_vmem(x) for x in (h0, ex, ez, v, d, fz, forced)]),
        in_specs=[VMEM] * 10,
        out_specs=(HBM, VMEM),
        micros=4,
        sems=4,
        mib=8,
    )


def solution(mesh):
    in_specs = (P(None, "slab", "cross", None), P("slab", "cross", None), P())
    out_specs = (P(None, "slab", "cross", None), P("slab", "cross"))
    return jax.shard_map(shards, mesh=mesh, in_specs=in_specs, out_specs=out_specs, check_vma=False)
```

```python
import functools

import jax
import jax.numpy as jnp
from jax import lax
from jax.experimental import pallas as pl
from jax.experimental.pallas import tpu as pltpu
from jax.sharding import PartitionSpec as P

OUTER = 2
DEGREE = 3
cheb_theta = 1.025
cheb_delta = 0.975


def series():
    sigma = cheb_theta / cheb_delta
    rho0 = 1.0 / sigma
    rho1 = 1.0 / (2.0 * sigma - rho0)
    rho2 = 1.0 / (2.0 * sigma - rho1)
    g1, g2 = 2.0 * rho1 / cheb_delta, 2.0 * rho2 / cheb_delta
    p0, p1 = (1.0 + rho1 * rho0) / cheb_theta + g1, -g1 / cheb_theta
    q = rho2 * rho1
    c0 = (1.0 + q) * p0 - q / cheb_theta + g2
    c1 = (1.0 + q) * p1 - g2 * p0
    c2 = -g2 * p1
    return c0 + c1 + c2, -c1 - 2.0 * c2, c2


E0, E1, E2 = (2.0 * e for e in series())

NY, NZ = 64, 512
ROWS = 4
FRAME = 80
LO, HI = 8, 72
FORWARD = ((0, 0), (0, 1), (0, 2), (1, -1), (1, 0), (1, 1), (2, 0))
PAYLOAD = 40


def up_z(x):
    return pltpu.roll(x, NZ - 1, x.ndim - 1)


def down_z(x):
    return pltpu.roll(x, 1, x.ndim - 1)


def lane(shape):
    return lax.broadcasted_iota(jnp.int32, shape, len(shape) - 1)


def edge_kernel(own_hbm, f_hbm, out, own, f, sems):
    copies = [pltpu.make_async_copy(own_hbm, own, sems.at[0]), pltpu.make_async_copy(f_hbm, f, sems.at[1])]
    for copy in copies:
        copy.start()
    copies[0].wait()
    out[:, 0:3] = own[:, 0:3]
    out[:, 7:10] = own[:, NY - 3 : NY]
    copies[1].wait()
    for c in range(2):
        out[:, 3 + 2 * c : 5 + 2 * c] = f[c, :, 0:2]
        out[:, 10 + 2 * c : 12 + 2 * c] = f[c, :, NY - 2 : NY]


def pass_kernel(own, od_e, ev_e, out):
    pass


def pack(par, f, to_od, to_ev, sems):
    return [
        pltpu.make_async_copy(f.at[:, pl.ds(2 * last, 2)], out, sems.at[n])
        for n, (out, last) in enumerate(((to_od, par), (to_ev, 1 - par)))
    ]


def corner_kernel(par_ref, own, od, ev, first, second, low, high):
    odd = par_ref[0] == 1
    below = lax.select(odd, ev[2:4], od[2:4])
    above = lax.select(odd, od[0:2], ev[0:2])
    for out, near, forced, base in ((low, (0, 2), 0, 0), (high, (1, 3), 1, 7)):
        for n in range(4):
            out[7 * n : 7 * n + 7] = own[n, base : base + 7]
        for at, x, far, far_at in ((28, below[1], below[0], 36), (32, above[0], above[1], 37)):
            out[at : at + 2] = x[base + near[0] : base + near[1]]
            for c in range(2):
                row = base + 3 + 2 * c + forced
                out[at + 2 + c : at + 3 + c] = x[row : row + 1]
            row = base + 2 * forced
            out[far_at : far_at + 1] = far[row : row + 1]
        out[38:40] = jnp.zeros((2, NZ), jnp.float32)
    odd = par_ref[2] == 1
    first[...] = lax.select(odd, low[...], high[...])
    second[...] = lax.select(odd, high[...], low[...])


def sides(odd, first, second):
    return lax.select(odd, first[...], second[...]), lax.select(odd, second[...], first[...])


def fill_viscosity(par, v, own, od, ev, lo, hi, sems):
    copies = [pltpu.make_async_copy(own, v.at[3:7, LO:HI], sems.at[0])]
    for n, at, last, x in ((1, par * 7, 1 - par, od), (2, 7 - par * 7, par, ev)):
        copies.append(pltpu.make_async_copy(x.at[pl.ds(last, 3)], v.at[pl.ds(at, 3), LO:HI], sems.at[n]))
    for copy in copies:
        copy.start()
    for n in range(4):
        v[3 + n, LO - 3 : LO] = lo[7 * n : 7 * n + 3]
        v[3 + n, HI : HI + 3] = hi[7 * n : 7 * n + 3]
    for r, at in ((2, 28), (7, 32)):
        v[r, LO - 2 : LO] = lo[at : at + 2]
        v[r, HI : HI + 2] = hi[at : at + 2]
    for r, at in ((1, 36), (8, 37)):
        v[r, LO - 1 : LO] = lo[at : at + 1]
        v[r, HI : HI + 1] = hi[at : at + 1]
    for copy in copies:
        copy.wait()


def fill_inverse(v, d, fz):
    ids = lane((FRAME, NZ))

    def layer(r, _):
        mid = v[r + 1]
        nxt = jnp.where(ids == NZ - 1, 0.0, up_z(mid))
        prv = jnp.where(ids == 0, 0.0, down_z(mid))
        total = 6.0 * mid + v[r] + v[r + 2] + nxt + prv
        total = total + pltpu.roll(mid, 1, 0) + pltpu.roll(mid, FRAME - 1, 0)
        d[r] = jnp.where(mid > 0.0, 1.0 / total, 0.0)
        fz[r] = jnp.where(ids == NZ - 1, 0.0, mid + nxt)
        return 0

    lax.fori_loop(0, 8, layer, 0)


def stencil_kernel(par_ref, own, od, ev, first, second, f, out, to_od, to_ev, v, d, fz, h0, ex, ez, ezm, acc, s_acc, sems):
    par = par_ref[0]
    lo, hi = sides(par_ref[2] == 1, first, second)
    fill_viscosity(par, v, own, od, ev, lo, hi, sems)
    packs = pack(par, f, to_od, to_ev, sems.at[pl.ds(3, 2)])
    for copy in packs:
        copy.start()
    fill_inverse(v, d, fz)

    ex[0] = E2 * d[0] * (v[1] + v[2]) * d[1]

    def edges(r, _):
        dm, vm = d[r], v[r + 1]
        ex[r] = E2 * dm * (vm + v[r + 2]) * d[r + 1]
        dy = pltpu.roll(dm, FRAME - 1, 0)
        ey = E2 * dm * (vm + pltpu.roll(vm, FRAME - 1, 0)) * dy
        h0[r] = E1 * dm + ey + pltpu.roll(ey, 1, 0)
        e = E2 * dm * fz[r] * up_z(dm)
        ez[r] = e
        ezm[r] = down_z(e)
        return 0

    lax.fori_loop(1, 7, edges, 0)

    acc[...] = jnp.zeros_like(acc)
    own_rows = slice(LO, HI)
    above = slice(LO + 1, HI + 1)
    under = slice(LO - 1, HI - 1)

    def layer(i, _):
        r = i + 2
        vm = v[r + 1, own_rows]
        fyp = vm + v[r + 1, above]
        fym = vm + v[r + 1, under]
        fxp = vm + v[r + 2, own_rows]
        fxm = vm + v[r, own_rows]
        fzp = fz[r, own_rows]
        fzm = down_z(fzp)
        dm = d[r, own_rows]
        u0, u1 = dm * f[0, i], dm * f[1, i]

        def fold(x):
            return jnp.sum(x.reshape(8, 8, NZ), axis=0)

        def weigh(di, dk, s):
            for c, u in ((0, u0), (1, u1)):
                at = i + di + 2
                acc[dk + 2, c, at] = acc[dk + 2, c, at] + fold(u * s)
            if (di, dk) in FORWARD:
                s_acc[FORWARD.index((di, dk)), i] = fold(dm * s)

        exi, exm = ex[r, own_rows], ex[r - 1, own_rows]
        ezi, ezmi = ez[r, own_rows], ezm[r, own_rows]
        h = h0[r, own_rows]
        weigh(
            0,
            0,
            E0
            + fyp * h0[r, above]
            + fym * h0[r, under]
            + fxp * exi
            + fxm * exm
            + fzp * ezi
            + fzm * ezmi,
        )
        weigh(1, 0, fyp * ex[r, above] + fym * ex[r, under] + fxp * h0[r + 1, own_rows])
        weigh(-1, 0, fyp * ex[r - 1, above] + fym * ex[r - 1, under] + fxm * h0[r - 1, own_rows])
        weigh(0, 1, fyp * ez[r, above] + fym * ez[r, under] + fzp * up_z(h))
        weigh(0, -1, fyp * ezm[r, above] + fym * ezm[r, under] + fzm * down_z(h))
        weigh(2, 0, fxp * ex[r + 1, own_rows])
        weigh(-2, 0, fxm * ex[r - 2, own_rows])
        weigh(0, 2, fzp * up_z(ezi))
        weigh(0, -2, fzm * down_z(ezmi))
        weigh(1, 1, fxp * ez[r + 1, own_rows] + fzp * up_z(exi))
        weigh(1, -1, fxp * ezm[r + 1, own_rows] + fzm * down_z(exi))
        weigh(-1, 1, fxm * ez[r - 1, own_rows] + fzp * up_z(exm))
        weigh(-1, -1, fxm * ezm[r - 1, own_rows] + fzm * down_z(exm))
        return 0

    lax.fori_loop(0, ROWS, layer, 0)

    for n in range(7):
        out[n] = jnp.sum(s_acc[n], axis=1)

    def columns(c):
        total = jnp.sum(acc[2, c], axis=1)
        for dk in (-2, -1, 1, 2):
            total = total + pltpu.roll(jnp.sum(acc[dk + 2, c], axis=1), dk % NZ, 1)
        return jnp.concatenate([total, jnp.zeros((8, NZ), jnp.float32)], 0)

    cx, cz = columns(0), columns(1)
    zero = lane((16, NZ)) == 0
    e = cx - pltpu.roll(cx, 1, 0) + cz - jnp.where(zero, 0.0, down_z(cz))
    out[7:9] = e[0:8].reshape(2, 4, NZ)
    out[9, 0:1] = e[8:9]
    out[9, 1:4] = jnp.zeros((3, NZ), jnp.float32)
    for copy in packs:
        copy.wait()


def krylov_kernel(par_ref, mine, mate, first, second, basis, dots, s_ref, g_ref):
    par, chip = par_ref[0], par_ref[1]
    odd = par == 1

    def pair(a, b):
        return lax.select(odd, b, a), lax.select(odd, a, b)

    slabs = []
    below, above = sides(par_ref[3] == 1, first, second)
    for a, b in ((below[0], below[1]), (mine[...], mate[...]), (above[0], above[1])):
        slabs += pair(a, b)
    W = 24
    g_ref[...] = jnp.zeros_like(g_ref)
    for n, slab in enumerate(slabs):
        for o in range(7):
            s_ref[o, 4 * n : 4 * n + 4] = slab[o]
        flat = slab[7:10].reshape(12, NZ)[0:9]
        at = 8 + 4 * n - 2
        g_ref[at : at + 9] = g_ref[at : at + 9] + flat
    ids = lane((W, NZ))
    layer = lax.broadcasted_iota(jnp.int32, (W, NZ), 0) - 8 + 8 * chip
    inside = jnp.logical_and(layer >= 0, layer < 64)

    def next_layer(x, n=1):
        return pltpu.roll(x, (W - n) % W, 0)

    def shift(x, di, dk):
        if di:
            x = pltpu.roll(x, (-di) % W, 0)
        if dk:
            x = pltpu.roll(x, (-dk) % NZ, 1)
        return x

    def spread(q):
        qx = q - next_layer(q)
        qz = q - jnp.where(ids == NZ - 1, 0.0, up_z(q))
        return qx, qz

    def times_s(b):
        total = None
        for n, (di, dk) in enumerate(FORWARD):
            s = s_ref[n]
            if n == 0:
                total = s * b
            else:
                total = total + s * shift(b, di, dk) + shift(s * b, -di, -dk)
        return total

    g = jnp.where(inside, g_ref[8 : 8 + W], 0.0)
    gx, gz = spread(g)
    tx, tz = times_s(gx), times_s(gz)
    h = tx - pltpu.roll(tx, 1, 0) + tz - jnp.where(ids == 0, 0.0, down_z(tz))
    h = jnp.where(inside, h, 0.0)
    hx, hz = spread(h)
    energy = hx * times_s(hx) + hz * times_s(hz)

    def own(x):
        return lax.select(odd, pltpu.roll(x, W - 4, 0), x)

    for n, x in enumerate((gx, gz, hx, hz)):
        basis[8 * n : 8 * n + 8] = own(x)[6:14]
    basis[32:40] = own(g)[8:16]
    basis[40:48] = own(h)[8:16]
    rows = []
    for x in (g * g, g * h, h * h, energy):
        part = x[8:16]
        part = part[:, 0:128] + part[:, 128:256] + part[:, 256:384] + part[:, 384:512]
        rows.append(jnp.sum(part, axis=0, keepdims=True))
    packed = jnp.concatenate(rows + [jnp.zeros((4, 128), jnp.float32)], 0)
    dots[...] = jnp.broadcast_to(packed[None], dots.shape)


def forced_kernel(par_ref, f, od, ev, first, second, v, d, fz, out, u, t):
    par = par_ref[0]
    lo, hi = sides(par_ref[2] == 1, first, second)

    def scale(i, _):
        dm = d[i + 2, LO:HI]
        for c in range(2):
            u[c, i + 2, LO:HI] = dm * f[c, i]
        return 0

    lax.fori_loop(0, ROWS, scale, 0)
    for at, x in ((par * 6, od), (6 - par * 6, ev)):
        dm = d[pl.ds(at, 2), LO:HI]
        for c in range(2):
            u[c, pl.ds(at, 2), LO:HI] = dm * x[c]
    for c in range(2):
        for n in range(4):
            u[c, 2 + n, LO - 2 : LO] = d[2 + n, LO - 2 : LO] * lo[7 * n + 3 + 2 * c : 7 * n + 5 + 2 * c]
            u[c, 2 + n, HI : HI + 2] = d[2 + n, HI : HI + 2] * hi[7 * n + 3 + 2 * c : 7 * n + 5 + 2 * c]
        for r, at in ((1, 30), (6, 34)):
            u[c, r, LO - 1 : LO] = d[r, LO - 1 : LO] * lo[at + c : at + c + 1]
            u[c, r, HI : HI + 1] = d[r, HI : HI + 1] * hi[at + c : at + c + 1]

    def first(r, _):
        vm = v[r + 1]
        fy = vm + pltpu.roll(vm, FRAME - 1, 0)
        fxp, fxm = vm + v[r + 2], vm + v[r]
        fzp, dm = fz[r], d[r]
        for c in range(2):
            x = u[c, r]
            y = fy * pltpu.roll(x, FRAME - 1, 0) + pltpu.roll(fy * x, 1, 0)
            y = y + fxp * u[c, r + 1] + fxm * u[c, r - 1]
            y = y + fzp * up_z(x) + down_z(fzp * x)
            t[c, r] = E1 * x + E2 * (dm * y)
        return 0

    lax.fori_loop(1, 7, first, 0)

    def store(c, i, y):
        out[c, i] = E0 * u[c, i + 2, LO:HI] + y

    for i in range(ROWS):
        couple(i, v, d, fz, t, lambda c, y: store(c, i, y))


def couple(i, v, d, fz, t, done):
    own_rows = slice(LO, HI)
    above = slice(LO + 1, HI + 1)
    under = slice(LO - 1, HI - 1)
    r = i + 2
    vm = v[r + 1, own_rows]
    fyp = vm + v[r + 1, above]
    fym = vm + v[r + 1, under]
    fxp, fxm = vm + v[r + 2, own_rows], vm + v[r, own_rows]
    fzp, dm = fz[r, own_rows], d[r, own_rows]
    for c in range(2):
        x = t[c, r, own_rows]
        y = fyp * t[c, r, above] + fym * t[c, r, under]
        y = y + fxp * t[c, r + 1, own_rows] + fxm * t[c, r - 1, own_rows]
        y = y + fzp * up_z(x) + down_z(fzp * x)
        done(c, dm * y)


def velocity_kernel(basis, dots, onehot, h0, ex, ez, v, d, fz, forced, vel_hbm, press, vel, t, b, bz, sems):
    sums = jnp.sum(jnp.sum(dots[...], axis=0), axis=1, keepdims=True)
    gg, gh, hh, hkh = sums[0:1], sums[1:2], sums[2:3], sums[3:4]
    alpha0 = gg / gh
    fresh = gg - 2.0 * alpha0 * gh + alpha0 * alpha0 * hh
    beta = fresh / gg
    grow = 1.0 + beta
    alpha1 = fresh / (grow * grow * gh - 2.0 * grow * alpha0 * hh + alpha0 * alpha0 * hkh)
    on_g = alpha0 + alpha1 * grow
    on_h = alpha1 * alpha0
    grad = on_g * basis[0:16] - on_h * basis[16:32]
    b[...] = grad
    bz[0:16] = up_z(grad)
    bz[16:32] = down_z(grad)
    p = on_g * basis[32:40] - on_h * basis[40:48]
    press[...] = jnp.dot(
        p, onehot[...], precision=lax.Precision.HIGHEST, preferred_element_type=jnp.float32
    )[0:4]

    def first(r, _):
        h, exi, exm, ezi = h0[r], ex[r], ex[r - 1], ez[r]
        ezm = down_z(ezi)
        for c in range(2):
            at = 8 * c + r
            y = h * b[pl.ds(at, 1)] + exi * b[pl.ds(at + 1, 1)] + exm * b[pl.ds(at - 1, 1)]
            t[c, r] = y + ezi * bz[pl.ds(at, 1)] + ezm * bz[pl.ds(16 + at, 1)]
        return 0

    lax.fori_loop(1, 7, first, 0)

    def store(c, i, y):
        own = E0 * (d[i + 2, LO:HI] * b[pl.ds(8 * c + i + 2, 1)])
        vel[c, i] = forced[c, i] - (own + y)

    saves = []
    for i in range(ROWS):
        couple(i, v, d, fz, t, lambda c, y: store(c, i, y))
        saves.append(pltpu.make_async_copy(vel.at[:, i], vel_hbm.at[:, i], sems.at[i]))
        saves[-1].start()
    for copy in saves:
        copy.wait()


VMEM = pl.BlockSpec(memory_space=pltpu.VMEM)
SMEM = pl.BlockSpec(memory_space=pltpu.SMEM)
ANY = pl.BlockSpec(memory_space=pl.ANY)
HBM = pl.BlockSpec(memory_space=pltpu.HBM)


def call(kernel, out_shape, scratch, args, in_specs, out_specs=None, micros=1.0, sems=0, mib=16, aliases={}):
    return pl.pallas_call(
        kernel,
        out_shape=out_shape,
        in_specs=in_specs,
        out_specs=out_specs or jax.tree.map(lambda _: VMEM, out_shape),
        scratch_shapes=[pltpu.VMEM(s, jnp.float32) for s in scratch]
        + ([pltpu.SemaphoreType.DMA((sems,))] if sems else []),
        input_output_aliases=aliases,
        compiler_params=pltpu.CompilerParams(vmem_limit_bytes=mib * 1024 * 1024),
        cost_estimate=pl.CostEstimate(flops=0, transcendentals=0, bytes_accessed=int(micros * 3.6e6)),
    )(*args)


def in_vmem(x):
    return pltpu.with_memory_space_constraint(x, pltpu.VMEM)


def in_hbm(x):
    return pltpu.with_memory_space_constraint(x, pltpu.HBM)


def f32(*shape):
    return jax.ShapeDtypeStruct(shape, jnp.float32)


def pairs(n, first):
    up = [(i, i + 1) for i in range(first, n - 1, 2)]
    return up + [(b, a) for a, b in up]


def shards(forcing, viscosity, owner_slot):
    slabs, cross = lax.axis_size("slab"), lax.axis_size("cross")
    slab = lax.axis_index("slab")
    par = slab % 2
    where = jnp.stack([par, slab // 2, lax.axis_index("cross") % 2, slab // 2 % 2]).astype(jnp.int32)
    mates, others = pairs(slabs, 0), pairs(slabs, 1)
    chips = slabs // 2
    first_chips = [(2 * a + c, 2 * b + c) for a, b in pairs(chips, 0) for c in range(2)]
    second_chips = [(2 * a + c, 2 * b + c) for a, b in pairs(chips, 1) for c in range(2)]

    edges, own, f = call(
        edge_kernel,
        (
            pltpu.VMEM((ROWS, 14, NZ), jnp.float32),
            pltpu.VMEM(viscosity.shape, jnp.float32),
            pltpu.VMEM(forcing.shape, jnp.float32),
        ),
        [],
        (in_hbm(viscosity), in_hbm(forcing)),
        in_specs=[ANY, ANY],
        sems=2,
        mib=4,
    )
    od_e = lax.ppermute(edges, "slab", others)
    ev_e = lax.ppermute(edges, "slab", mates)
    late = call(
        pass_kernel,
        pltpu.VMEM(viscosity.shape, jnp.float32),
        [],
        (in_vmem(own), in_vmem(od_e), in_vmem(ev_e)),
        in_specs=[VMEM] * 3,
        mib=2,
        aliases={0: 0},
    )
    od = lax.ppermute(late, "slab", others)
    ev = lax.ppermute(late, "slab", mates)
    rows = pltpu.VMEM((40, NZ), jnp.float32)
    first, second = call(
        corner_kernel,
        (rows, rows),
        [(40, NZ), (40, NZ)],
        (where, in_vmem(edges), in_vmem(od_e), in_vmem(ev_e)),
        in_specs=[SMEM] + [VMEM] * 3,
        mib=4,
    )
    first = lax.ppermute(first, "cross", pairs(cross, 0))
    second = lax.ppermute(second, "cross", pairs(cross, 1))

    kept = (f32(10, FRAME, NZ), f32(8, FRAME, NZ), f32(8, FRAME, NZ)) + (f32(7, FRAME, NZ),) * 3
    layers = pltpu.VMEM((2, 2, NY, NZ), jnp.float32)
    part, to_od, to_ev, v, d, fz, h0, ex, ez = call(
        stencil_kernel,
        (f32(10, 4, NZ), layers, layers, *[pltpu.VMEM(x.shape, x.dtype) for x in kept]),
        [(7, FRAME, NZ), (5, 2, 8, 8, NZ), (7, ROWS, 8, NZ)],
        (where, in_vmem(late), in_vmem(od), in_vmem(ev), in_vmem(first), in_vmem(second), in_vmem(f)),
        in_specs=[SMEM] + [VMEM] * 6,
        micros=6,
        sems=5,
        mib=8,
    )

    width = owner_slot.shape[0] // cross
    column = lax.axis_index("cross") * width + jnp.arange(width, dtype=jnp.int32)
    onehot = (owner_slot[:, None] == column[None, :]).astype(jnp.float32)

    def among(x, step):
        return [lax.ppermute(x, "cross", [(i, i ^ (n * step)) for i in range(cross)]) for n in (1, 2, 3)]

    part, onehot = lax.optimization_barrier((part, onehot))
    od_f = lax.ppermute(to_od, "slab", others)
    ev_f = lax.ppermute(to_ev, "slab", mates)
    got = among(part, 1)
    part = part + got[0] + got[1] + got[2]
    got = among(part, 4)
    forced = call(
        forced_kernel,
        pltpu.VMEM((2, ROWS, NY, NZ), jnp.float32),
        [(2, 8, FRAME, NZ)] * 2,
        (where, in_vmem(f), in_vmem(od_f), in_vmem(ev_f), in_vmem(first), in_vmem(second), in_vmem(v), in_vmem(d), in_vmem(fz)),
        in_specs=[SMEM] + [VMEM] * 8,
        micros=5,
        mib=8,
    )
    got, forced = lax.optimization_barrier((got, forced))
    part = part + got[0] + got[1] + got[2]

    mate = lax.ppermute(part, "slab", mates)
    both = jnp.stack([part, mate])
    window = (lax.ppermute(both, "slab", first_chips), lax.ppermute(both, "slab", second_chips))
    basis, dots = call(
        krylov_kernel,
        (f32(48, NZ), f32(chips, 8, 128)),
        [(7, 24, NZ), (40, NZ)],
        (where, part, mate, *window),
        in_specs=[SMEM] + [VMEM] * 4,
        mib=4,
    )
    groups = [[2 * z + c for z in range(chips)] for c in range(2)]
    dots = lax.all_to_all(dots, "slab", 0, 0, tiled=True, axis_index_groups=groups)

    return call(
        velocity_kernel,
        (pltpu.HBM((2, ROWS, NY, NZ), jnp.float32), f32(ROWS, width)),
        [(2, ROWS, NY, NZ), (2, 8, FRAME, NZ), (16, NZ), (32, NZ)],
        (basis, dots, onehot, *[in_vmem(x) for x in (h0, ex, ez, v, d, fz, forced)]),
        in_specs=[VMEM] * 10,
        out_specs=(HBM, VMEM),
        micros=4,
        sems=4,
        mib=8,
    )


def solution(mesh):
    in_specs = (P(None, "slab", "cross", None), P("slab", "cross", None), P())
    out_specs = (P(None, "slab", "cross", None), P("slab", "cross"))
    return jax.shard_map(shards, mesh=mesh, in_specs=in_specs, out_specs=out_specs, check_vma=False)
```

```python
import functools

import jax
import jax.numpy as jnp
from jax import lax
from jax.experimental import pallas as pl
from jax.experimental.pallas import tpu as pltpu
from jax.sharding import PartitionSpec as P

OUTER = 2
DEGREE = 3
cheb_theta = 1.025
cheb_delta = 0.975


def series():
    sigma = cheb_theta / cheb_delta
    rho0 = 1.0 / sigma
    rho1 = 1.0 / (2.0 * sigma - rho0)
    rho2 = 1.0 / (2.0 * sigma - rho1)
    g1, g2 = 2.0 * rho1 / cheb_delta, 2.0 * rho2 / cheb_delta
    p0, p1 = (1.0 + rho1 * rho0) / cheb_theta + g1, -g1 / cheb_theta
    q = rho2 * rho1
    c0 = (1.0 + q) * p0 - q / cheb_theta + g2
    c1 = (1.0 + q) * p1 - g2 * p0
    c2 = -g2 * p1
    return c0 + c1 + c2, -c1 - 2.0 * c2, c2


E0, E1, E2 = (2.0 * e for e in series())

NY, NZ = 64, 512
ROWS = 4
FRAME = 80
LO, HI = 8, 72
FORWARD = ((0, 0), (0, 1), (0, 2), (1, -1), (1, 0), (1, 1), (2, 0))
PAYLOAD = 40


def up_z(x):
    return pltpu.roll(x, NZ - 1, x.ndim - 1)


def down_z(x):
    return pltpu.roll(x, 1, x.ndim - 1)


def lane(shape):
    return lax.broadcasted_iota(jnp.int32, shape, len(shape) - 1)


def edge_kernel(own_hbm, f_hbm, out, own, f, sems):
    copies = [pltpu.make_async_copy(own_hbm, own, sems.at[0]), pltpu.make_async_copy(f_hbm, f, sems.at[1])]
    for copy in copies:
        copy.start()
    copies[0].wait()
    out[:, 0:3] = own[:, 0:3]
    out[:, 7:10] = own[:, NY - 3 : NY]
    copies[1].wait()
    for c in range(2):
        out[:, 3 + 2 * c : 5 + 2 * c] = f[c, :, 0:2]
        out[:, 10 + 2 * c : 12 + 2 * c] = f[c, :, NY - 2 : NY]


def pass_kernel(own, od_e, ev_e, out):
    pass


def pack(par, f, to_od, to_ev, sems):
    return [
        pltpu.make_async_copy(f.at[:, pl.ds(2 * last, 2)], out, sems.at[n])
        for n, (out, last) in enumerate(((to_od, par), (to_ev, 1 - par)))
    ]


def corner_kernel(par_ref, own, od, ev, first, second, low, high):
    odd = par_ref[0] == 1
    below = lax.select(odd, ev[2:4], od[2:4])
    above = lax.select(odd, od[0:2], ev[0:2])
    for out, near, forced, base in ((low, (0, 2), 0, 0), (high, (1, 3), 1, 7)):
        for n in range(4):
            out[7 * n : 7 * n + 7] = own[n, base : base + 7]
        for at, x, far, far_at in ((28, below[1], below[0], 36), (32, above[0], above[1], 37)):
            out[at : at + 2] = x[base + near[0] : base + near[1]]
            for c in range(2):
                row = base + 3 + 2 * c + forced
                out[at + 2 + c : at + 3 + c] = x[row : row + 1]
            row = base + 2 * forced
            out[far_at : far_at + 1] = far[row : row + 1]
        out[38:40] = jnp.zeros((2, NZ), jnp.float32)
    odd = par_ref[2] == 1
    first[...] = lax.select(odd, low[...], high[...])
    second[...] = lax.select(odd, high[...], low[...])


def sides(odd, first, second):
    return lax.select(odd, first[...], second[...]), lax.select(odd, second[...], first[...])


def fill_viscosity(par, v, own, od, ev, lo, hi, sems):
    copies = [pltpu.make_async_copy(own, v.at[3:7, LO:HI], sems.at[0])]
    for n, at, last, x in ((1, par * 7, 1 - par, od), (2, 7 - par * 7, par, ev)):
        copies.append(pltpu.make_async_copy(x.at[pl.ds(last, 3)], v.at[pl.ds(at, 3), LO:HI], sems.at[n]))
    for copy in copies:
        copy.start()
    for n in range(4):
        v[3 + n, LO - 3 : LO] = lo[7 * n : 7 * n + 3]
        v[3 + n, HI : HI + 3] = hi[7 * n : 7 * n + 3]
    for r, at in ((2, 28), (7, 32)):
        v[r, LO - 2 : LO] = lo[at : at + 2]
        v[r, HI : HI + 2] = hi[at : at + 2]
    for r, at in ((1, 36), (8, 37)):
        v[r, LO - 1 : LO] = lo[at : at + 1]
        v[r, HI : HI + 1] = hi[at : at + 1]
    for copy in copies:
        copy.wait()


def fill_inverse(v, d, fz):
    ids = lane((FRAME, NZ))

    def layer(r, _):
        mid = v[r + 1]
        nxt = jnp.where(ids == NZ - 1, 0.0, up_z(mid))
        prv = jnp.where(ids == 0, 0.0, down_z(mid))
        total = 6.0 * mid + v[r] + v[r + 2] + nxt + prv
        total = total + pltpu.roll(mid, 1, 0) + pltpu.roll(mid, FRAME - 1, 0)
        d[r] = jnp.where(mid > 0.0, 1.0 / total, 0.0)
        fz[r] = jnp.where(ids == NZ - 1, 0.0, mid + nxt)
        return 0

    lax.fori_loop(0, 8, layer, 0)


def stencil_kernel(par_ref, own, od, ev, first, second, f, out, to_od, to_ev, v, d, fz, h0, ex, ez, ezm, acc, s_acc, sems):
    par = par_ref[0]
    lo, hi = sides(par_ref[2] == 1, first, second)
    fill_viscosity(par, v, own, od, ev, lo, hi, sems)
    packs = pack(par, f, to_od, to_ev, sems.at[pl.ds(3, 2)])
    for copy in packs:
        copy.start()
    fill_inverse(v, d, fz)

    ex[0] = E2 * d[0] * (v[1] + v[2]) * d[1]

    def edges(r, _):
        dm, vm = d[r], v[r + 1]
        ex[r] = E2 * dm * (vm + v[r + 2]) * d[r + 1]
        dy = pltpu.roll(dm, FRAME - 1, 0)
        ey = E2 * dm * (vm + pltpu.roll(vm, FRAME - 1, 0)) * dy
        h0[r] = E1 * dm + ey + pltpu.roll(ey, 1, 0)
        e = E2 * dm * fz[r] * up_z(dm)
        ez[r] = e
        ezm[r] = down_z(e)
        return 0

    lax.fori_loop(1, 7, edges, 0)

    acc[...] = jnp.zeros_like(acc)
    own_rows = slice(LO, HI)
    above = slice(LO + 1, HI + 1)
    under = slice(LO - 1, HI - 1)

    def layer(i, _):
        r = i + 2
        vm = v[r + 1, own_rows]
        fyp = vm + v[r + 1, above]
        fym = vm + v[r + 1, under]
        fxp = vm + v[r + 2, own_rows]
        fxm = vm + v[r, own_rows]
        fzp = fz[r, own_rows]
        fzm = down_z(fzp)
        dm = d[r, own_rows]
        u0, u1 = dm * f[0, i], dm * f[1, i]

        def fold(x):
            return jnp.sum(x.reshape(8, 8, NZ), axis=0)

        def weigh(di, dk, s):
            for c, u in ((0, u0), (1, u1)):
                at = i + di + 2
                acc[dk + 2, c, at] = acc[dk + 2, c, at] + fold(u * s)
            if (di, dk) in FORWARD:
                s_acc[FORWARD.index((di, dk)), i] = fold(dm * s)

        exi, exm = ex[r, own_rows], ex[r - 1, own_rows]
        ezi, ezmi = ez[r, own_rows], ezm[r, own_rows]
        h = h0[r, own_rows]
        weigh(
            0,
            0,
            E0
            + fyp * h0[r, above]
            + fym * h0[r, under]
            + fxp * exi
            + fxm * exm
            + fzp * ezi
            + fzm * ezmi,
        )
        weigh(1, 0, fyp * ex[r, above] + fym * ex[r, under] + fxp * h0[r + 1, own_rows])
        weigh(-1, 0, fyp * ex[r - 1, above] + fym * ex[r - 1, under] + fxm * h0[r - 1, own_rows])
        weigh(0, 1, fyp * ez[r, above] + fym * ez[r, under] + fzp * up_z(h))
        weigh(0, -1, fyp * ezm[r, above] + fym * ezm[r, under] + fzm * down_z(h))
        weigh(2, 0, fxp * ex[r + 1, own_rows])
        weigh(-2, 0, fxm * ex[r - 2, own_rows])
        weigh(0, 2, fzp * up_z(ezi))
        weigh(0, -2, fzm * down_z(ezmi))
        weigh(1, 1, fxp * ez[r + 1, own_rows] + fzp * up_z(exi))
        weigh(1, -1, fxp * ezm[r + 1, own_rows] + fzm * down_z(exi))
        weigh(-1, 1, fxm * ez[r - 1, own_rows] + fzp * up_z(exm))
        weigh(-1, -1, fxm * ezm[r - 1, own_rows] + fzm * down_z(exm))
        return 0

    lax.fori_loop(0, ROWS, layer, 0)

    for n in range(7):
        out[n] = jnp.sum(s_acc[n], axis=1)

    def columns(c):
        total = jnp.sum(acc[2, c], axis=1)
        for dk in (-2, -1, 1, 2):
            total = total + pltpu.roll(jnp.sum(acc[dk + 2, c], axis=1), dk % NZ, 1)
        return jnp.concatenate([total, jnp.zeros((8, NZ), jnp.float32)], 0)

    cx, cz = columns(0), columns(1)
    zero = lane((16, NZ)) == 0
    e = cx - pltpu.roll(cx, 1, 0) + cz - jnp.where(zero, 0.0, down_z(cz))
    out[7:9] = e[0:8].reshape(2, 4, NZ)
    out[9, 0:1] = e[8:9]
    out[9, 1:4] = jnp.zeros((3, NZ), jnp.float32)
    for copy in packs:
        copy.wait()


def krylov_kernel(par_ref, mine, mate, first, second, crossed, basis, dots, s_ref, g_ref):
    par, chip = par_ref[0], par_ref[1]
    odd = par == 1

    def pair(a, b):
        return lax.select(odd, b, a), lax.select(odd, a, b)

    slabs = []
    high = par_ref[3] == 1
    below, above = sides(high, first, second)
    below_mate, above_mate = sides(high, crossed.at[0], crossed.at[1])
    for a, b in ((below, below_mate), (mine[...], mate[...]), (above, above_mate)):
        slabs += pair(a, b)
    W = 24
    g_ref[...] = jnp.zeros_like(g_ref)
    for n, slab in enumerate(slabs):
        for o in range(7):
            s_ref[o, 4 * n : 4 * n + 4] = slab[o]
        flat = slab[7:10].reshape(12, NZ)[0:9]
        at = 8 + 4 * n - 2
        g_ref[at : at + 9] = g_ref[at : at + 9] + flat
    ids = lane((W, NZ))
    layer = lax.broadcasted_iota(jnp.int32, (W, NZ), 0) - 8 + 8 * chip
    inside = jnp.logical_and(layer >= 0, layer < 64)

    def next_layer(x, n=1):
        return pltpu.roll(x, (W - n) % W, 0)

    def shift(x, di, dk):
        if di:
            x = pltpu.roll(x, (-di) % W, 0)
        if dk:
            x = pltpu.roll(x, (-dk) % NZ, 1)
        return x

    def spread(q):
        qx = q - next_layer(q)
        qz = q - jnp.where(ids == NZ - 1, 0.0, up_z(q))
        return qx, qz

    def times_s(b):
        total = None
        for n, (di, dk) in enumerate(FORWARD):
            s = s_ref[n]
            if n == 0:
                total = s * b
            else:
                total = total + s * shift(b, di, dk) + shift(s * b, -di, -dk)
        return total

    g = jnp.where(inside, g_ref[8 : 8 + W], 0.0)
    gx, gz = spread(g)
    tx, tz = times_s(gx), times_s(gz)
    h = tx - pltpu.roll(tx, 1, 0) + tz - jnp.where(ids == 0, 0.0, down_z(tz))
    h = jnp.where(inside, h, 0.0)
    hx, hz = spread(h)
    energy = hx * times_s(hx) + hz * times_s(hz)

    def own(x):
        return lax.select(odd, pltpu.roll(x, W - 4, 0), x)

    for n, x in enumerate((gx, gz, hx, hz)):
        basis[8 * n : 8 * n + 8] = own(x)[6:14]
    basis[32:40] = own(g)[8:16]
    basis[40:48] = own(h)[8:16]
    rows = []
    for x in (g * g, g * h, h * h, energy):
        part = x[8:16]
        part = part[:, 0:128] + part[:, 128:256] + part[:, 256:384] + part[:, 384:512]
        rows.append(jnp.sum(part, axis=0, keepdims=True))
    packed = jnp.concatenate(rows + [jnp.zeros((4, 128), jnp.float32)], 0)
    dots[...] = jnp.broadcast_to(packed[None], dots.shape)


def forced_kernel(par_ref, f, od, ev, first, second, v, d, fz, out, u, t):
    par = par_ref[0]
    lo, hi = sides(par_ref[2] == 1, first, second)

    def scale(i, _):
        dm = d[i + 2, LO:HI]
        for c in range(2):
            u[c, i + 2, LO:HI] = dm * f[c, i]
        return 0

    lax.fori_loop(0, ROWS, scale, 0)
    for at, x in ((par * 6, od), (6 - par * 6, ev)):
        dm = d[pl.ds(at, 2), LO:HI]
        for c in range(2):
            u[c, pl.ds(at, 2), LO:HI] = dm * x[c]
    for c in range(2):
        for n in range(4):
            u[c, 2 + n, LO - 2 : LO] = d[2 + n, LO - 2 : LO] * lo[7 * n + 3 + 2 * c : 7 * n + 5 + 2 * c]
            u[c, 2 + n, HI : HI + 2] = d[2 + n, HI : HI + 2] * hi[7 * n + 3 + 2 * c : 7 * n + 5 + 2 * c]
        for r, at in ((1, 30), (6, 34)):
            u[c, r, LO - 1 : LO] = d[r, LO - 1 : LO] * lo[at + c : at + c + 1]
            u[c, r, HI : HI + 1] = d[r, HI : HI + 1] * hi[at + c : at + c + 1]

    def first(r, _):
        vm = v[r + 1]
        fy = vm + pltpu.roll(vm, FRAME - 1, 0)
        fxp, fxm = vm + v[r + 2], vm + v[r]
        fzp, dm = fz[r], d[r]
        for c in range(2):
            x = u[c, r]
            y = fy * pltpu.roll(x, FRAME - 1, 0) + pltpu.roll(fy * x, 1, 0)
            y = y + fxp * u[c, r + 1] + fxm * u[c, r - 1]
            y = y + fzp * up_z(x) + down_z(fzp * x)
            t[c, r] = E1 * x + E2 * (dm * y)
        return 0

    lax.fori_loop(1, 7, first, 0)

    def store(c, i, y):
        out[c, i] = E0 * u[c, i + 2, LO:HI] + y

    for i in range(ROWS):
        couple(i, v, d, fz, t, lambda c, y: store(c, i, y))


def couple(i, v, d, fz, t, done):
    own_rows = slice(LO, HI)
    above = slice(LO + 1, HI + 1)
    under = slice(LO - 1, HI - 1)
    r = i + 2
    vm = v[r + 1, own_rows]
    fyp = vm + v[r + 1, above]
    fym = vm + v[r + 1, under]
    fxp, fxm = vm + v[r + 2, own_rows], vm + v[r, own_rows]
    fzp, dm = fz[r, own_rows], d[r, own_rows]
    for c in range(2):
        x = t[c, r, own_rows]
        y = fyp * t[c, r, above] + fym * t[c, r, under]
        y = y + fxp * t[c, r + 1, own_rows] + fxm * t[c, r - 1, own_rows]
        y = y + fzp * up_z(x) + down_z(fzp * x)
        done(c, dm * y)


def velocity_kernel(basis, dots, onehot, h0, ex, ez, v, d, fz, forced, vel_hbm, press, vel, t, b, bz, sems):
    sums = jnp.sum(jnp.sum(dots[...], axis=0), axis=1, keepdims=True)
    gg, gh, hh, hkh = sums[0:1], sums[1:2], sums[2:3], sums[3:4]
    alpha0 = gg / gh
    fresh = gg - 2.0 * alpha0 * gh + alpha0 * alpha0 * hh
    beta = fresh / gg
    grow = 1.0 + beta
    alpha1 = fresh / (grow * grow * gh - 2.0 * grow * alpha0 * hh + alpha0 * alpha0 * hkh)
    on_g = alpha0 + alpha1 * grow
    on_h = alpha1 * alpha0
    grad = on_g * basis[0:16] - on_h * basis[16:32]
    b[...] = grad
    bz[0:16] = up_z(grad)
    bz[16:32] = down_z(grad)
    p = on_g * basis[32:40] - on_h * basis[40:48]
    press[...] = jnp.dot(
        p, onehot[...], precision=lax.Precision.HIGHEST, preferred_element_type=jnp.float32
    )[0:4]

    def first(r, _):
        h, exi, exm, ezi = h0[r], ex[r], ex[r - 1], ez[r]
        ezm = down_z(ezi)
        for c in range(2):
            at = 8 * c + r
            y = h * b[pl.ds(at, 1)] + exi * b[pl.ds(at + 1, 1)] + exm * b[pl.ds(at - 1, 1)]
            t[c, r] = y + ezi * bz[pl.ds(at, 1)] + ezm * bz[pl.ds(16 + at, 1)]
        return 0

    lax.fori_loop(1, 7, first, 0)

    def store(c, i, y):
        own = E0 * (d[i + 2, LO:HI] * b[pl.ds(8 * c + i + 2, 1)])
        vel[c, i] = forced[c, i] - (own + y)

    saves = []
    for i in range(ROWS):
        couple(i, v, d, fz, t, lambda c, y: store(c, i, y))
        saves.append(pltpu.make_async_copy(vel.at[:, i], vel_hbm.at[:, i], sems.at[i]))
        saves[-1].start()
    for copy in saves:
        copy.wait()


VMEM = pl.BlockSpec(memory_space=pltpu.VMEM)
SMEM = pl.BlockSpec(memory_space=pltpu.SMEM)
ANY = pl.BlockSpec(memory_space=pl.ANY)
HBM = pl.BlockSpec(memory_space=pltpu.HBM)


def call(kernel, out_shape, scratch, args, in_specs, out_specs=None, micros=1.0, sems=0, mib=16, aliases={}):
    return pl.pallas_call(
        kernel,
        out_shape=out_shape,
        in_specs=in_specs,
        out_specs=out_specs or jax.tree.map(lambda _: VMEM, out_shape),
        scratch_shapes=[pltpu.VMEM(s, jnp.float32) for s in scratch]
        + ([pltpu.SemaphoreType.DMA((sems,))] if sems else []),
        input_output_aliases=aliases,
        compiler_params=pltpu.CompilerParams(vmem_limit_bytes=mib * 1024 * 1024),
        cost_estimate=pl.CostEstimate(flops=0, transcendentals=0, bytes_accessed=int(micros * 3.6e6)),
    )(*args)


def in_vmem(x):
    return pltpu.with_memory_space_constraint(x, pltpu.VMEM)


def in_hbm(x):
    return pltpu.with_memory_space_constraint(x, pltpu.HBM)


def f32(*shape):
    return jax.ShapeDtypeStruct(shape, jnp.float32)


def pairs(n, first):
    up = [(i, i + 1) for i in range(first, n - 1, 2)]
    return up + [(b, a) for a, b in up]


def shards(forcing, viscosity, owner_slot):
    slabs, cross = lax.axis_size("slab"), lax.axis_size("cross")
    slab = lax.axis_index("slab")
    par = slab % 2
    where = jnp.stack([par, slab // 2, lax.axis_index("cross") % 2, slab // 2 % 2]).astype(jnp.int32)
    mates, others = pairs(slabs, 0), pairs(slabs, 1)
    chips = slabs // 2
    first_chips = [(2 * a + c, 2 * b + c) for a, b in pairs(chips, 0) for c in range(2)]
    second_chips = [(2 * a + c, 2 * b + c) for a, b in pairs(chips, 1) for c in range(2)]

    edges, own, f = call(
        edge_kernel,
        (
            pltpu.VMEM((ROWS, 14, NZ), jnp.float32),
            pltpu.VMEM(viscosity.shape, jnp.float32),
            pltpu.VMEM(forcing.shape, jnp.float32),
        ),
        [],
        (in_hbm(viscosity), in_hbm(forcing)),
        in_specs=[ANY, ANY],
        sems=2,
        mib=4,
    )
    od_e = lax.ppermute(edges, "slab", others)
    ev_e = lax.ppermute(edges, "slab", mates)
    late = call(
        pass_kernel,
        pltpu.VMEM(viscosity.shape, jnp.float32),
        [],
        (in_vmem(own), in_vmem(od_e), in_vmem(ev_e)),
        in_specs=[VMEM] * 3,
        mib=2,
        aliases={0: 0},
    )
    od = lax.ppermute(late, "slab", others)
    ev = lax.ppermute(late, "slab", mates)
    rows = pltpu.VMEM((40, NZ), jnp.float32)
    first, second = call(
        corner_kernel,
        (rows, rows),
        [(40, NZ), (40, NZ)],
        (where, in_vmem(edges), in_vmem(od_e), in_vmem(ev_e)),
        in_specs=[SMEM] + [VMEM] * 3,
        mib=4,
    )
    first = lax.ppermute(first, "cross", pairs(cross, 0))
    second = lax.ppermute(second, "cross", pairs(cross, 1))

    kept = (f32(10, FRAME, NZ), f32(8, FRAME, NZ), f32(8, FRAME, NZ)) + (f32(7, FRAME, NZ),) * 3
    layers = pltpu.VMEM((2, 2, NY, NZ), jnp.float32)
    part, to_od, to_ev, v, d, fz, h0, ex, ez = call(
        stencil_kernel,
        (f32(10, 4, NZ), layers, layers, *[pltpu.VMEM(x.shape, x.dtype) for x in kept]),
        [(7, FRAME, NZ), (5, 2, 8, 8, NZ), (7, ROWS, 8, NZ)],
        (where, in_vmem(late), in_vmem(od), in_vmem(ev), in_vmem(first), in_vmem(second), in_vmem(f)),
        in_specs=[SMEM] + [VMEM] * 6,
        micros=6,
        sems=5,
        mib=8,
    )

    width = owner_slot.shape[0] // cross
    column = lax.axis_index("cross") * width + jnp.arange(width, dtype=jnp.int32)
    onehot = (owner_slot[:, None] == column[None, :]).astype(jnp.float32)

    def among(x, step):
        return [lax.ppermute(x, "cross", [(i, i ^ (n * step)) for i in range(cross)]) for n in (1, 2, 3)]

    part, onehot = lax.optimization_barrier((part, onehot))
    od_f = lax.ppermute(to_od, "slab", others)
    ev_f = lax.ppermute(to_ev, "slab", mates)
    got = among(part, 1)
    part = part + got[0] + got[1] + got[2]
    got = among(part, 4)
    forced = call(
        forced_kernel,
        pltpu.VMEM((2, ROWS, NY, NZ), jnp.float32),
        [(2, 8, FRAME, NZ)] * 2,
        (where, in_vmem(f), in_vmem(od_f), in_vmem(ev_f), in_vmem(first), in_vmem(second), in_vmem(v), in_vmem(d), in_vmem(fz)),
        in_specs=[SMEM] + [VMEM] * 8,
        micros=5,
        mib=8,
    )
    got, forced = lax.optimization_barrier((got, forced))
    part = part + got[0] + got[1] + got[2]

    mate = lax.ppermute(part, "slab", mates)
    near = (lax.ppermute(part, "slab", first_chips), lax.ppermute(part, "slab", second_chips))
    crossed = lax.ppermute(jnp.stack(near), "slab", mates)
    basis, dots = call(
        krylov_kernel,
        (f32(48, NZ), f32(chips, 8, 128)),
        [(7, 24, NZ), (40, NZ)],
        (where, part, mate, *near, crossed),
        in_specs=[SMEM] + [VMEM] * 5,
        mib=4,
    )
    groups = [[2 * z + c for z in range(chips)] for c in range(2)]
    dots = lax.all_to_all(dots, "slab", 0, 0, tiled=True, axis_index_groups=groups)

    return call(
        velocity_kernel,
        (pltpu.HBM((2, ROWS, NY, NZ), jnp.float32), f32(ROWS, width)),
        [(2, ROWS, NY, NZ), (2, 8, FRAME, NZ), (16, NZ), (32, NZ)],
        (basis, dots, onehot, *[in_vmem(x) for x in (h0, ex, ez, v, d, fz, forced)]),
        in_specs=[VMEM] * 10,
        out_specs=(HBM, VMEM),
        micros=4,
        sems=4,
        mib=8,
    )


def solution(mesh):
    in_specs = (P(None, "slab", "cross", None), P("slab", "cross", None), P())
    out_specs = (P(None, "slab", "cross", None), P("slab", "cross"))
    return jax.shard_map(shards, mesh=mesh, in_specs=in_specs, out_specs=out_specs, check_vma=False)
```

```python
import functools

import jax
import jax.numpy as jnp
from jax import lax
from jax.experimental import pallas as pl
from jax.experimental.pallas import tpu as pltpu
from jax.sharding import PartitionSpec as P

OUTER = 2
DEGREE = 3
cheb_theta = 1.025
cheb_delta = 0.975


def series():
    sigma = cheb_theta / cheb_delta
    rho0 = 1.0 / sigma
    rho1 = 1.0 / (2.0 * sigma - rho0)
    rho2 = 1.0 / (2.0 * sigma - rho1)
    g1, g2 = 2.0 * rho1 / cheb_delta, 2.0 * rho2 / cheb_delta
    p0, p1 = (1.0 + rho1 * rho0) / cheb_theta + g1, -g1 / cheb_theta
    q = rho2 * rho1
    c0 = (1.0 + q) * p0 - q / cheb_theta + g2
    c1 = (1.0 + q) * p1 - g2 * p0
    c2 = -g2 * p1
    return c0 + c1 + c2, -c1 - 2.0 * c2, c2


E0, E1, E2 = (2.0 * e for e in series())

NY, NZ = 64, 512
ROWS = 4
FRAME = 80
LO, HI = 8, 72
FORWARD = ((0, 0), (0, 1), (0, 2), (1, -1), (1, 0), (1, 1), (2, 0))
PAYLOAD = 40


def up_z(x):
    return pltpu.roll(x, NZ - 1, x.ndim - 1)


def down_z(x):
    return pltpu.roll(x, 1, x.ndim - 1)


def lane(shape):
    return lax.broadcasted_iota(jnp.int32, shape, len(shape) - 1)


def edge_kernel(own_hbm, f_hbm, out, own, f, sems):
    copies = [pltpu.make_async_copy(own_hbm, own, sems.at[0]), pltpu.make_async_copy(f_hbm, f, sems.at[1])]
    for copy in copies:
        copy.start()
    copies[0].wait()
    out[:, 0:3] = own[:, 0:3]
    out[:, 7:10] = own[:, NY - 3 : NY]
    copies[1].wait()
    for c in range(2):
        out[:, 3 + 2 * c : 5 + 2 * c] = f[c, :, 0:2]
        out[:, 10 + 2 * c : 12 + 2 * c] = f[c, :, NY - 2 : NY]


def pass_kernel(own, od_e, ev_e, out):
    pass


def pack(par, f, to_od, to_ev, sems):
    return [
        pltpu.make_async_copy(f.at[:, pl.ds(2 * last, 2)], out, sems.at[n])
        for n, (out, last) in enumerate(((to_od, par), (to_ev, 1 - par)))
    ]


def corner_kernel(par_ref, own, od, ev, first, second, low, high):
    odd = par_ref[0] == 1
    below = lax.select(odd, ev[2:4], od[2:4])
    above = lax.select(odd, od[0:2], ev[0:2])
    for out, near, forced, base in ((low, (0, 2), 0, 0), (high, (1, 3), 1, 7)):
        for n in range(4):
            out[7 * n : 7 * n + 7] = own[n, base : base + 7]
        for at, x, far, far_at in ((28, below[1], below[0], 36), (32, above[0], above[1], 37)):
            out[at : at + 2] = x[base + near[0] : base + near[1]]
            for c in range(2):
                row = base + 3 + 2 * c + forced
                out[at + 2 + c : at + 3 + c] = x[row : row + 1]
            row = base + 2 * forced
            out[far_at : far_at + 1] = far[row : row + 1]
        out[38:40] = jnp.zeros((2, NZ), jnp.float32)
    odd = par_ref[2] == 1
    first[...] = lax.select(odd, low[...], high[...])
    second[...] = lax.select(odd, high[...], low[...])


def sides(odd, first, second):
    return lax.select(odd, first[...], second[...]), lax.select(odd, second[...], first[...])


def fill_viscosity(par, v, own, od, ev, lo, hi, sems):
    copies = [pltpu.make_async_copy(own, v.at[3:7, LO:HI], sems.at[0])]
    for n, at, last, x in ((1, par * 7, 1 - par, od), (2, 7 - par * 7, par, ev)):
        copies.append(pltpu.make_async_copy(x.at[pl.ds(last, 3)], v.at[pl.ds(at, 3), LO:HI], sems.at[n]))
    for copy in copies:
        copy.start()
    for n in range(4):
        v[3 + n, LO - 3 : LO] = lo[7 * n : 7 * n + 3]
        v[3 + n, HI : HI + 3] = hi[7 * n : 7 * n + 3]
    for r, at in ((2, 28), (7, 32)):
        v[r, LO - 2 : LO] = lo[at : at + 2]
        v[r, HI : HI + 2] = hi[at : at + 2]
    for r, at in ((1, 36), (8, 37)):
        v[r, LO - 1 : LO] = lo[at : at + 1]
        v[r, HI : HI + 1] = hi[at : at + 1]
    for copy in copies:
        copy.wait()


def fill_inverse(v, d, fz):
    ids = lane((FRAME, NZ))

    def layer(r, _):
        mid = v[r + 1]
        nxt = jnp.where(ids == NZ - 1, 0.0, up_z(mid))
        prv = jnp.where(ids == 0, 0.0, down_z(mid))
        total = 6.0 * mid + v[r] + v[r + 2] + nxt + prv
        total = total + pltpu.roll(mid, 1, 0) + pltpu.roll(mid, FRAME - 1, 0)
        d[r] = jnp.where(mid > 0.0, 1.0 / total, 0.0)
        fz[r] = jnp.where(ids == NZ - 1, 0.0, mid + nxt)
        return 0

    lax.fori_loop(0, 8, layer, 0)


def stencil_kernel(par_ref, own, od, ev, first, second, f, out, to_od, to_ev, v, d, fz, h0, ex, ez, ezm, acc, s_acc, sems):
    par = par_ref[0]
    lo, hi = sides(par_ref[2] == 1, first, second)
    fill_viscosity(par, v, own, od, ev, lo, hi, sems)
    packs = pack(par, f, to_od, to_ev, sems.at[pl.ds(3, 2)])
    for copy in packs:
        copy.start()
    fill_inverse(v, d, fz)

    ex[0] = E2 * d[0] * (v[1] + v[2]) * d[1]

    def edges(r, _):
        dm, vm = d[r], v[r + 1]
        ex[r] = E2 * dm * (vm + v[r + 2]) * d[r + 1]
        dy = pltpu.roll(dm, FRAME - 1, 0)
        ey = E2 * dm * (vm + pltpu.roll(vm, FRAME - 1, 0)) * dy
        h0[r] = E1 * dm + ey + pltpu.roll(ey, 1, 0)
        e = E2 * dm * fz[r] * up_z(dm)
        ez[r] = e
        ezm[r] = down_z(e)
        return 0

    lax.fori_loop(1, 7, edges, 0)

    acc[...] = jnp.zeros_like(acc)
    own_rows = slice(LO, HI)
    above = slice(LO + 1, HI + 1)
    under = slice(LO - 1, HI - 1)

    def layer(i, _):
        r = i + 2
        vm = v[r + 1, own_rows]
        fyp = vm + v[r + 1, above]
        fym = vm + v[r + 1, under]
        fxp = vm + v[r + 2, own_rows]
        fxm = vm + v[r, own_rows]
        fzp = fz[r, own_rows]
        fzm = down_z(fzp)
        dm = d[r, own_rows]
        u0, u1 = dm * f[0, i], dm * f[1, i]

        def fold(x):
            return jnp.sum(x.reshape(8, 8, NZ), axis=0)

        def weigh(di, dk, s):
            for c, u in ((0, u0), (1, u1)):
                at = i + di + 2
                acc[dk + 2, c, at] = acc[dk + 2, c, at] + fold(u * s)
            if (di, dk) in FORWARD:
                s_acc[FORWARD.index((di, dk)), i] = fold(dm * s)

        exi, exm = ex[r, own_rows], ex[r - 1, own_rows]
        ezi, ezmi = ez[r, own_rows], ezm[r, own_rows]
        h = h0[r, own_rows]
        weigh(
            0,
            0,
            E0
            + fyp * h0[r, above]
            + fym * h0[r, under]
            + fxp * exi
            + fxm * exm
            + fzp * ezi
            + fzm * ezmi,
        )
        weigh(1, 0, fyp * ex[r, above] + fym * ex[r, under] + fxp * h0[r + 1, own_rows])
        weigh(-1, 0, fyp * ex[r - 1, above] + fym * ex[r - 1, under] + fxm * h0[r - 1, own_rows])
        weigh(0, 1, fyp * ez[r, above] + fym * ez[r, under] + fzp * up_z(h))
        weigh(0, -1, fyp * ezm[r, above] + fym * ezm[r, under] + fzm * down_z(h))
        weigh(2, 0, fxp * ex[r + 1, own_rows])
        weigh(-2, 0, fxm * ex[r - 2, own_rows])
        weigh(0, 2, fzp * up_z(ezi))
        weigh(0, -2, fzm * down_z(ezmi))
        weigh(1, 1, fxp * ez[r + 1, own_rows] + fzp * up_z(exi))
        weigh(1, -1, fxp * ezm[r + 1, own_rows] + fzm * down_z(exi))
        weigh(-1, 1, fxm * ez[r - 1, own_rows] + fzp * up_z(exm))
        weigh(-1, -1, fxm * ezm[r - 1, own_rows] + fzm * down_z(exm))
        return 0

    lax.fori_loop(0, ROWS, layer, 0)

    for n in range(7):
        out[n] = jnp.sum(s_acc[n], axis=1)

    def columns(c):
        total = jnp.sum(acc[2, c], axis=1)
        for dk in (-2, -1, 1, 2):
            total = total + pltpu.roll(jnp.sum(acc[dk + 2, c], axis=1), dk % NZ, 1)
        return jnp.concatenate([total, jnp.zeros((8, NZ), jnp.float32)], 0)

    cx, cz = columns(0), columns(1)
    zero = lane((16, NZ)) == 0
    e = cx - pltpu.roll(cx, 1, 0) + cz - jnp.where(zero, 0.0, down_z(cz))
    out[7:9] = e[0:8].reshape(2, 4, NZ)
    out[9, 0:1] = e[8:9]
    out[9, 1:4] = jnp.zeros((3, NZ), jnp.float32)
    for copy in packs:
        copy.wait()


def krylov_kernel(par_ref, mine, first, second, crossed, basis, dots, s_ref, g_ref):
    par, chip = par_ref[0], par_ref[1]
    odd = par == 1

    def pair(a, b):
        return lax.select(odd, b, a), lax.select(odd, a, b)

    slabs = []
    high = par_ref[3] == 1
    below, above = sides(high, first, second)
    below_mate, above_mate = sides(high, crossed.at[0], crossed.at[1])
    for a, b in ((below, below_mate), (mine[...], crossed[2]), (above, above_mate)):
        slabs += pair(a, b)
    W = 24
    g_ref[...] = jnp.zeros_like(g_ref)
    for n, slab in enumerate(slabs):
        for o in range(7):
            s_ref[o, 4 * n : 4 * n + 4] = slab[o]
        flat = slab[7:10].reshape(12, NZ)[0:9]
        at = 8 + 4 * n - 2
        g_ref[at : at + 9] = g_ref[at : at + 9] + flat
    ids = lane((W, NZ))
    layer = lax.broadcasted_iota(jnp.int32, (W, NZ), 0) - 8 + 8 * chip
    inside = jnp.logical_and(layer >= 0, layer < 64)

    def next_layer(x, n=1):
        return pltpu.roll(x, (W - n) % W, 0)

    def shift(x, di, dk):
        if di:
            x = pltpu.roll(x, (-di) % W, 0)
        if dk:
            x = pltpu.roll(x, (-dk) % NZ, 1)
        return x

    def spread(q):
        qx = q - next_layer(q)
        qz = q - jnp.where(ids == NZ - 1, 0.0, up_z(q))
        return qx, qz

    def times_s(b):
        total = None
        for n, (di, dk) in enumerate(FORWARD):
            s = s_ref[n]
            if n == 0:
                total = s * b
            else:
                total = total + s * shift(b, di, dk) + shift(s * b, -di, -dk)
        return total

    g = jnp.where(inside, g_ref[8 : 8 + W], 0.0)
    gx, gz = spread(g)
    tx, tz = times_s(gx), times_s(gz)
    h = tx - pltpu.roll(tx, 1, 0) + tz - jnp.where(ids == 0, 0.0, down_z(tz))
    h = jnp.where(inside, h, 0.0)
    hx, hz = spread(h)
    energy = hx * times_s(hx) + hz * times_s(hz)

    def own(x):
        return lax.select(odd, pltpu.roll(x, W - 4, 0), x)

    for n, x in enumerate((gx, gz, hx, hz)):
        basis[8 * n : 8 * n + 8] = own(x)[6:14]
    basis[32:40] = own(g)[8:16]
    basis[40:48] = own(h)[8:16]
    rows = []
    for x in (g * g, g * h, h * h, energy):
        part = x[8:16]
        part = part[:, 0:128] + part[:, 128:256] + part[:, 256:384] + part[:, 384:512]
        rows.append(jnp.sum(part, axis=0, keepdims=True))
    packed = jnp.concatenate(rows + [jnp.zeros((4, 128), jnp.float32)], 0)
    dots[...] = jnp.broadcast_to(packed[None], dots.shape)


def forced_kernel(par_ref, f, od, ev, first, second, v, d, fz, out, u, t):
    par = par_ref[0]
    lo, hi = sides(par_ref[2] == 1, first, second)

    def scale(i, _):
        dm = d[i + 2, LO:HI]
        for c in range(2):
            u[c, i + 2, LO:HI] = dm * f[c, i]
        return 0

    lax.fori_loop(0, ROWS, scale, 0)
    for at, x in ((par * 6, od), (6 - par * 6, ev)):
        dm = d[pl.ds(at, 2), LO:HI]
        for c in range(2):
            u[c, pl.ds(at, 2), LO:HI] = dm * x[c]
    for c in range(2):
        for n in range(4):
            u[c, 2 + n, LO - 2 : LO] = d[2 + n, LO - 2 : LO] * lo[7 * n + 3 + 2 * c : 7 * n + 5 + 2 * c]
            u[c, 2 + n, HI : HI + 2] = d[2 + n, HI : HI + 2] * hi[7 * n + 3 + 2 * c : 7 * n + 5 + 2 * c]
        for r, at in ((1, 30), (6, 34)):
            u[c, r, LO - 1 : LO] = d[r, LO - 1 : LO] * lo[at + c : at + c + 1]
            u[c, r, HI : HI + 1] = d[r, HI : HI + 1] * hi[at + c : at + c + 1]

    def first(r, _):
        vm = v[r + 1]
        fy = vm + pltpu.roll(vm, FRAME - 1, 0)
        fxp, fxm = vm + v[r + 2], vm + v[r]
        fzp, dm = fz[r], d[r]
        for c in range(2):
            x = u[c, r]
            y = fy * pltpu.roll(x, FRAME - 1, 0) + pltpu.roll(fy * x, 1, 0)
            y = y + fxp * u[c, r + 1] + fxm * u[c, r - 1]
            y = y + fzp * up_z(x) + down_z(fzp * x)
            t[c, r] = E1 * x + E2 * (dm * y)
        return 0

    lax.fori_loop(1, 7, first, 0)

    def store(c, i, y):
        out[c, i] = E0 * u[c, i + 2, LO:HI] + y

    for i in range(ROWS):
        couple(i, v, d, fz, t, lambda c, y: store(c, i, y))


def couple(i, v, d, fz, t, done):
    own_rows = slice(LO, HI)
    above = slice(LO + 1, HI + 1)
    under = slice(LO - 1, HI - 1)
    r = i + 2
    vm = v[r + 1, own_rows]
    fyp = vm + v[r + 1, above]
    fym = vm + v[r + 1, under]
    fxp, fxm = vm + v[r + 2, own_rows], vm + v[r, own_rows]
    fzp, dm = fz[r, own_rows], d[r, own_rows]
    for c in range(2):
        x = t[c, r, own_rows]
        y = fyp * t[c, r, above] + fym * t[c, r, under]
        y = y + fxp * t[c, r + 1, own_rows] + fxm * t[c, r - 1, own_rows]
        y = y + fzp * up_z(x) + down_z(fzp * x)
        done(c, dm * y)


def velocity_kernel(basis, dots, onehot, h0, ex, ez, v, d, fz, forced, vel_hbm, press, vel, t, b, bz, sems):
    sums = jnp.sum(jnp.sum(dots[...], axis=0), axis=1, keepdims=True)
    gg, gh, hh, hkh = sums[0:1], sums[1:2], sums[2:3], sums[3:4]
    alpha0 = gg / gh
    fresh = gg - 2.0 * alpha0 * gh + alpha0 * alpha0 * hh
    beta = fresh / gg
    grow = 1.0 + beta
    alpha1 = fresh / (grow * grow * gh - 2.0 * grow * alpha0 * hh + alpha0 * alpha0 * hkh)
    on_g = alpha0 + alpha1 * grow
    on_h = alpha1 * alpha0
    grad = on_g * basis[0:16] - on_h * basis[16:32]
    b[...] = grad
    bz[0:16] = up_z(grad)
    bz[16:32] = down_z(grad)
    p = on_g * basis[32:40] - on_h * basis[40:48]
    press[...] = jnp.dot(
        p, onehot[...], precision=lax.Precision.HIGHEST, preferred_element_type=jnp.float32
    )[0:4]

    def first(r, _):
        h, exi, exm, ezi = h0[r], ex[r], ex[r - 1], ez[r]
        ezm = down_z(ezi)
        for c in range(2):
            at = 8 * c + r
            y = h * b[pl.ds(at, 1)] + exi * b[pl.ds(at + 1, 1)] + exm * b[pl.ds(at - 1, 1)]
            t[c, r] = y + ezi * bz[pl.ds(at, 1)] + ezm * bz[pl.ds(16 + at, 1)]
        return 0

    lax.fori_loop(1, 7, first, 0)

    def store(c, i, y):
        own = E0 * (d[i + 2, LO:HI] * b[pl.ds(8 * c + i + 2, 1)])
        vel[c, i] = forced[c, i] - (own + y)

    saves = []
    for i in range(ROWS):
        couple(i, v, d, fz, t, lambda c, y: store(c, i, y))
        saves.append(pltpu.make_async_copy(vel.at[:, i], vel_hbm.at[:, i], sems.at[i]))
        saves[-1].start()
    for copy in saves:
        copy.wait()


VMEM = pl.BlockSpec(memory_space=pltpu.VMEM)
SMEM = pl.BlockSpec(memory_space=pltpu.SMEM)
ANY = pl.BlockSpec(memory_space=pl.ANY)
HBM = pl.BlockSpec(memory_space=pltpu.HBM)


def call(kernel, out_shape, scratch, args, in_specs, out_specs=None, micros=1.0, sems=0, mib=16, aliases={}):
    return pl.pallas_call(
        kernel,
        out_shape=out_shape,
        in_specs=in_specs,
        out_specs=out_specs or jax.tree.map(lambda _: VMEM, out_shape),
        scratch_shapes=[pltpu.VMEM(s, jnp.float32) for s in scratch]
        + ([pltpu.SemaphoreType.DMA((sems,))] if sems else []),
        input_output_aliases=aliases,
        compiler_params=pltpu.CompilerParams(vmem_limit_bytes=mib * 1024 * 1024),
        cost_estimate=pl.CostEstimate(flops=0, transcendentals=0, bytes_accessed=int(micros * 3.6e6)),
    )(*args)


def in_vmem(x):
    return pltpu.with_memory_space_constraint(x, pltpu.VMEM)


def in_hbm(x):
    return pltpu.with_memory_space_constraint(x, pltpu.HBM)


def f32(*shape):
    return jax.ShapeDtypeStruct(shape, jnp.float32)


def pairs(n, first):
    up = [(i, i + 1) for i in range(first, n - 1, 2)]
    return up + [(b, a) for a, b in up]


def shards(forcing, viscosity, owner_slot):
    slabs, cross = lax.axis_size("slab"), lax.axis_size("cross")
    slab = lax.axis_index("slab")
    par = slab % 2
    where = jnp.stack([par, slab // 2, lax.axis_index("cross") % 2, slab // 2 % 2]).astype(jnp.int32)
    mates, others = pairs(slabs, 0), pairs(slabs, 1)
    chips = slabs // 2
    first_chips = [(2 * a + c, 2 * b + c) for a, b in pairs(chips, 0) for c in range(2)]
    second_chips = [(2 * a + c, 2 * b + c) for a, b in pairs(chips, 1) for c in range(2)]

    edges, own, f = call(
        edge_kernel,
        (
            pltpu.VMEM((ROWS, 14, NZ), jnp.float32),
            pltpu.VMEM(viscosity.shape, jnp.float32),
            pltpu.VMEM(forcing.shape, jnp.float32),
        ),
        [],
        (in_hbm(viscosity), in_hbm(forcing)),
        in_specs=[ANY, ANY],
        sems=2,
        mib=4,
    )
    od_e = lax.ppermute(edges, "slab", others)
    ev_e = lax.ppermute(edges, "slab", mates)
    late = call(
        pass_kernel,
        pltpu.VMEM(viscosity.shape, jnp.float32),
        [],
        (in_vmem(own), in_vmem(od_e), in_vmem(ev_e)),
        in_specs=[VMEM] * 3,
        mib=2,
        aliases={0: 0},
    )
    od = lax.ppermute(late, "slab", others)
    ev = lax.ppermute(late, "slab", mates)
    rows = pltpu.VMEM((40, NZ), jnp.float32)
    first, second = call(
        corner_kernel,
        (rows, rows),
        [(40, NZ), (40, NZ)],
        (where, in_vmem(edges), in_vmem(od_e), in_vmem(ev_e)),
        in_specs=[SMEM] + [VMEM] * 3,
        mib=4,
    )
    first = lax.ppermute(first, "cross", pairs(cross, 0))
    second = lax.ppermute(second, "cross", pairs(cross, 1))

    kept = (f32(10, FRAME, NZ), f32(8, FRAME, NZ), f32(8, FRAME, NZ)) + (f32(7, FRAME, NZ),) * 3
    layers = pltpu.VMEM((2, 2, NY, NZ), jnp.float32)
    part, to_od, to_ev, v, d, fz, h0, ex, ez = call(
        stencil_kernel,
        (f32(10, 4, NZ), layers, layers, *[pltpu.VMEM(x.shape, x.dtype) for x in kept]),
        [(7, FRAME, NZ), (5, 2, 8, 8, NZ), (7, ROWS, 8, NZ)],
        (where, in_vmem(late), in_vmem(od), in_vmem(ev), in_vmem(first), in_vmem(second), in_vmem(f)),
        in_specs=[SMEM] + [VMEM] * 6,
        micros=6,
        sems=5,
        mib=8,
    )

    width = owner_slot.shape[0] // cross
    column = lax.axis_index("cross") * width + jnp.arange(width, dtype=jnp.int32)
    onehot = (owner_slot[:, None] == column[None, :]).astype(jnp.float32)

    def among(x, step):
        return [lax.ppermute(x, "cross", [(i, i ^ (n * step)) for i in range(cross)]) for n in (1, 2, 3)]

    part, onehot = lax.optimization_barrier((part, onehot))
    od_f = lax.ppermute(to_od, "slab", others)
    ev_f = lax.ppermute(to_ev, "slab", mates)
    got = among(part, 1)
    part = part + got[0] + got[1] + got[2]
    got = among(part, 4)
    forced = call(
        forced_kernel,
        pltpu.VMEM((2, ROWS, NY, NZ), jnp.float32),
        [(2, 8, FRAME, NZ)] * 2,
        (where, in_vmem(f), in_vmem(od_f), in_vmem(ev_f), in_vmem(first), in_vmem(second), in_vmem(v), in_vmem(d), in_vmem(fz)),
        in_specs=[SMEM] + [VMEM] * 8,
        micros=5,
        mib=8,
    )
    got, forced = lax.optimization_barrier((got, forced))
    part = part + got[0] + got[1] + got[2]

    near = (lax.ppermute(part, "slab", first_chips), lax.ppermute(part, "slab", second_chips))
    crossed = lax.ppermute(jnp.stack([*near, part]), "slab", mates)
    basis, dots = call(
        krylov_kernel,
        (f32(48, NZ), f32(chips, 8, 128)),
        [(7, 24, NZ), (40, NZ)],
        (where, part, *near, crossed),
        in_specs=[SMEM] + [VMEM] * 4,
        mib=4,
    )
    groups = [[2 * z + c for z in range(chips)] for c in range(2)]
    dots = lax.all_to_all(dots, "slab", 0, 0, tiled=True, axis_index_groups=groups)

    return call(
        velocity_kernel,
        (pltpu.HBM((2, ROWS, NY, NZ), jnp.float32), f32(ROWS, width)),
        [(2, ROWS, NY, NZ), (2, 8, FRAME, NZ), (16, NZ), (32, NZ)],
        (basis, dots, onehot, *[in_vmem(x) for x in (h0, ex, ez, v, d, fz, forced)]),
        in_specs=[VMEM] * 10,
        out_specs=(HBM, VMEM),
        micros=4,
        sems=4,
        mib=8,
    )


def solution(mesh):
    in_specs = (P(None, "slab", "cross", None), P("slab", "cross", None), P())
    out_specs = (P(None, "slab", "cross", None), P("slab", "cross"))
    return jax.shard_map(shards, mesh=mesh, in_specs=in_specs, out_specs=out_specs, check_vma=False)
```

```python
import functools

import jax
import jax.numpy as jnp
from jax import lax
from jax.experimental import pallas as pl
from jax.experimental.pallas import tpu as pltpu
from jax.sharding import PartitionSpec as P

OUTER = 2
DEGREE = 3
cheb_theta = 1.025
cheb_delta = 0.975


def series():
    sigma = cheb_theta / cheb_delta
    rho0 = 1.0 / sigma
    rho1 = 1.0 / (2.0 * sigma - rho0)
    rho2 = 1.0 / (2.0 * sigma - rho1)
    g1, g2 = 2.0 * rho1 / cheb_delta, 2.0 * rho2 / cheb_delta
    p0, p1 = (1.0 + rho1 * rho0) / cheb_theta + g1, -g1 / cheb_theta
    q = rho2 * rho1
    c0 = (1.0 + q) * p0 - q / cheb_theta + g2
    c1 = (1.0 + q) * p1 - g2 * p0
    c2 = -g2 * p1
    return c0 + c1 + c2, -c1 - 2.0 * c2, c2


E0, E1, E2 = (2.0 * e for e in series())

NY, NZ = 64, 512
ROWS = 4
FRAME = 80
LO, HI = 8, 72
FORWARD = ((0, 0), (0, 1), (0, 2), (1, -1), (1, 0), (1, 1), (2, 0))
PAYLOAD = 40


def up_z(x):
    return pltpu.roll(x, NZ - 1, x.ndim - 1)


def down_z(x):
    return pltpu.roll(x, 1, x.ndim - 1)


def lane(shape):
    return lax.broadcasted_iota(jnp.int32, shape, len(shape) - 1)


def edge_kernel(own_hbm, f_hbm, out, bundle, f, sems):
    own = bundle.at[:, 0:NY]
    copies = [pltpu.make_async_copy(own_hbm, own, sems.at[0]), pltpu.make_async_copy(f_hbm, f, sems.at[1])]
    for copy in copies:
        copy.start()
    copies[0].wait()
    out[:, 0:3] = bundle[:, 0:3]
    out[:, 7:10] = bundle[:, NY - 3 : NY]
    copies[1].wait()
    for c in range(2):
        low, high = f[c, :, 0:2], f[c, :, NY - 2 : NY]
        out[:, 3 + 2 * c : 5 + 2 * c] = low
        out[:, 10 + 2 * c : 12 + 2 * c] = high
        bundle[:, NY + 2 * c : NY + 2 * c + 2] = low
        bundle[:, NY + 4 + 2 * c : NY + 6 + 2 * c] = high


def pass_kernel(own, od_e, ev, out):
    pass


def pack(par, f, to_od, to_ev, sems):
    return [
        pltpu.make_async_copy(f.at[:, pl.ds(2 * last, 2)], out, sems.at[n])
        for n, (out, last) in enumerate(((to_od, par), (to_ev, 1 - par)))
    ]


def corner_kernel(par_ref, own, od, ev, first, second, low, high, mate):
    odd = par_ref[0] == 1
    mate[:, 0:3] = ev[:, 0:3]
    mate[:, 3:7] = ev[:, NY : NY + 4]
    mate[:, 7:10] = ev[:, NY - 3 : NY]
    mate[:, 10:14] = ev[:, NY + 4 : NY + 8]
    below = lax.select(odd, mate[2:4], od[2:4])
    above = lax.select(odd, od[0:2], mate[0:2])
    for out, near, forced, base in ((low, (0, 2), 0, 0), (high, (1, 3), 1, 7)):
        for n in range(4):
            out[7 * n : 7 * n + 7] = own[n, base : base + 7]
        for at, x, far, far_at in ((28, below[1], below[0], 36), (32, above[0], above[1], 37)):
            out[at : at + 2] = x[base + near[0] : base + near[1]]
            for c in range(2):
                row = base + 3 + 2 * c + forced
                out[at + 2 + c : at + 3 + c] = x[row : row + 1]
            row = base + 2 * forced
            out[far_at : far_at + 1] = far[row : row + 1]
        out[38:40] = jnp.zeros((2, NZ), jnp.float32)
    odd = par_ref[2] == 1
    first[...] = lax.select(odd, low[...], high[...])
    second[...] = lax.select(odd, high[...], low[...])


def sides(odd, first, second):
    return lax.select(odd, first[...], second[...]), lax.select(odd, second[...], first[...])


def fill_viscosity(par, v, own, od, ev, lo, hi, sems):
    copies = [pltpu.make_async_copy(own.at[:, 0:NY], v.at[3:7, LO:HI], sems.at[0])]
    for n, at, last, x in ((1, par * 7, 1 - par, od), (2, 7 - par * 7, par, ev)):
        copies.append(pltpu.make_async_copy(x.at[pl.ds(last, 3), 0:NY], v.at[pl.ds(at, 3), LO:HI], sems.at[n]))
    for copy in copies:
        copy.start()
    for n in range(4):
        v[3 + n, LO - 3 : LO] = lo[7 * n : 7 * n + 3]
        v[3 + n, HI : HI + 3] = hi[7 * n : 7 * n + 3]
    for r, at in ((2, 28), (7, 32)):
        v[r, LO - 2 : LO] = lo[at : at + 2]
        v[r, HI : HI + 2] = hi[at : at + 2]
    for r, at in ((1, 36), (8, 37)):
        v[r, LO - 1 : LO] = lo[at : at + 1]
        v[r, HI : HI + 1] = hi[at : at + 1]
    for copy in copies:
        copy.wait()


def fill_inverse(v, d, fz):
    ids = lane((FRAME, NZ))

    def layer(r, _):
        mid = v[r + 1]
        nxt = jnp.where(ids == NZ - 1, 0.0, up_z(mid))
        prv = jnp.where(ids == 0, 0.0, down_z(mid))
        total = 6.0 * mid + v[r] + v[r + 2] + nxt + prv
        total = total + pltpu.roll(mid, 1, 0) + pltpu.roll(mid, FRAME - 1, 0)
        d[r] = jnp.where(mid > 0.0, 1.0 / total, 0.0)
        fz[r] = jnp.where(ids == NZ - 1, 0.0, mid + nxt)
        return 0

    lax.fori_loop(0, 8, layer, 0)


def stencil_kernel(par_ref, own, od, ev, first, second, f, out, to_od, to_ev, v, d, fz, h0, ex, ez, ezm, acc, s_acc, sems):
    par = par_ref[0]
    lo, hi = sides(par_ref[2] == 1, first, second)
    fill_viscosity(par, v, own, od, ev, lo, hi, sems)
    packs = pack(par, f, to_od, to_ev, sems.at[pl.ds(3, 2)])
    for copy in packs:
        copy.start()
    fill_inverse(v, d, fz)

    ex[0] = E2 * d[0] * (v[1] + v[2]) * d[1]

    def edges(r, _):
        dm, vm = d[r], v[r + 1]
        ex[r] = E2 * dm * (vm + v[r + 2]) * d[r + 1]
        dy = pltpu.roll(dm, FRAME - 1, 0)
        ey = E2 * dm * (vm + pltpu.roll(vm, FRAME - 1, 0)) * dy
        h0[r] = E1 * dm + ey + pltpu.roll(ey, 1, 0)
        e = E2 * dm * fz[r] * up_z(dm)
        ez[r] = e
        ezm[r] = down_z(e)
        return 0

    lax.fori_loop(1, 7, edges, 0)

    acc[...] = jnp.zeros_like(acc)
    own_rows = slice(LO, HI)
    above = slice(LO + 1, HI + 1)
    under = slice(LO - 1, HI - 1)

    def layer(i, _):
        r = i + 2
        vm = v[r + 1, own_rows]
        fyp = vm + v[r + 1, above]
        fym = vm + v[r + 1, under]
        fxp = vm + v[r + 2, own_rows]
        fxm = vm + v[r, own_rows]
        fzp = fz[r, own_rows]
        fzm = down_z(fzp)
        dm = d[r, own_rows]
        u0, u1 = dm * f[0, i], dm * f[1, i]

        def fold(x):
            return jnp.sum(x.reshape(8, 8, NZ), axis=0)

        def weigh(di, dk, s):
            for c, u in ((0, u0), (1, u1)):
                at = i + di + 2
                acc[dk + 2, c, at] = acc[dk + 2, c, at] + fold(u * s)
            if (di, dk) in FORWARD:
                s_acc[FORWARD.index((di, dk)), i] = fold(dm * s)

        exi, exm = ex[r, own_rows], ex[r - 1, own_rows]
        ezi, ezmi = ez[r, own_rows], ezm[r, own_rows]
        h = h0[r, own_rows]
        weigh(
            0,
            0,
            E0
            + fyp * h0[r, above]
            + fym * h0[r, under]
            + fxp * exi
            + fxm * exm
            + fzp * ezi
            + fzm * ezmi,
        )
        weigh(1, 0, fyp * ex[r, above] + fym * ex[r, under] + fxp * h0[r + 1, own_rows])
        weigh(-1, 0, fyp * ex[r - 1, above] + fym * ex[r - 1, under] + fxm * h0[r - 1, own_rows])
        weigh(0, 1, fyp * ez[r, above] + fym * ez[r, under] + fzp * up_z(h))
        weigh(0, -1, fyp * ezm[r, above] + fym * ezm[r, under] + fzm * down_z(h))
        weigh(2, 0, fxp * ex[r + 1, own_rows])
        weigh(-2, 0, fxm * ex[r - 2, own_rows])
        weigh(0, 2, fzp * up_z(ezi))
        weigh(0, -2, fzm * down_z(ezmi))
        weigh(1, 1, fxp * ez[r + 1, own_rows] + fzp * up_z(exi))
        weigh(1, -1, fxp * ezm[r + 1, own_rows] + fzm * down_z(exi))
        weigh(-1, 1, fxm * ez[r - 1, own_rows] + fzp * up_z(exm))
        weigh(-1, -1, fxm * ezm[r - 1, own_rows] + fzm * down_z(exm))
        return 0

    lax.fori_loop(0, ROWS, layer, 0)

    for n in range(7):
        out[n] = jnp.sum(s_acc[n], axis=1)

    def columns(c):
        total = jnp.sum(acc[2, c], axis=1)
        for dk in (-2, -1, 1, 2):
            total = total + pltpu.roll(jnp.sum(acc[dk + 2, c], axis=1), dk % NZ, 1)
        return jnp.concatenate([total, jnp.zeros((8, NZ), jnp.float32)], 0)

    cx, cz = columns(0), columns(1)
    zero = lane((16, NZ)) == 0
    e = cx - pltpu.roll(cx, 1, 0) + cz - jnp.where(zero, 0.0, down_z(cz))
    out[7:9] = e[0:8].reshape(2, 4, NZ)
    out[9, 0:1] = e[8:9]
    out[9, 1:4] = jnp.zeros((3, NZ), jnp.float32)
    for copy in packs:
        copy.wait()


def krylov_kernel(par_ref, mine, first, second, crossed, basis, dots, s_ref, g_ref):
    par, chip = par_ref[0], par_ref[1]
    odd = par == 1

    def pair(a, b):
        return lax.select(odd, b, a), lax.select(odd, a, b)

    slabs = []
    high = par_ref[3] == 1
    below, above = sides(high, first, second)
    below_mate, above_mate = sides(high, crossed.at[0], crossed.at[1])
    for a, b in ((below, below_mate), (mine[...], crossed[2]), (above, above_mate)):
        slabs += pair(a, b)
    W = 24
    g_ref[...] = jnp.zeros_like(g_ref)
    for n, slab in enumerate(slabs):
        for o in range(7):
            s_ref[o, 4 * n : 4 * n + 4] = slab[o]
        flat = slab[7:10].reshape(12, NZ)[0:9]
        at = 8 + 4 * n - 2
        g_ref[at : at + 9] = g_ref[at : at + 9] + flat
    ids = lane((W, NZ))
    layer = lax.broadcasted_iota(jnp.int32, (W, NZ), 0) - 8 + 8 * chip
    inside = jnp.logical_and(layer >= 0, layer < 64)

    def next_layer(x, n=1):
        return pltpu.roll(x, (W - n) % W, 0)

    def shift(x, di, dk):
        if di:
            x = pltpu.roll(x, (-di) % W, 0)
        if dk:
            x = pltpu.roll(x, (-dk) % NZ, 1)
        return x

    def spread(q):
        qx = q - next_layer(q)
        qz = q - jnp.where(ids == NZ - 1, 0.0, up_z(q))
        return qx, qz

    def times_s(b):
        total = None
        for n, (di, dk) in enumerate(FORWARD):
            s = s_ref[n]
            if n == 0:
                total = s * b
            else:
                total = total + s * shift(b, di, dk) + shift(s * b, -di, -dk)
        return total

    g = jnp.where(inside, g_ref[8 : 8 + W], 0.0)
    gx, gz = spread(g)
    tx, tz = times_s(gx), times_s(gz)
    h = tx - pltpu.roll(tx, 1, 0) + tz - jnp.where(ids == 0, 0.0, down_z(tz))
    h = jnp.where(inside, h, 0.0)
    hx, hz = spread(h)
    energy = hx * times_s(hx) + hz * times_s(hz)

    def own(x):
        return lax.select(odd, pltpu.roll(x, W - 4, 0), x)

    for n, x in enumerate((gx, gz, hx, hz)):
        basis[8 * n : 8 * n + 8] = own(x)[6:14]
    basis[32:40] = own(g)[8:16]
    basis[40:48] = own(h)[8:16]
    rows = []
    for x in (g * g, g * h, h * h, energy):
        part = x[8:16]
        part = part[:, 0:128] + part[:, 128:256] + part[:, 256:384] + part[:, 384:512]
        rows.append(jnp.sum(part, axis=0, keepdims=True))
    packed = jnp.concatenate(rows + [jnp.zeros((4, 128), jnp.float32)], 0)
    dots[...] = jnp.broadcast_to(packed[None], dots.shape)


def forced_kernel(par_ref, f, od, ev, first, second, v, d, fz, out, u, t):
    par = par_ref[0]
    lo, hi = sides(par_ref[2] == 1, first, second)

    def scale(i, _):
        dm = d[i + 2, LO:HI]
        for c in range(2):
            u[c, i + 2, LO:HI] = dm * f[c, i]
        return 0

    lax.fori_loop(0, ROWS, scale, 0)
    for at, x in ((par * 6, od), (6 - par * 6, ev)):
        dm = d[pl.ds(at, 2), LO:HI]
        for c in range(2):
            u[c, pl.ds(at, 2), LO:HI] = dm * x[c]
    for c in range(2):
        for n in range(4):
            u[c, 2 + n, LO - 2 : LO] = d[2 + n, LO - 2 : LO] * lo[7 * n + 3 + 2 * c : 7 * n + 5 + 2 * c]
            u[c, 2 + n, HI : HI + 2] = d[2 + n, HI : HI + 2] * hi[7 * n + 3 + 2 * c : 7 * n + 5 + 2 * c]
        for r, at in ((1, 30), (6, 34)):
            u[c, r, LO - 1 : LO] = d[r, LO - 1 : LO] * lo[at + c : at + c + 1]
            u[c, r, HI : HI + 1] = d[r, HI : HI + 1] * hi[at + c : at + c + 1]

    def first(r, _):
        vm = v[r + 1]
        fy = vm + pltpu.roll(vm, FRAME - 1, 0)
        fxp, fxm = vm + v[r + 2], vm + v[r]
        fzp, dm = fz[r], d[r]
        for c in range(2):
            x = u[c, r]
            y = fy * pltpu.roll(x, FRAME - 1, 0) + pltpu.roll(fy * x, 1, 0)
            y = y + fxp * u[c, r + 1] + fxm * u[c, r - 1]
            y = y + fzp * up_z(x) + down_z(fzp * x)
            t[c, r] = E1 * x + E2 * (dm * y)
        return 0

    lax.fori_loop(1, 7, first, 0)

    def store(c, i, y):
        out[c, i] = E0 * u[c, i + 2, LO:HI] + y

    for i in range(ROWS):
        couple(i, v, d, fz, t, lambda c, y: store(c, i, y))


def couple(i, v, d, fz, t, done):
    own_rows = slice(LO, HI)
    above = slice(LO + 1, HI + 1)
    under = slice(LO - 1, HI - 1)
    r = i + 2
    vm = v[r + 1, own_rows]
    fyp = vm + v[r + 1, above]
    fym = vm + v[r + 1, under]
    fxp, fxm = vm + v[r + 2, own_rows], vm + v[r, own_rows]
    fzp, dm = fz[r, own_rows], d[r, own_rows]
    for c in range(2):
        x = t[c, r, own_rows]
        y = fyp * t[c, r, above] + fym * t[c, r, under]
        y = y + fxp * t[c, r + 1, own_rows] + fxm * t[c, r - 1, own_rows]
        y = y + fzp * up_z(x) + down_z(fzp * x)
        done(c, dm * y)


def velocity_kernel(basis, dots, onehot, h0, ex, ez, v, d, fz, forced, vel_hbm, press, vel, t, b, bz, sems):
    sums = jnp.sum(jnp.sum(dots[...], axis=0), axis=1, keepdims=True)
    gg, gh, hh, hkh = sums[0:1], sums[1:2], sums[2:3], sums[3:4]
    alpha0 = gg / gh
    fresh = gg - 2.0 * alpha0 * gh + alpha0 * alpha0 * hh
    beta = fresh / gg
    grow = 1.0 + beta
    alpha1 = fresh / (grow * grow * gh - 2.0 * grow * alpha0 * hh + alpha0 * alpha0 * hkh)
    on_g = alpha0 + alpha1 * grow
    on_h = alpha1 * alpha0
    grad = on_g * basis[0:16] - on_h * basis[16:32]
    b[...] = grad
    bz[0:16] = up_z(grad)
    bz[16:32] = down_z(grad)
    p = on_g * basis[32:40] - on_h * basis[40:48]
    press[...] = jnp.dot(
        p, onehot[...], precision=lax.Precision.HIGHEST, preferred_element_type=jnp.float32
    )[0:4]

    def first(r, _):
        h, exi, exm, ezi = h0[r], ex[r], ex[r - 1], ez[r]
        ezm = down_z(ezi)
        for c in range(2):
            at = 8 * c + r
            y = h * b[pl.ds(at, 1)] + exi * b[pl.ds(at + 1, 1)] + exm * b[pl.ds(at - 1, 1)]
            t[c, r] = y + ezi * bz[pl.ds(at, 1)] + ezm * bz[pl.ds(16 + at, 1)]
        return 0

    lax.fori_loop(1, 7, first, 0)

    def store(c, i, y):
        own = E0 * (d[i + 2, LO:HI] * b[pl.ds(8 * c + i + 2, 1)])
        vel[c, i] = forced[c, i] - (own + y)

    saves = []
    for i in range(ROWS):
        couple(i, v, d, fz, t, lambda c, y: store(c, i, y))
        saves.append(pltpu.make_async_copy(vel.at[:, i], vel_hbm.at[:, i], sems.at[i]))
        saves[-1].start()
    for copy in saves:
        copy.wait()


VMEM = pl.BlockSpec(memory_space=pltpu.VMEM)
SMEM = pl.BlockSpec(memory_space=pltpu.SMEM)
ANY = pl.BlockSpec(memory_space=pl.ANY)
HBM = pl.BlockSpec(memory_space=pltpu.HBM)


def call(kernel, out_shape, scratch, args, in_specs, out_specs=None, micros=1.0, sems=0, mib=16, aliases={}):
    return pl.pallas_call(
        kernel,
        out_shape=out_shape,
        in_specs=in_specs,
        out_specs=out_specs or jax.tree.map(lambda _: VMEM, out_shape),
        scratch_shapes=[pltpu.VMEM(s, jnp.float32) for s in scratch]
        + ([pltpu.SemaphoreType.DMA((sems,))] if sems else []),
        input_output_aliases=aliases,
        compiler_params=pltpu.CompilerParams(vmem_limit_bytes=mib * 1024 * 1024),
        cost_estimate=pl.CostEstimate(flops=0, transcendentals=0, bytes_accessed=int(micros * 3.6e6)),
    )(*args)


def in_vmem(x):
    return pltpu.with_memory_space_constraint(x, pltpu.VMEM)


def in_hbm(x):
    return pltpu.with_memory_space_constraint(x, pltpu.HBM)


def f32(*shape):
    return jax.ShapeDtypeStruct(shape, jnp.float32)


def pairs(n, first):
    up = [(i, i + 1) for i in range(first, n - 1, 2)]
    return up + [(b, a) for a, b in up]


def shards(forcing, viscosity, owner_slot):
    slabs, cross = lax.axis_size("slab"), lax.axis_size("cross")
    slab = lax.axis_index("slab")
    par = slab % 2
    where = jnp.stack([par, slab // 2, lax.axis_index("cross") % 2, slab // 2 % 2]).astype(jnp.int32)
    mates, others = pairs(slabs, 0), pairs(slabs, 1)
    chips = slabs // 2
    first_chips = [(2 * a + c, 2 * b + c) for a, b in pairs(chips, 0) for c in range(2)]
    second_chips = [(2 * a + c, 2 * b + c) for a, b in pairs(chips, 1) for c in range(2)]

    edges, own, f = call(
        edge_kernel,
        (
            pltpu.VMEM((ROWS, 14, NZ), jnp.float32),
            pltpu.VMEM((ROWS, NY + 8, NZ), jnp.float32),
            pltpu.VMEM(forcing.shape, jnp.float32),
        ),
        [],
        (in_hbm(viscosity), in_hbm(forcing)),
        in_specs=[ANY, ANY],
        sems=2,
        mib=4,
    )
    od_e = lax.ppermute(edges, "slab", others)
    ev = lax.ppermute(own, "slab", mates)
    late = call(
        pass_kernel,
        pltpu.VMEM((ROWS, NY + 8, NZ), jnp.float32),
        [],
        (in_vmem(own), in_vmem(od_e), in_vmem(ev)),
        in_specs=[VMEM] * 3,
        mib=2,
        aliases={0: 0},
    )
    od = lax.ppermute(late, "slab", others)
    rows = pltpu.VMEM((40, NZ), jnp.float32)
    first, second = call(
        corner_kernel,
        (rows, rows),
        [(40, NZ), (40, NZ), (ROWS, 14, NZ)],
        (where, in_vmem(edges), in_vmem(od_e), in_vmem(ev)),
        in_specs=[SMEM] + [VMEM] * 3,
        mib=4,
    )
    first = lax.ppermute(first, "cross", pairs(cross, 0))
    second = lax.ppermute(second, "cross", pairs(cross, 1))

    kept = (f32(10, FRAME, NZ), f32(8, FRAME, NZ), f32(8, FRAME, NZ)) + (f32(7, FRAME, NZ),) * 3
    layers = pltpu.VMEM((2, 2, NY, NZ), jnp.float32)
    part, to_od, to_ev, v, d, fz, h0, ex, ez = call(
        stencil_kernel,
        (f32(10, 4, NZ), layers, layers, *[pltpu.VMEM(x.shape, x.dtype) for x in kept]),
        [(7, FRAME, NZ), (5, 2, 8, 8, NZ), (7, ROWS, 8, NZ)],
        (where, in_vmem(late), in_vmem(od), in_vmem(ev), in_vmem(first), in_vmem(second), in_vmem(f)),
        in_specs=[SMEM] + [VMEM] * 6,
        micros=6,
        sems=5,
        mib=8,
    )

    width = owner_slot.shape[0] // cross
    column = lax.axis_index("cross") * width + jnp.arange(width, dtype=jnp.int32)
    onehot = (owner_slot[:, None] == column[None, :]).astype(jnp.float32)

    def among(x, step):
        return [lax.ppermute(x, "cross", [(i, i ^ (n * step)) for i in range(cross)]) for n in (1, 2, 3)]

    part, onehot = lax.optimization_barrier((part, onehot))
    od_f = lax.ppermute(to_od, "slab", others)
    ev_f = lax.ppermute(to_ev, "slab", mates)
    got = among(part, 1)
    part = part + got[0] + got[1] + got[2]
    got = among(part, 4)
    forced = call(
        forced_kernel,
        pltpu.VMEM((2, ROWS, NY, NZ), jnp.float32),
        [(2, 8, FRAME, NZ)] * 2,
        (where, in_vmem(f), in_vmem(od_f), in_vmem(ev_f), in_vmem(first), in_vmem(second), in_vmem(v), in_vmem(d), in_vmem(fz)),
        in_specs=[SMEM] + [VMEM] * 8,
        micros=5,
        mib=8,
    )
    got, forced = lax.optimization_barrier((got, forced))
    part = part + got[0] + got[1] + got[2]

    near = (lax.ppermute(part, "slab", first_chips), lax.ppermute(part, "slab", second_chips))
    crossed = lax.ppermute(jnp.stack([*near, part]), "slab", mates)
    basis, dots = call(
        krylov_kernel,
        (f32(48, NZ), f32(chips, 8, 128)),
        [(7, 24, NZ), (40, NZ)],
        (where, part, *near, crossed),
        in_specs=[SMEM] + [VMEM] * 4,
        mib=4,
    )
    groups = [[2 * z + c for z in range(chips)] for c in range(2)]
    dots = lax.all_to_all(dots, "slab", 0, 0, tiled=True, axis_index_groups=groups)

    return call(
        velocity_kernel,
        (pltpu.HBM((2, ROWS, NY, NZ), jnp.float32), f32(ROWS, width)),
        [(2, ROWS, NY, NZ), (2, 8, FRAME, NZ), (16, NZ), (32, NZ)],
        (basis, dots, onehot, *[in_vmem(x) for x in (h0, ex, ez, v, d, fz, forced)]),
        in_specs=[VMEM] * 10,
        out_specs=(HBM, VMEM),
        micros=4,
        sems=4,
        mib=8,
    )


def solution(mesh):
    in_specs = (P(None, "slab", "cross", None), P("slab", "cross", None), P())
    out_specs = (P(None, "slab", "cross", None), P("slab", "cross"))
    return jax.shard_map(shards, mesh=mesh, in_specs=in_specs, out_specs=out_specs, check_vma=False)
```

```python
import functools

import jax
import jax.numpy as jnp
from jax import lax
from jax.experimental import pallas as pl
from jax.experimental.pallas import tpu as pltpu
from jax.sharding import PartitionSpec as P

OUTER = 2
DEGREE = 3
cheb_theta = 1.025
cheb_delta = 0.975


def series():
    sigma = cheb_theta / cheb_delta
    rho0 = 1.0 / sigma
    rho1 = 1.0 / (2.0 * sigma - rho0)
    rho2 = 1.0 / (2.0 * sigma - rho1)
    g1, g2 = 2.0 * rho1 / cheb_delta, 2.0 * rho2 / cheb_delta
    p0, p1 = (1.0 + rho1 * rho0) / cheb_theta + g1, -g1 / cheb_theta
    q = rho2 * rho1
    c0 = (1.0 + q) * p0 - q / cheb_theta + g2
    c1 = (1.0 + q) * p1 - g2 * p0
    c2 = -g2 * p1
    return c0 + c1 + c2, -c1 - 2.0 * c2, c2


E0, E1, E2 = (2.0 * e for e in series())

NY, NZ = 64, 512
ROWS = 4
FRAME = 80
LO, HI = 8, 72
FORWARD = ((0, 0), (0, 1), (0, 2), (1, -1), (1, 0), (1, 1), (2, 0))
PAYLOAD = 40


def up_z(x):
    return pltpu.roll(x, NZ - 1, x.ndim - 1)


def down_z(x):
    return pltpu.roll(x, 1, x.ndim - 1)


def lane(shape):
    return lax.broadcasted_iota(jnp.int32, shape, len(shape) - 1)


def edge_kernel(par_ref, own_hbm, f_hbm, out, bundle, three, f, sems):
    par = par_ref[0]
    own = bundle.at[:, 0:NY]
    extra = pltpu.make_async_copy(own_hbm.at[pl.ds(par, 3)], three.at[:, 0:NY], sems.at[2])
    extra.start()
    copies = [pltpu.make_async_copy(own_hbm, own, sems.at[0]), pltpu.make_async_copy(f_hbm, f, sems.at[1])]
    for copy in copies:
        copy.start()
    copies[0].wait()
    out[:, 0:3] = bundle[:, 0:3]
    out[:, 7:10] = bundle[:, NY - 3 : NY]
    copies[1].wait()
    for c in range(2):
        low, high = f[c, :, 0:2], f[c, :, NY - 2 : NY]
        out[:, 3 + 2 * c : 5 + 2 * c] = low
        out[:, 10 + 2 * c : 12 + 2 * c] = high
        bundle[:, NY + 2 * c : NY + 2 * c + 2] = low
        bundle[:, NY + 4 + 2 * c : NY + 6 + 2 * c] = high
        three[:, NY + 2 * c : NY + 2 * c + 2] = f[c, pl.ds(par, 3), 0:2]
        three[:, NY + 4 + 2 * c : NY + 6 + 2 * c] = f[c, pl.ds(par, 3), NY - 2 : NY]
    extra.wait()


def pack(par, f, to_od, to_ev, sems):
    return [
        pltpu.make_async_copy(f.at[:, pl.ds(2 * last, 2)], out, sems.at[n])
        for n, (out, last) in enumerate(((to_od, par), (to_ev, 1 - par)))
    ]


def corner_kernel(par_ref, own, od, ev, first, second, low, high, mate, other):
    odd = par_ref[0] == 1
    for rows, x in ((mate, ev), (other, od)):
        rows[:, 0:3] = x[:, 0:3]
        rows[:, 3:7] = x[:, NY : NY + 4]
        rows[:, 7:10] = x[:, NY - 3 : NY]
        rows[:, 10:14] = x[:, NY + 4 : NY + 8]
    below = lax.select(odd, mate[2:4], other[1:3])
    above = lax.select(odd, other[0:2], mate[0:2])
    for out, near, forced, base in ((low, (0, 2), 0, 0), (high, (1, 3), 1, 7)):
        for n in range(4):
            out[7 * n : 7 * n + 7] = own[n, base : base + 7]
        for at, x, far, far_at in ((28, below[1], below[0], 36), (32, above[0], above[1], 37)):
            out[at : at + 2] = x[base + near[0] : base + near[1]]
            for c in range(2):
                row = base + 3 + 2 * c + forced
                out[at + 2 + c : at + 3 + c] = x[row : row + 1]
            row = base + 2 * forced
            out[far_at : far_at + 1] = far[row : row + 1]
        out[38:40] = jnp.zeros((2, NZ), jnp.float32)
    odd = par_ref[2] == 1
    first[...] = lax.select(odd, low[...], high[...])
    second[...] = lax.select(odd, high[...], low[...])


def sides(odd, first, second):
    return lax.select(odd, first[...], second[...]), lax.select(odd, second[...], first[...])


def fill_viscosity(par, v, own, od, ev, lo, hi, sems):
    copies = [pltpu.make_async_copy(own.at[:, 0:NY], v.at[3:7, LO:HI], sems.at[0])]
    for n, at, last, x in ((1, par * 7, 0, od), (2, 7 - par * 7, par, ev)):
        copies.append(pltpu.make_async_copy(x.at[pl.ds(last, 3), 0:NY], v.at[pl.ds(at, 3), LO:HI], sems.at[n]))
    for copy in copies:
        copy.start()
    for n in range(4):
        v[3 + n, LO - 3 : LO] = lo[7 * n : 7 * n + 3]
        v[3 + n, HI : HI + 3] = hi[7 * n : 7 * n + 3]
    for r, at in ((2, 28), (7, 32)):
        v[r, LO - 2 : LO] = lo[at : at + 2]
        v[r, HI : HI + 2] = hi[at : at + 2]
    for r, at in ((1, 36), (8, 37)):
        v[r, LO - 1 : LO] = lo[at : at + 1]
        v[r, HI : HI + 1] = hi[at : at + 1]
    for copy in copies:
        copy.wait()


def fill_inverse(v, d, fz):
    ids = lane((FRAME, NZ))

    def layer(r, _):
        mid = v[r + 1]
        nxt = jnp.where(ids == NZ - 1, 0.0, up_z(mid))
        prv = jnp.where(ids == 0, 0.0, down_z(mid))
        total = 6.0 * mid + v[r] + v[r + 2] + nxt + prv
        total = total + pltpu.roll(mid, 1, 0) + pltpu.roll(mid, FRAME - 1, 0)
        d[r] = jnp.where(mid > 0.0, 1.0 / total, 0.0)
        fz[r] = jnp.where(ids == NZ - 1, 0.0, mid + nxt)
        return 0

    lax.fori_loop(0, 8, layer, 0)


def stencil_kernel(par_ref, own, od, ev, first, second, f, out, to_od, to_ev, v, d, fz, h0, ex, ez, ezm, acc, s_acc, sems):
    par = par_ref[0]
    lo, hi = sides(par_ref[2] == 1, first, second)
    fill_viscosity(par, v, own, od, ev, lo, hi, sems)
    packs = pack(par, f, to_od, to_ev, sems.at[pl.ds(3, 2)])
    for copy in packs:
        copy.start()
    fill_inverse(v, d, fz)

    ex[0] = E2 * d[0] * (v[1] + v[2]) * d[1]

    def edges(r, _):
        dm, vm = d[r], v[r + 1]
        ex[r] = E2 * dm * (vm + v[r + 2]) * d[r + 1]
        dy = pltpu.roll(dm, FRAME - 1, 0)
        ey = E2 * dm * (vm + pltpu.roll(vm, FRAME - 1, 0)) * dy
        h0[r] = E1 * dm + ey + pltpu.roll(ey, 1, 0)
        e = E2 * dm * fz[r] * up_z(dm)
        ez[r] = e
        ezm[r] = down_z(e)
        return 0

    lax.fori_loop(1, 7, edges, 0)

    acc[...] = jnp.zeros_like(acc)
    own_rows = slice(LO, HI)
    above = slice(LO + 1, HI + 1)
    under = slice(LO - 1, HI - 1)

    def layer(i, _):
        r = i + 2
        vm = v[r + 1, own_rows]
        fyp = vm + v[r + 1, above]
        fym = vm + v[r + 1, under]
        fxp = vm + v[r + 2, own_rows]
        fxm = vm + v[r, own_rows]
        fzp = fz[r, own_rows]
        fzm = down_z(fzp)
        dm = d[r, own_rows]
        u0, u1 = dm * f[0, i], dm * f[1, i]

        def fold(x):
            return jnp.sum(x.reshape(8, 8, NZ), axis=0)

        def weigh(di, dk, s):
            for c, u in ((0, u0), (1, u1)):
                at = i + di + 2
                acc[dk + 2, c, at] = acc[dk + 2, c, at] + fold(u * s)
            if (di, dk) in FORWARD:
                s_acc[FORWARD.index((di, dk)), i] = fold(dm * s)

        exi, exm = ex[r, own_rows], ex[r - 1, own_rows]
        ezi, ezmi = ez[r, own_rows], ezm[r, own_rows]
        h = h0[r, own_rows]
        weigh(
            0,
            0,
            E0
            + fyp * h0[r, above]
            + fym * h0[r, under]
            + fxp * exi
            + fxm * exm
            + fzp * ezi
            + fzm * ezmi,
        )
        weigh(1, 0, fyp * ex[r, above] + fym * ex[r, under] + fxp * h0[r + 1, own_rows])
        weigh(-1, 0, fyp * ex[r - 1, above] + fym * ex[r - 1, under] + fxm * h0[r - 1, own_rows])
        weigh(0, 1, fyp * ez[r, above] + fym * ez[r, under] + fzp * up_z(h))
        weigh(0, -1, fyp * ezm[r, above] + fym * ezm[r, under] + fzm * down_z(h))
        weigh(2, 0, fxp * ex[r + 1, own_rows])
        weigh(-2, 0, fxm * ex[r - 2, own_rows])
        weigh(0, 2, fzp * up_z(ezi))
        weigh(0, -2, fzm * down_z(ezmi))
        weigh(1, 1, fxp * ez[r + 1, own_rows] + fzp * up_z(exi))
        weigh(1, -1, fxp * ezm[r + 1, own_rows] + fzm * down_z(exi))
        weigh(-1, 1, fxm * ez[r - 1, own_rows] + fzp * up_z(exm))
        weigh(-1, -1, fxm * ezm[r - 1, own_rows] + fzm * down_z(exm))
        return 0

    lax.fori_loop(0, ROWS, layer, 0)

    for n in range(7):
        out[n] = jnp.sum(s_acc[n], axis=1)

    def columns(c):
        total = jnp.sum(acc[2, c], axis=1)
        for dk in (-2, -1, 1, 2):
            total = total + pltpu.roll(jnp.sum(acc[dk + 2, c], axis=1), dk % NZ, 1)
        return jnp.concatenate([total, jnp.zeros((8, NZ), jnp.float32)], 0)

    cx, cz = columns(0), columns(1)
    zero = lane((16, NZ)) == 0
    e = cx - pltpu.roll(cx, 1, 0) + cz - jnp.where(zero, 0.0, down_z(cz))
    out[7:9] = e[0:8].reshape(2, 4, NZ)
    out[9, 0:1] = e[8:9]
    out[9, 1:4] = jnp.zeros((3, NZ), jnp.float32)
    for copy in packs:
        copy.wait()


def krylov_kernel(par_ref, mine, first, second, crossed, basis, dots, s_ref, g_ref):
    par, chip = par_ref[0], par_ref[1]
    odd = par == 1

    def pair(a, b):
        return lax.select(odd, b, a), lax.select(odd, a, b)

    slabs = []
    high = par_ref[3] == 1
    below, above = sides(high, first, second)
    below_mate, above_mate = sides(high, crossed.at[0], crossed.at[1])
    for a, b in ((below, below_mate), (mine[...], crossed[2]), (above, above_mate)):
        slabs += pair(a, b)
    W = 24
    g_ref[...] = jnp.zeros_like(g_ref)
    for n, slab in enumerate(slabs):
        for o in range(7):
            s_ref[o, 4 * n : 4 * n + 4] = slab[o]
        flat = slab[7:10].reshape(12, NZ)[0:9]
        at = 8 + 4 * n - 2
        g_ref[at : at + 9] = g_ref[at : at + 9] + flat
    ids = lane((W, NZ))
    layer = lax.broadcasted_iota(jnp.int32, (W, NZ), 0) - 8 + 8 * chip
    inside = jnp.logical_and(layer >= 0, layer < 64)

    def next_layer(x, n=1):
        return pltpu.roll(x, (W - n) % W, 0)

    def shift(x, di, dk):
        if di:
            x = pltpu.roll(x, (-di) % W, 0)
        if dk:
            x = pltpu.roll(x, (-dk) % NZ, 1)
        return x

    def spread(q):
        qx = q - next_layer(q)
        qz = q - jnp.where(ids == NZ - 1, 0.0, up_z(q))
        return qx, qz

    def times_s(b):
        total = None
        for n, (di, dk) in enumerate(FORWARD):
            s = s_ref[n]
            if n == 0:
                total = s * b
            else:
                total = total + s * shift(b, di, dk) + shift(s * b, -di, -dk)
        return total

    g = jnp.where(inside, g_ref[8 : 8 + W], 0.0)
    gx, gz = spread(g)
    tx, tz = times_s(gx), times_s(gz)
    h = tx - pltpu.roll(tx, 1, 0) + tz - jnp.where(ids == 0, 0.0, down_z(tz))
    h = jnp.where(inside, h, 0.0)
    hx, hz = spread(h)
    energy = hx * times_s(hx) + hz * times_s(hz)

    def own(x):
        return lax.select(odd, pltpu.roll(x, W - 4, 0), x)

    for n, x in enumerate((gx, gz, hx, hz)):
        basis[8 * n : 8 * n + 8] = own(x)[6:14]
    basis[32:40] = own(g)[8:16]
    basis[40:48] = own(h)[8:16]
    rows = []
    for x in (g * g, g * h, h * h, energy):
        part = x[8:16]
        part = part[:, 0:128] + part[:, 128:256] + part[:, 256:384] + part[:, 384:512]
        rows.append(jnp.sum(part, axis=0, keepdims=True))
    packed = jnp.concatenate(rows + [jnp.zeros((4, 128), jnp.float32)], 0)
    dots[...] = jnp.broadcast_to(packed[None], dots.shape)


def forced_kernel(par_ref, f, od, ev, first, second, v, d, fz, out, u, t):
    par = par_ref[0]
    lo, hi = sides(par_ref[2] == 1, first, second)

    def scale(i, _):
        dm = d[i + 2, LO:HI]
        for c in range(2):
            u[c, i + 2, LO:HI] = dm * f[c, i]
        return 0

    lax.fori_loop(0, ROWS, scale, 0)
    for at, x in ((par * 6, od), (6 - par * 6, ev)):
        dm = d[pl.ds(at, 2), LO:HI]
        for c in range(2):
            u[c, pl.ds(at, 2), LO:HI] = dm * x[c]
    for c in range(2):
        for n in range(4):
            u[c, 2 + n, LO - 2 : LO] = d[2 + n, LO - 2 : LO] * lo[7 * n + 3 + 2 * c : 7 * n + 5 + 2 * c]
            u[c, 2 + n, HI : HI + 2] = d[2 + n, HI : HI + 2] * hi[7 * n + 3 + 2 * c : 7 * n + 5 + 2 * c]
        for r, at in ((1, 30), (6, 34)):
            u[c, r, LO - 1 : LO] = d[r, LO - 1 : LO] * lo[at + c : at + c + 1]
            u[c, r, HI : HI + 1] = d[r, HI : HI + 1] * hi[at + c : at + c + 1]

    def first(r, _):
        vm = v[r + 1]
        fy = vm + pltpu.roll(vm, FRAME - 1, 0)
        fxp, fxm = vm + v[r + 2], vm + v[r]
        fzp, dm = fz[r], d[r]
        for c in range(2):
            x = u[c, r]
            y = fy * pltpu.roll(x, FRAME - 1, 0) + pltpu.roll(fy * x, 1, 0)
            y = y + fxp * u[c, r + 1] + fxm * u[c, r - 1]
            y = y + fzp * up_z(x) + down_z(fzp * x)
            t[c, r] = E1 * x + E2 * (dm * y)
        return 0

    lax.fori_loop(1, 7, first, 0)

    def store(c, i, y):
        out[c, i] = E0 * u[c, i + 2, LO:HI] + y

    for i in range(ROWS):
        couple(i, v, d, fz, t, lambda c, y: store(c, i, y))


def couple(i, v, d, fz, t, done):
    own_rows = slice(LO, HI)
    above = slice(LO + 1, HI + 1)
    under = slice(LO - 1, HI - 1)
    r = i + 2
    vm = v[r + 1, own_rows]
    fyp = vm + v[r + 1, above]
    fym = vm + v[r + 1, under]
    fxp, fxm = vm + v[r + 2, own_rows], vm + v[r, own_rows]
    fzp, dm = fz[r, own_rows], d[r, own_rows]
    for c in range(2):
        x = t[c, r, own_rows]
        y = fyp * t[c, r, above] + fym * t[c, r, under]
        y = y + fxp * t[c, r + 1, own_rows] + fxm * t[c, r - 1, own_rows]
        y = y + fzp * up_z(x) + down_z(fzp * x)
        done(c, dm * y)


def velocity_kernel(basis, dots, onehot, h0, ex, ez, v, d, fz, forced, vel_hbm, press, vel, t, b, bz, sems):
    sums = jnp.sum(jnp.sum(dots[...], axis=0), axis=1, keepdims=True)
    gg, gh, hh, hkh = sums[0:1], sums[1:2], sums[2:3], sums[3:4]
    alpha0 = gg / gh
    fresh = gg - 2.0 * alpha0 * gh + alpha0 * alpha0 * hh
    beta = fresh / gg
    grow = 1.0 + beta
    alpha1 = fresh / (grow * grow * gh - 2.0 * grow * alpha0 * hh + alpha0 * alpha0 * hkh)
    on_g = alpha0 + alpha1 * grow
    on_h = alpha1 * alpha0
    grad = on_g * basis[0:16] - on_h * basis[16:32]
    b[...] = grad
    bz[0:16] = up_z(grad)
    bz[16:32] = down_z(grad)
    p = on_g * basis[32:40] - on_h * basis[40:48]
    press[...] = jnp.dot(
        p, onehot[...], precision=lax.Precision.HIGHEST, preferred_element_type=jnp.float32
    )[0:4]

    def first(r, _):
        h, exi, exm, ezi = h0[r], ex[r], ex[r - 1], ez[r]
        ezm = down_z(ezi)
        for c in range(2):
            at = 8 * c + r
            y = h * b[pl.ds(at, 1)] + exi * b[pl.ds(at + 1, 1)] + exm * b[pl.ds(at - 1, 1)]
            t[c, r] = y + ezi * bz[pl.ds(at, 1)] + ezm * bz[pl.ds(16 + at, 1)]
        return 0

    lax.fori_loop(1, 7, first, 0)

    def store(c, i, y):
        own = E0 * (d[i + 2, LO:HI] * b[pl.ds(8 * c + i + 2, 1)])
        vel[c, i] = forced[c, i] - (own + y)

    saves = []
    for i in range(ROWS):
        couple(i, v, d, fz, t, lambda c, y: store(c, i, y))
        saves.append(pltpu.make_async_copy(vel.at[:, i], vel_hbm.at[:, i], sems.at[i]))
        saves[-1].start()
    for copy in saves:
        copy.wait()


VMEM = pl.BlockSpec(memory_space=pltpu.VMEM)
SMEM = pl.BlockSpec(memory_space=pltpu.SMEM)
ANY = pl.BlockSpec(memory_space=pl.ANY)
HBM = pl.BlockSpec(memory_space=pltpu.HBM)


def call(kernel, out_shape, scratch, args, in_specs, out_specs=None, micros=1.0, sems=0, mib=16, aliases={}):
    return pl.pallas_call(
        kernel,
        out_shape=out_shape,
        in_specs=in_specs,
        out_specs=out_specs or jax.tree.map(lambda _: VMEM, out_shape),
        scratch_shapes=[pltpu.VMEM(s, jnp.float32) for s in scratch]
        + ([pltpu.SemaphoreType.DMA((sems,))] if sems else []),
        input_output_aliases=aliases,
        compiler_params=pltpu.CompilerParams(vmem_limit_bytes=mib * 1024 * 1024),
        cost_estimate=pl.CostEstimate(flops=0, transcendentals=0, bytes_accessed=int(micros * 3.6e6)),
    )(*args)


def in_vmem(x):
    return pltpu.with_memory_space_constraint(x, pltpu.VMEM)


def in_hbm(x):
    return pltpu.with_memory_space_constraint(x, pltpu.HBM)


def f32(*shape):
    return jax.ShapeDtypeStruct(shape, jnp.float32)


def pairs(n, first):
    up = [(i, i + 1) for i in range(first, n - 1, 2)]
    return up + [(b, a) for a, b in up]


def shards(forcing, viscosity, owner_slot):
    slabs, cross = lax.axis_size("slab"), lax.axis_size("cross")
    slab = lax.axis_index("slab")
    par = slab % 2
    where = jnp.stack([par, slab // 2, lax.axis_index("cross") % 2, slab // 2 % 2]).astype(jnp.int32)
    mates, others = pairs(slabs, 0), pairs(slabs, 1)
    chips = slabs // 2
    first_chips = [(2 * a + c, 2 * b + c) for a, b in pairs(chips, 0) for c in range(2)]
    second_chips = [(2 * a + c, 2 * b + c) for a, b in pairs(chips, 1) for c in range(2)]

    edges, own, three, f = call(
        edge_kernel,
        (
            pltpu.VMEM((ROWS, 14, NZ), jnp.float32),
            pltpu.VMEM((ROWS, NY + 8, NZ), jnp.float32),
            pltpu.VMEM((3, NY + 8, NZ), jnp.float32),
            pltpu.VMEM(forcing.shape, jnp.float32),
        ),
        [],
        (where, in_hbm(viscosity), in_hbm(forcing)),
        in_specs=[SMEM, ANY, ANY],
        sems=3,
        mib=4,
    )
    od = lax.ppermute(three, "slab", others)
    ev = lax.ppermute(own, "slab", mates)
    rows = pltpu.VMEM((40, NZ), jnp.float32)
    first, second = call(
        corner_kernel,
        (rows, rows),
        [(40, NZ), (40, NZ), (ROWS, 14, NZ), (3, 14, NZ)],
        (where, in_vmem(edges), in_vmem(od), in_vmem(ev)),
        in_specs=[SMEM] + [VMEM] * 3,
        mib=4,
    )
    first = lax.ppermute(first, "cross", pairs(cross, 0))
    second = lax.ppermute(second, "cross", pairs(cross, 1))

    kept = (f32(10, FRAME, NZ), f32(8, FRAME, NZ), f32(8, FRAME, NZ)) + (f32(7, FRAME, NZ),) * 3
    layers = pltpu.VMEM((2, 2, NY, NZ), jnp.float32)
    part, to_od, to_ev, v, d, fz, h0, ex, ez = call(
        stencil_kernel,
        (f32(10, 4, NZ), layers, layers, *[pltpu.VMEM(x.shape, x.dtype) for x in kept]),
        [(7, FRAME, NZ), (5, 2, 8, 8, NZ), (7, ROWS, 8, NZ)],
        (where, in_vmem(own), in_vmem(od), in_vmem(ev), in_vmem(first), in_vmem(second), in_vmem(f)),
        in_specs=[SMEM] + [VMEM] * 6,
        micros=6,
        sems=5,
        mib=8,
    )

    width = owner_slot.shape[0] // cross
    column = lax.axis_index("cross") * width + jnp.arange(width, dtype=jnp.int32)
    onehot = (owner_slot[:, None] == column[None, :]).astype(jnp.float32)

    def among(x, step):
        return [lax.ppermute(x, "cross", [(i, i ^ (n * step)) for i in range(cross)]) for n in (1, 2, 3)]

    part, onehot = lax.optimization_barrier((part, onehot))
    od_f = lax.ppermute(to_od, "slab", others)
    ev_f = lax.ppermute(to_ev, "slab", mates)
    got = among(part, 1)
    part = part + got[0] + got[1] + got[2]
    got = among(part, 4)
    forced = call(
        forced_kernel,
        pltpu.VMEM((2, ROWS, NY, NZ), jnp.float32),
        [(2, 8, FRAME, NZ)] * 2,
        (where, in_vmem(f), in_vmem(od_f), in_vmem(ev_f), in_vmem(first), in_vmem(second), in_vmem(v), in_vmem(d), in_vmem(fz)),
        in_specs=[SMEM] + [VMEM] * 8,
        micros=5,
        mib=8,
    )
    got, forced = lax.optimization_barrier((got, forced))
    part = part + got[0] + got[1] + got[2]

    near = (lax.ppermute(part, "slab", first_chips), lax.ppermute(part, "slab", second_chips))
    crossed = lax.ppermute(jnp.stack([*near, part]), "slab", mates)
    basis, dots = call(
        krylov_kernel,
        (f32(48, NZ), f32(chips, 8, 128)),
        [(7, 24, NZ), (40, NZ)],
        (where, part, *near, crossed),
        in_specs=[SMEM] + [VMEM] * 4,
        mib=4,
    )
    groups = [[2 * z + c for z in range(chips)] for c in range(2)]
    dots = lax.all_to_all(dots, "slab", 0, 0, tiled=True, axis_index_groups=groups)

    return call(
        velocity_kernel,
        (pltpu.HBM((2, ROWS, NY, NZ), jnp.float32), f32(ROWS, width)),
        [(2, ROWS, NY, NZ), (2, 8, FRAME, NZ), (16, NZ), (32, NZ)],
        (basis, dots, onehot, *[in_vmem(x) for x in (h0, ex, ez, v, d, fz, forced)]),
        in_specs=[VMEM] * 10,
        out_specs=(HBM, VMEM),
        micros=4,
        sems=4,
        mib=8,
    )


def solution(mesh):
    in_specs = (P(None, "slab", "cross", None), P("slab", "cross", None), P())
    out_specs = (P(None, "slab", "cross", None), P("slab", "cross"))
    return jax.shard_map(shards, mesh=mesh, in_specs=in_specs, out_specs=out_specs, check_vma=False)
```

```python
import functools

import jax
import jax.numpy as jnp
from jax import lax
from jax.experimental import pallas as pl
from jax.experimental.pallas import tpu as pltpu
from jax.sharding import PartitionSpec as P

OUTER = 2
DEGREE = 3
cheb_theta = 1.025
cheb_delta = 0.975


def series():
    sigma = cheb_theta / cheb_delta
    rho0 = 1.0 / sigma
    rho1 = 1.0 / (2.0 * sigma - rho0)
    rho2 = 1.0 / (2.0 * sigma - rho1)
    g1, g2 = 2.0 * rho1 / cheb_delta, 2.0 * rho2 / cheb_delta
    p0, p1 = (1.0 + rho1 * rho0) / cheb_theta + g1, -g1 / cheb_theta
    q = rho2 * rho1
    c0 = (1.0 + q) * p0 - q / cheb_theta + g2
    c1 = (1.0 + q) * p1 - g2 * p0
    c2 = -g2 * p1
    return c0 + c1 + c2, -c1 - 2.0 * c2, c2


E0, E1, E2 = (2.0 * e for e in series())

NY, NZ = 64, 512
ROWS = 4
FRAME = 80
LO, HI = 8, 72
FORWARD = ((0, 0), (0, 1), (0, 2), (1, -1), (1, 0), (1, 1), (2, 0))
PAYLOAD = 40


def up_z(x):
    return pltpu.roll(x, NZ - 1, x.ndim - 1)


def down_z(x):
    return pltpu.roll(x, 1, x.ndim - 1)


def lane(shape):
    return lax.broadcasted_iota(jnp.int32, shape, len(shape) - 1)


def edge_kernel(par_ref, own_hbm, f_hbm, out, bundle, three, f, sems):
    par = par_ref[0]
    own = bundle.at[:, 0:NY]
    extra = pltpu.make_async_copy(own_hbm.at[pl.ds(par, 3)], three.at[:, 0:NY], sems.at[2])
    extra.start()
    copies = [pltpu.make_async_copy(own_hbm, own, sems.at[0]), pltpu.make_async_copy(f_hbm, f, sems.at[1])]
    for copy in copies:
        copy.start()
    copies[0].wait()
    out[:, 0:3] = bundle[:, 0:3]
    out[:, 7:10] = bundle[:, NY - 3 : NY]
    copies[1].wait()
    for c in range(2):
        low, high = f[c, :, 0:2], f[c, :, NY - 2 : NY]
        out[:, 3 + 2 * c : 5 + 2 * c] = low
        out[:, 10 + 2 * c : 12 + 2 * c] = high
        bundle[:, NY + 2 * c : NY + 2 * c + 2] = low
        bundle[:, NY + 4 + 2 * c : NY + 6 + 2 * c] = high
        three[:, NY + 2 * c : NY + 2 * c + 2] = f[c, pl.ds(par, 3), 0:2]
        three[:, NY + 4 + 2 * c : NY + 6 + 2 * c] = f[c, pl.ds(par, 3), NY - 2 : NY]
    extra.wait()


def pack_kernel(par_ref, f, three, to_od, to_ev, sems):
    par = par_ref[0]
    copies = [
        pltpu.make_async_copy(f.at[:, pl.ds(2 * last, 2)], out, sems.at[n])
        for n, (out, last) in enumerate(((to_od, par), (to_ev, 1 - par)))
    ]
    for copy in copies:
        copy.start()
    for copy in copies:
        copy.wait()


def corner_kernel(par_ref, own, od, ev, first, second, low, high, mate, other):
    odd = par_ref[0] == 1
    for rows, x in ((mate, ev), (other, od)):
        rows[:, 0:3] = x[:, 0:3]
        rows[:, 3:7] = x[:, NY : NY + 4]
        rows[:, 7:10] = x[:, NY - 3 : NY]
        rows[:, 10:14] = x[:, NY + 4 : NY + 8]
    below = lax.select(odd, mate[2:4], other[1:3])
    above = lax.select(odd, other[0:2], mate[0:2])
    for out, near, forced, base in ((low, (0, 2), 0, 0), (high, (1, 3), 1, 7)):
        for n in range(4):
            out[7 * n : 7 * n + 7] = own[n, base : base + 7]
        for at, x, far, far_at in ((28, below[1], below[0], 36), (32, above[0], above[1], 37)):
            out[at : at + 2] = x[base + near[0] : base + near[1]]
            for c in range(2):
                row = base + 3 + 2 * c + forced
                out[at + 2 + c : at + 3 + c] = x[row : row + 1]
            row = base + 2 * forced
            out[far_at : far_at + 1] = far[row : row + 1]
        out[38:40] = jnp.zeros((2, NZ), jnp.float32)
    odd = par_ref[2] == 1
    first[...] = lax.select(odd, low[...], high[...])
    second[...] = lax.select(odd, high[...], low[...])


def sides(odd, first, second):
    return lax.select(odd, first[...], second[...]), lax.select(odd, second[...], first[...])


def fill_viscosity(par, v, own, od, ev, lo, hi, sems):
    copies = [pltpu.make_async_copy(own.at[:, 0:NY], v.at[3:7, LO:HI], sems.at[0])]
    for n, at, last, x in ((1, par * 7, 0, od), (2, 7 - par * 7, par, ev)):
        copies.append(pltpu.make_async_copy(x.at[pl.ds(last, 3), 0:NY], v.at[pl.ds(at, 3), LO:HI], sems.at[n]))
    for copy in copies:
        copy.start()
    for n in range(4):
        v[3 + n, LO - 3 : LO] = lo[7 * n : 7 * n + 3]
        v[3 + n, HI : HI + 3] = hi[7 * n : 7 * n + 3]
    for r, at in ((2, 28), (7, 32)):
        v[r, LO - 2 : LO] = lo[at : at + 2]
        v[r, HI : HI + 2] = hi[at : at + 2]
    for r, at in ((1, 36), (8, 37)):
        v[r, LO - 1 : LO] = lo[at : at + 1]
        v[r, HI : HI + 1] = hi[at : at + 1]
    for copy in copies:
        copy.wait()


def fill_inverse(v, d, fz):
    ids = lane((FRAME, NZ))

    def layer(r, _):
        mid = v[r + 1]
        nxt = jnp.where(ids == NZ - 1, 0.0, up_z(mid))
        prv = jnp.where(ids == 0, 0.0, down_z(mid))
        total = 6.0 * mid + v[r] + v[r + 2] + nxt + prv
        total = total + pltpu.roll(mid, 1, 0) + pltpu.roll(mid, FRAME - 1, 0)
        d[r] = jnp.where(mid > 0.0, 1.0 / total, 0.0)
        fz[r] = jnp.where(ids == NZ - 1, 0.0, mid + nxt)
        return 0

    lax.fori_loop(0, 8, layer, 0)


def stencil_kernel(par_ref, own, od, ev, first, second, f, out, v, d, fz, h0, ex, ez, ezm, acc, s_acc, sems):
    par = par_ref[0]
    lo, hi = sides(par_ref[2] == 1, first, second)
    fill_viscosity(par, v, own, od, ev, lo, hi, sems)
    fill_inverse(v, d, fz)

    ex[0] = E2 * d[0] * (v[1] + v[2]) * d[1]

    def edges(r, _):
        dm, vm = d[r], v[r + 1]
        ex[r] = E2 * dm * (vm + v[r + 2]) * d[r + 1]
        dy = pltpu.roll(dm, FRAME - 1, 0)
        ey = E2 * dm * (vm + pltpu.roll(vm, FRAME - 1, 0)) * dy
        h0[r] = E1 * dm + ey + pltpu.roll(ey, 1, 0)
        e = E2 * dm * fz[r] * up_z(dm)
        ez[r] = e
        ezm[r] = down_z(e)
        return 0

    lax.fori_loop(1, 7, edges, 0)

    acc[...] = jnp.zeros_like(acc)
    own_rows = slice(LO, HI)
    above = slice(LO + 1, HI + 1)
    under = slice(LO - 1, HI - 1)

    def layer(i, _):
        r = i + 2
        vm = v[r + 1, own_rows]
        fyp = vm + v[r + 1, above]
        fym = vm + v[r + 1, under]
        fxp = vm + v[r + 2, own_rows]
        fxm = vm + v[r, own_rows]
        fzp = fz[r, own_rows]
        fzm = down_z(fzp)
        dm = d[r, own_rows]
        u0, u1 = dm * f[0, i], dm * f[1, i]

        def fold(x):
            return jnp.sum(x.reshape(8, 8, NZ), axis=0)

        def weigh(di, dk, s):
            for c, u in ((0, u0), (1, u1)):
                at = i + di + 2
                acc[dk + 2, c, at] = acc[dk + 2, c, at] + fold(u * s)
            if (di, dk) in FORWARD:
                s_acc[FORWARD.index((di, dk)), i] = fold(dm * s)

        exi, exm = ex[r, own_rows], ex[r - 1, own_rows]
        ezi, ezmi = ez[r, own_rows], ezm[r, own_rows]
        h = h0[r, own_rows]
        weigh(
            0,
            0,
            E0
            + fyp * h0[r, above]
            + fym * h0[r, under]
            + fxp * exi
            + fxm * exm
            + fzp * ezi
            + fzm * ezmi,
        )
        weigh(1, 0, fyp * ex[r, above] + fym * ex[r, under] + fxp * h0[r + 1, own_rows])
        weigh(-1, 0, fyp * ex[r - 1, above] + fym * ex[r - 1, under] + fxm * h0[r - 1, own_rows])
        weigh(0, 1, fyp * ez[r, above] + fym * ez[r, under] + fzp * up_z(h))
        weigh(0, -1, fyp * ezm[r, above] + fym * ezm[r, under] + fzm * down_z(h))
        weigh(2, 0, fxp * ex[r + 1, own_rows])
        weigh(-2, 0, fxm * ex[r - 2, own_rows])
        weigh(0, 2, fzp * up_z(ezi))
        weigh(0, -2, fzm * down_z(ezmi))
        weigh(1, 1, fxp * ez[r + 1, own_rows] + fzp * up_z(exi))
        weigh(1, -1, fxp * ezm[r + 1, own_rows] + fzm * down_z(exi))
        weigh(-1, 1, fxm * ez[r - 1, own_rows] + fzp * up_z(exm))
        weigh(-1, -1, fxm * ezm[r - 1, own_rows] + fzm * down_z(exm))
        return 0

    lax.fori_loop(0, ROWS, layer, 0)

    for n in range(7):
        out[n] = jnp.sum(s_acc[n], axis=1)

    def columns(c):
        total = jnp.sum(acc[2, c], axis=1)
        for dk in (-2, -1, 1, 2):
            total = total + pltpu.roll(jnp.sum(acc[dk + 2, c], axis=1), dk % NZ, 1)
        return jnp.concatenate([total, jnp.zeros((8, NZ), jnp.float32)], 0)

    cx, cz = columns(0), columns(1)
    zero = lane((16, NZ)) == 0
    e = cx - pltpu.roll(cx, 1, 0) + cz - jnp.where(zero, 0.0, down_z(cz))
    out[7:9] = e[0:8].reshape(2, 4, NZ)
    out[9, 0:1] = e[8:9]
    out[9, 1:4] = jnp.zeros((3, NZ), jnp.float32)


def krylov_kernel(par_ref, mine, first, second, crossed, basis, dots, s_ref, g_ref):
    par, chip = par_ref[0], par_ref[1]
    odd = par == 1

    def pair(a, b):
        return lax.select(odd, b, a), lax.select(odd, a, b)

    slabs = []
    high = par_ref[3] == 1
    below, above = sides(high, first, second)
    below_mate, above_mate = sides(high, crossed.at[0], crossed.at[1])
    for a, b in ((below, below_mate), (mine[...], crossed[2]), (above, above_mate)):
        slabs += pair(a, b)
    W = 24
    g_ref[...] = jnp.zeros_like(g_ref)
    for n, slab in enumerate(slabs):
        for o in range(7):
            s_ref[o, 4 * n : 4 * n + 4] = slab[o]
        flat = slab[7:10].reshape(12, NZ)[0:9]
        at = 8 + 4 * n - 2
        g_ref[at : at + 9] = g_ref[at : at + 9] + flat
    ids = lane((W, NZ))
    layer = lax.broadcasted_iota(jnp.int32, (W, NZ), 0) - 8 + 8 * chip
    inside = jnp.logical_and(layer >= 0, layer < 64)

    def next_layer(x, n=1):
        return pltpu.roll(x, (W - n) % W, 0)

    def shift(x, di, dk):
        if di:
            x = pltpu.roll(x, (-di) % W, 0)
        if dk:
            x = pltpu.roll(x, (-dk) % NZ, 1)
        return x

    def spread(q):
        qx = q - next_layer(q)
        qz = q - jnp.where(ids == NZ - 1, 0.0, up_z(q))
        return qx, qz

    def times_s(b):
        total = None
        for n, (di, dk) in enumerate(FORWARD):
            s = s_ref[n]
            if n == 0:
                total = s * b
            else:
                total = total + s * shift(b, di, dk) + shift(s * b, -di, -dk)
        return total

    g = jnp.where(inside, g_ref[8 : 8 + W], 0.0)
    gx, gz = spread(g)
    tx, tz = times_s(gx), times_s(gz)
    h = tx - pltpu.roll(tx, 1, 0) + tz - jnp.where(ids == 0, 0.0, down_z(tz))
    h = jnp.where(inside, h, 0.0)
    hx, hz = spread(h)
    energy = hx * times_s(hx) + hz * times_s(hz)

    def own(x):
        return lax.select(odd, pltpu.roll(x, W - 4, 0), x)

    for n, x in enumerate((gx, gz, hx, hz)):
        basis[8 * n : 8 * n + 8] = own(x)[6:14]
    basis[32:40] = own(g)[8:16]
    basis[40:48] = own(h)[8:16]
    rows = []
    for x in (g * g, g * h, h * h, energy):
        part = x[8:16]
        part = part[:, 0:128] + part[:, 128:256] + part[:, 256:384] + part[:, 384:512]
        rows.append(jnp.sum(part, axis=0, keepdims=True))
    packed = jnp.concatenate(rows + [jnp.zeros((4, 128), jnp.float32)], 0)
    dots[...] = jnp.broadcast_to(packed[None], dots.shape)


def forced_kernel(par_ref, f, od, ev, first, second, v, d, fz, out, u, t):
    par = par_ref[0]
    lo, hi = sides(par_ref[2] == 1, first, second)

    def scale(i, _):
        dm = d[i + 2, LO:HI]
        for c in range(2):
            u[c, i + 2, LO:HI] = dm * f[c, i]
        return 0

    lax.fori_loop(0, ROWS, scale, 0)
    for at, x in ((par * 6, od), (6 - par * 6, ev)):
        dm = d[pl.ds(at, 2), LO:HI]
        for c in range(2):
            u[c, pl.ds(at, 2), LO:HI] = dm * x[c]
    for c in range(2):
        for n in range(4):
            u[c, 2 + n, LO - 2 : LO] = d[2 + n, LO - 2 : LO] * lo[7 * n + 3 + 2 * c : 7 * n + 5 + 2 * c]
            u[c, 2 + n, HI : HI + 2] = d[2 + n, HI : HI + 2] * hi[7 * n + 3 + 2 * c : 7 * n + 5 + 2 * c]
        for r, at in ((1, 30), (6, 34)):
            u[c, r, LO - 1 : LO] = d[r, LO - 1 : LO] * lo[at + c : at + c + 1]
            u[c, r, HI : HI + 1] = d[r, HI : HI + 1] * hi[at + c : at + c + 1]

    def first(r, _):
        vm = v[r + 1]
        fy = vm + pltpu.roll(vm, FRAME - 1, 0)
        fxp, fxm = vm + v[r + 2], vm + v[r]
        fzp, dm = fz[r], d[r]
        for c in range(2):
            x = u[c, r]
            y = fy * pltpu.roll(x, FRAME - 1, 0) + pltpu.roll(fy * x, 1, 0)
            y = y + fxp * u[c, r + 1] + fxm * u[c, r - 1]
            y = y + fzp * up_z(x) + down_z(fzp * x)
            t[c, r] = E1 * x + E2 * (dm * y)
        return 0

    lax.fori_loop(1, 7, first, 0)

    def store(c, i, y):
        out[c, i] = E0 * u[c, i + 2, LO:HI] + y

    for i in range(ROWS):
        couple(i, v, d, fz, t, lambda c, y: store(c, i, y))


def couple(i, v, d, fz, t, done):
    own_rows = slice(LO, HI)
    above = slice(LO + 1, HI + 1)
    under = slice(LO - 1, HI - 1)
    r = i + 2
    vm = v[r + 1, own_rows]
    fyp = vm + v[r + 1, above]
    fym = vm + v[r + 1, under]
    fxp, fxm = vm + v[r + 2, own_rows], vm + v[r, own_rows]
    fzp, dm = fz[r, own_rows], d[r, own_rows]
    for c in range(2):
        x = t[c, r, own_rows]
        y = fyp * t[c, r, above] + fym * t[c, r, under]
        y = y + fxp * t[c, r + 1, own_rows] + fxm * t[c, r - 1, own_rows]
        y = y + fzp * up_z(x) + down_z(fzp * x)
        done(c, dm * y)


def velocity_kernel(basis, dots, onehot, h0, ex, ez, v, d, fz, forced, vel_hbm, press, vel, t, b, bz, sems):
    sums = jnp.sum(jnp.sum(dots[...], axis=0), axis=1, keepdims=True)
    gg, gh, hh, hkh = sums[0:1], sums[1:2], sums[2:3], sums[3:4]
    alpha0 = gg / gh
    fresh = gg - 2.0 * alpha0 * gh + alpha0 * alpha0 * hh
    beta = fresh / gg
    grow = 1.0 + beta
    alpha1 = fresh / (grow * grow * gh - 2.0 * grow * alpha0 * hh + alpha0 * alpha0 * hkh)
    on_g = alpha0 + alpha1 * grow
    on_h = alpha1 * alpha0
    grad = on_g * basis[0:16] - on_h * basis[16:32]
    b[...] = grad
    bz[0:16] = up_z(grad)
    bz[16:32] = down_z(grad)
    p = on_g * basis[32:40] - on_h * basis[40:48]
    press[...] = jnp.dot(
        p, onehot[...], precision=lax.Precision.HIGHEST, preferred_element_type=jnp.float32
    )[0:4]

    def first(r, _):
        h, exi, exm, ezi = h0[r], ex[r], ex[r - 1], ez[r]
        ezm = down_z(ezi)
        for c in range(2):
            at = 8 * c + r
            y = h * b[pl.ds(at, 1)] + exi * b[pl.ds(at + 1, 1)] + exm * b[pl.ds(at - 1, 1)]
            t[c, r] = y + ezi * bz[pl.ds(at, 1)] + ezm * bz[pl.ds(16 + at, 1)]
        return 0

    lax.fori_loop(1, 7, first, 0)

    def store(c, i, y):
        own = E0 * (d[i + 2, LO:HI] * b[pl.ds(8 * c + i + 2, 1)])
        vel[c, i] = forced[c, i] - (own + y)

    saves = []
    for i in range(ROWS):
        couple(i, v, d, fz, t, lambda c, y: store(c, i, y))
        saves.append(pltpu.make_async_copy(vel.at[:, i], vel_hbm.at[:, i], sems.at[i]))
        saves[-1].start()
    for copy in saves:
        copy.wait()


VMEM = pl.BlockSpec(memory_space=pltpu.VMEM)
SMEM = pl.BlockSpec(memory_space=pltpu.SMEM)
ANY = pl.BlockSpec(memory_space=pl.ANY)
HBM = pl.BlockSpec(memory_space=pltpu.HBM)


def call(kernel, out_shape, scratch, args, in_specs, out_specs=None, micros=1.0, sems=0, mib=16, aliases={}):
    return pl.pallas_call(
        kernel,
        out_shape=out_shape,
        in_specs=in_specs,
        out_specs=out_specs or jax.tree.map(lambda _: VMEM, out_shape),
        scratch_shapes=[pltpu.VMEM(s, jnp.float32) for s in scratch]
        + ([pltpu.SemaphoreType.DMA((sems,))] if sems else []),
        input_output_aliases=aliases,
        compiler_params=pltpu.CompilerParams(vmem_limit_bytes=mib * 1024 * 1024),
        cost_estimate=pl.CostEstimate(flops=0, transcendentals=0, bytes_accessed=int(micros * 3.6e6)),
    )(*args)


def in_vmem(x):
    return pltpu.with_memory_space_constraint(x, pltpu.VMEM)


def in_hbm(x):
    return pltpu.with_memory_space_constraint(x, pltpu.HBM)


def f32(*shape):
    return jax.ShapeDtypeStruct(shape, jnp.float32)


def pairs(n, first):
    up = [(i, i + 1) for i in range(first, n - 1, 2)]
    return up + [(b, a) for a, b in up]


def shards(forcing, viscosity, owner_slot):
    slabs, cross = lax.axis_size("slab"), lax.axis_size("cross")
    slab = lax.axis_index("slab")
    par = slab % 2
    where = jnp.stack([par, slab // 2, lax.axis_index("cross") % 2, slab // 2 % 2]).astype(jnp.int32)
    mates, others = pairs(slabs, 0), pairs(slabs, 1)
    chips = slabs // 2
    first_chips = [(2 * a + c, 2 * b + c) for a, b in pairs(chips, 0) for c in range(2)]
    second_chips = [(2 * a + c, 2 * b + c) for a, b in pairs(chips, 1) for c in range(2)]

    edges, own, three, f = call(
        edge_kernel,
        (
            pltpu.VMEM((ROWS, 14, NZ), jnp.float32),
            pltpu.VMEM((ROWS, NY + 8, NZ), jnp.float32),
            pltpu.VMEM((3, NY + 8, NZ), jnp.float32),
            pltpu.VMEM(forcing.shape, jnp.float32),
        ),
        [],
        (where, in_hbm(viscosity), in_hbm(forcing)),
        in_specs=[SMEM, ANY, ANY],
        sems=3,
        mib=4,
    )
    od = lax.ppermute(three, "slab", others)
    ev = lax.ppermute(own, "slab", mates)
    layers = pltpu.VMEM((2, 2, NY, NZ), jnp.float32)
    to_od, to_ev = call(
        pack_kernel,
        (layers, layers),
        [],
        (where, in_vmem(f), in_vmem(three)),
        in_specs=[SMEM, VMEM, VMEM],
        micros=4,
        sems=2,
        mib=2,
    )
    od_f = lax.ppermute(to_od, "slab", others)
    ev_f = lax.ppermute(to_ev, "slab", mates)
    rows = pltpu.VMEM((40, NZ), jnp.float32)
    first, second = call(
        corner_kernel,
        (rows, rows),
        [(40, NZ), (40, NZ), (ROWS, 14, NZ), (3, 14, NZ)],
        (where, in_vmem(edges), in_vmem(od), in_vmem(ev)),
        in_specs=[SMEM] + [VMEM] * 3,
        mib=4,
    )
    first = lax.ppermute(first, "cross", pairs(cross, 0))
    second = lax.ppermute(second, "cross", pairs(cross, 1))

    kept = (f32(10, FRAME, NZ), f32(8, FRAME, NZ), f32(8, FRAME, NZ)) + (f32(7, FRAME, NZ),) * 3
    part, v, d, fz, h0, ex, ez = call(
        stencil_kernel,
        (f32(10, 4, NZ), *[pltpu.VMEM(x.shape, x.dtype) for x in kept]),
        [(7, FRAME, NZ), (5, 2, 8, 8, NZ), (7, ROWS, 8, NZ)],
        (where, in_vmem(own), in_vmem(od), in_vmem(ev), in_vmem(first), in_vmem(second), in_vmem(f)),
        in_specs=[SMEM] + [VMEM] * 6,
        micros=6,
        sems=5,
        mib=8,
    )

    width = owner_slot.shape[0] // cross
    column = lax.axis_index("cross") * width + jnp.arange(width, dtype=jnp.int32)
    onehot = (owner_slot[:, None] == column[None, :]).astype(jnp.float32)

    def among(x, step):
        return [lax.ppermute(x, "cross", [(i, i ^ (n * step)) for i in range(cross)]) for n in (1, 2, 3)]

    part, onehot = lax.optimization_barrier((part, onehot))
    got = among(part, 1)
    part = part + got[0] + got[1] + got[2]
    got = among(part, 4)
    forced = call(
        forced_kernel,
        pltpu.VMEM((2, ROWS, NY, NZ), jnp.float32),
        [(2, 8, FRAME, NZ)] * 2,
        (where, in_vmem(f), in_vmem(od_f), in_vmem(ev_f), in_vmem(first), in_vmem(second), in_vmem(v), in_vmem(d), in_vmem(fz)),
        in_specs=[SMEM] + [VMEM] * 8,
        micros=5,
        mib=8,
    )
    got, forced = lax.optimization_barrier((got, forced))
    part = part + got[0] + got[1] + got[2]

    near = (lax.ppermute(part, "slab", first_chips), lax.ppermute(part, "slab", second_chips))
    crossed = lax.ppermute(jnp.stack([*near, part]), "slab", mates)
    basis, dots = call(
        krylov_kernel,
        (f32(48, NZ), f32(chips, 8, 128)),
        [(7, 24, NZ), (40, NZ)],
        (where, part, *near, crossed),
        in_specs=[SMEM] + [VMEM] * 4,
        mib=4,
    )
    groups = [[2 * z + c for z in range(chips)] for c in range(2)]
    dots = lax.all_to_all(dots, "slab", 0, 0, tiled=True, axis_index_groups=groups)

    return call(
        velocity_kernel,
        (pltpu.HBM((2, ROWS, NY, NZ), jnp.float32), f32(ROWS, width)),
        [(2, ROWS, NY, NZ), (2, 8, FRAME, NZ), (16, NZ), (32, NZ)],
        (basis, dots, onehot, *[in_vmem(x) for x in (h0, ex, ez, v, d, fz, forced)]),
        in_specs=[VMEM] * 10,
        out_specs=(HBM, VMEM),
        micros=4,
        sems=4,
        mib=8,
    )


def solution(mesh):
    in_specs = (P(None, "slab", "cross", None), P("slab", "cross", None), P())
    out_specs = (P(None, "slab", "cross", None), P("slab", "cross"))
    return jax.shard_map(shards, mesh=mesh, in_specs=in_specs, out_specs=out_specs, check_vma=False)
```

```python
import functools

import jax
import jax.numpy as jnp
from jax import lax
from jax.experimental import pallas as pl
from jax.experimental.pallas import tpu as pltpu
from jax.sharding import PartitionSpec as P

OUTER = 2
DEGREE = 3
cheb_theta = 1.025
cheb_delta = 0.975


def series():
    sigma = cheb_theta / cheb_delta
    rho0 = 1.0 / sigma
    rho1 = 1.0 / (2.0 * sigma - rho0)
    rho2 = 1.0 / (2.0 * sigma - rho1)
    g1, g2 = 2.0 * rho1 / cheb_delta, 2.0 * rho2 / cheb_delta
    p0, p1 = (1.0 + rho1 * rho0) / cheb_theta + g1, -g1 / cheb_theta
    q = rho2 * rho1
    c0 = (1.0 + q) * p0 - q / cheb_theta + g2
    c1 = (1.0 + q) * p1 - g2 * p0
    c2 = -g2 * p1
    return c0 + c1 + c2, -c1 - 2.0 * c2, c2


E0, E1, E2 = (2.0 * e for e in series())

NY, NZ = 64, 512
ROWS = 4
FRAME = 80
LO, HI = 8, 72
FORWARD = ((0, 0), (0, 1), (0, 2), (1, -1), (1, 0), (1, 1), (2, 0))
PAYLOAD = 40


def up_z(x):
    return pltpu.roll(x, NZ - 1, x.ndim - 1)


def down_z(x):
    return pltpu.roll(x, 1, x.ndim - 1)


def lane(shape):
    return lax.broadcasted_iota(jnp.int32, shape, len(shape) - 1)


def edge_kernel(par_ref, own_hbm, f_hbm, out, bundle, three, f, sems):
    par = par_ref[0]
    own = bundle.at[:, 0:NY]
    extra = pltpu.make_async_copy(own_hbm.at[pl.ds(par, 3)], three.at[:, 0:NY], sems.at[2])
    extra.start()
    copies = [pltpu.make_async_copy(own_hbm, own, sems.at[0]), pltpu.make_async_copy(f_hbm, f, sems.at[1])]
    for copy in copies:
        copy.start()
    copies[0].wait()
    out[:, 0:3] = bundle[:, 0:3]
    out[:, 7:10] = bundle[:, NY - 3 : NY]
    copies[1].wait()
    for c in range(2):
        low, high = f[c, :, 0:2], f[c, :, NY - 2 : NY]
        out[:, 3 + 2 * c : 5 + 2 * c] = low
        out[:, 10 + 2 * c : 12 + 2 * c] = high
        bundle[:, NY + 2 * c : NY + 2 * c + 2] = low
        bundle[:, NY + 4 + 2 * c : NY + 6 + 2 * c] = high
        three[:, NY + 2 * c : NY + 2 * c + 2] = f[c, pl.ds(par, 3), 0:2]
        three[:, NY + 4 + 2 * c : NY + 6 + 2 * c] = f[c, pl.ds(par, 3), NY - 2 : NY]
    extra.wait()


def pack_kernel(par_ref, f, ev, to_od, to_ev, sems):
    par = par_ref[0]
    copies = [
        pltpu.make_async_copy(f.at[:, pl.ds(2 * last, 2)], out, sems.at[n])
        for n, (out, last) in enumerate(((to_od, par), (to_ev, 1 - par)))
    ]
    for copy in copies:
        copy.start()
    for copy in copies:
        copy.wait()


def corner_kernel(par_ref, own, od, ev, first, second, low, high, mate, other):
    odd = par_ref[0] == 1
    for rows, x in ((mate, ev), (other, od)):
        rows[:, 0:3] = x[:, 0:3]
        rows[:, 3:7] = x[:, NY : NY + 4]
        rows[:, 7:10] = x[:, NY - 3 : NY]
        rows[:, 10:14] = x[:, NY + 4 : NY + 8]
    below = lax.select(odd, mate[2:4], other[1:3])
    above = lax.select(odd, other[0:2], mate[0:2])
    for out, near, forced, base in ((low, (0, 2), 0, 0), (high, (1, 3), 1, 7)):
        for n in range(4):
            out[7 * n : 7 * n + 7] = own[n, base : base + 7]
        for at, x, far, far_at in ((28, below[1], below[0], 36), (32, above[0], above[1], 37)):
            out[at : at + 2] = x[base + near[0] : base + near[1]]
            for c in range(2):
                row = base + 3 + 2 * c + forced
                out[at + 2 + c : at + 3 + c] = x[row : row + 1]
            row = base + 2 * forced
            out[far_at : far_at + 1] = far[row : row + 1]
        out[38:40] = jnp.zeros((2, NZ), jnp.float32)
    odd = par_ref[2] == 1
    first[...] = lax.select(odd, low[...], high[...])
    second[...] = lax.select(odd, high[...], low[...])


def sides(odd, first, second):
    return lax.select(odd, first[...], second[...]), lax.select(odd, second[...], first[...])


def fill_viscosity(par, v, own, od, ev, lo, hi, sems):
    copies = [pltpu.make_async_copy(own.at[:, 0:NY], v.at[3:7, LO:HI], sems.at[0])]
    for n, at, last, x in ((1, par * 7, 0, od), (2, 7 - par * 7, par, ev)):
        copies.append(pltpu.make_async_copy(x.at[pl.ds(last, 3), 0:NY], v.at[pl.ds(at, 3), LO:HI], sems.at[n]))
    for copy in copies:
        copy.start()
    for n in range(4):
        v[3 + n, LO - 3 : LO] = lo[7 * n : 7 * n + 3]
        v[3 + n, HI : HI + 3] = hi[7 * n : 7 * n + 3]
    for r, at in ((2, 28), (7, 32)):
        v[r, LO - 2 : LO] = lo[at : at + 2]
        v[r, HI : HI + 2] = hi[at : at + 2]
    for r, at in ((1, 36), (8, 37)):
        v[r, LO - 1 : LO] = lo[at : at + 1]
        v[r, HI : HI + 1] = hi[at : at + 1]
    for copy in copies:
        copy.wait()


def fill_inverse(v, d, fz):
    ids = lane((FRAME, NZ))

    def layer(r, _):
        mid = v[r + 1]
        nxt = jnp.where(ids == NZ - 1, 0.0, up_z(mid))
        prv = jnp.where(ids == 0, 0.0, down_z(mid))
        total = 6.0 * mid + v[r] + v[r + 2] + nxt + prv
        total = total + pltpu.roll(mid, 1, 0) + pltpu.roll(mid, FRAME - 1, 0)
        d[r] = jnp.where(mid > 0.0, 1.0 / total, 0.0)
        fz[r] = jnp.where(ids == NZ - 1, 0.0, mid + nxt)
        return 0

    lax.fori_loop(0, 8, layer, 0)


def stencil_kernel(par_ref, own, od, ev, first, second, f, out, v, d, fz, h0, ex, ez, ezm, acc, s_acc, sems):
    par = par_ref[0]
    lo, hi = sides(par_ref[2] == 1, first, second)
    fill_viscosity(par, v, own, od, ev, lo, hi, sems)
    fill_inverse(v, d, fz)

    ex[0] = E2 * d[0] * (v[1] + v[2]) * d[1]

    def edges(r, _):
        dm, vm = d[r], v[r + 1]
        ex[r] = E2 * dm * (vm + v[r + 2]) * d[r + 1]
        dy = pltpu.roll(dm, FRAME - 1, 0)
        ey = E2 * dm * (vm + pltpu.roll(vm, FRAME - 1, 0)) * dy
        h0[r] = E1 * dm + ey + pltpu.roll(ey, 1, 0)
        e = E2 * dm * fz[r] * up_z(dm)
        ez[r] = e
        ezm[r] = down_z(e)
        return 0

    lax.fori_loop(1, 7, edges, 0)

    acc[...] = jnp.zeros_like(acc)
    own_rows = slice(LO, HI)
    above = slice(LO + 1, HI + 1)
    under = slice(LO - 1, HI - 1)

    def layer(i, _):
        r = i + 2
        vm = v[r + 1, own_rows]
        fyp = vm + v[r + 1, above]
        fym = vm + v[r + 1, under]
        fxp = vm + v[r + 2, own_rows]
        fxm = vm + v[r, own_rows]
        fzp = fz[r, own_rows]
        fzm = down_z(fzp)
        dm = d[r, own_rows]
        u0, u1 = dm * f[0, i], dm * f[1, i]

        def fold(x):
            return jnp.sum(x.reshape(8, 8, NZ), axis=0)

        def weigh(di, dk, s):
            for c, u in ((0, u0), (1, u1)):
                at = i + di + 2
                acc[dk + 2, c, at] = acc[dk + 2, c, at] + fold(u * s)
            if (di, dk) in FORWARD:
                s_acc[FORWARD.index((di, dk)), i] = fold(dm * s)

        exi, exm = ex[r, own_rows], ex[r - 1, own_rows]
        ezi, ezmi = ez[r, own_rows], ezm[r, own_rows]
        h = h0[r, own_rows]
        weigh(
            0,
            0,
            E0
            + fyp * h0[r, above]
            + fym * h0[r, under]
            + fxp * exi
            + fxm * exm
            + fzp * ezi
            + fzm * ezmi,
        )
        weigh(1, 0, fyp * ex[r, above] + fym * ex[r, under] + fxp * h0[r + 1, own_rows])
        weigh(-1, 0, fyp * ex[r - 1, above] + fym * ex[r - 1, under] + fxm * h0[r - 1, own_rows])
        weigh(0, 1, fyp * ez[r, above] + fym * ez[r, under] + fzp * up_z(h))
        weigh(0, -1, fyp * ezm[r, above] + fym * ezm[r, under] + fzm * down_z(h))
        weigh(2, 0, fxp * ex[r + 1, own_rows])
        weigh(-2, 0, fxm * ex[r - 2, own_rows])
        weigh(0, 2, fzp * up_z(ezi))
        weigh(0, -2, fzm * down_z(ezmi))
        weigh(1, 1, fxp * ez[r + 1, own_rows] + fzp * up_z(exi))
        weigh(1, -1, fxp * ezm[r + 1, own_rows] + fzm * down_z(exi))
        weigh(-1, 1, fxm * ez[r - 1, own_rows] + fzp * up_z(exm))
        weigh(-1, -1, fxm * ezm[r - 1, own_rows] + fzm * down_z(exm))
        return 0

    lax.fori_loop(0, ROWS, layer, 0)

    for n in range(7):
        out[n] = jnp.sum(s_acc[n], axis=1)

    def columns(c):
        total = jnp.sum(acc[2, c], axis=1)
        for dk in (-2, -1, 1, 2):
            total = total + pltpu.roll(jnp.sum(acc[dk + 2, c], axis=1), dk % NZ, 1)
        return jnp.concatenate([total, jnp.zeros((8, NZ), jnp.float32)], 0)

    cx, cz = columns(0), columns(1)
    zero = lane((16, NZ)) == 0
    e = cx - pltpu.roll(cx, 1, 0) + cz - jnp.where(zero, 0.0, down_z(cz))
    out[7:9] = e[0:8].reshape(2, 4, NZ)
    out[9, 0:1] = e[8:9]
    out[9, 1:4] = jnp.zeros((3, NZ), jnp.float32)


def krylov_kernel(par_ref, mine, first, second, crossed, basis, dots, s_ref, g_ref):
    par, chip = par_ref[0], par_ref[1]
    odd = par == 1

    def pair(a, b):
        return lax.select(odd, b, a), lax.select(odd, a, b)

    slabs = []
    high = par_ref[3] == 1
    below, above = sides(high, first, second)
    below_mate, above_mate = sides(high, crossed.at[0], crossed.at[1])
    for a, b in ((below, below_mate), (mine[...], crossed[2]), (above, above_mate)):
        slabs += pair(a, b)
    W = 24
    g_ref[...] = jnp.zeros_like(g_ref)
    for n, slab in enumerate(slabs):
        for o in range(7):
            s_ref[o, 4 * n : 4 * n + 4] = slab[o]
        flat = slab[7:10].reshape(12, NZ)[0:9]
        at = 8 + 4 * n - 2
        g_ref[at : at + 9] = g_ref[at : at + 9] + flat
    ids = lane((W, NZ))
    layer = lax.broadcasted_iota(jnp.int32, (W, NZ), 0) - 8 + 8 * chip
    inside = jnp.logical_and(layer >= 0, layer < 64)

    def next_layer(x, n=1):
        return pltpu.roll(x, (W - n) % W, 0)

    def shift(x, di, dk):
        if di:
            x = pltpu.roll(x, (-di) % W, 0)
        if dk:
            x = pltpu.roll(x, (-dk) % NZ, 1)
        return x

    def spread(q):
        qx = q - next_layer(q)
        qz = q - jnp.where(ids == NZ - 1, 0.0, up_z(q))
        return qx, qz

    def times_s(b):
        total = None
        for n, (di, dk) in enumerate(FORWARD):
            s = s_ref[n]
            if n == 0:
                total = s * b
            else:
                total = total + s * shift(b, di, dk) + shift(s * b, -di, -dk)
        return total

    g = jnp.where(inside, g_ref[8 : 8 + W], 0.0)
    gx, gz = spread(g)
    tx, tz = times_s(gx), times_s(gz)
    h = tx - pltpu.roll(tx, 1, 0) + tz - jnp.where(ids == 0, 0.0, down_z(tz))
    h = jnp.where(inside, h, 0.0)
    hx, hz = spread(h)
    energy = hx * times_s(hx) + hz * times_s(hz)

    def own(x):
        return lax.select(odd, pltpu.roll(x, W - 4, 0), x)

    for n, x in enumerate((gx, gz, hx, hz)):
        basis[8 * n : 8 * n + 8] = own(x)[6:14]
    basis[32:40] = own(g)[8:16]
    basis[40:48] = own(h)[8:16]
    rows = []
    for x in (g * g, g * h, h * h, energy):
        part = x[8:16]
        part = part[:, 0:128] + part[:, 128:256] + part[:, 256:384] + part[:, 384:512]
        rows.append(jnp.sum(part, axis=0, keepdims=True))
    packed = jnp.concatenate(rows + [jnp.zeros((4, 128), jnp.float32)], 0)
    dots[...] = jnp.broadcast_to(packed[None], dots.shape)


def forced_kernel(par_ref, f, od, ev, first, second, v, d, fz, out, u, t):
    par = par_ref[0]
    lo, hi = sides(par_ref[2] == 1, first, second)

    def scale(i, _):
        dm = d[i + 2, LO:HI]
        for c in range(2):
            u[c, i + 2, LO:HI] = dm * f[c, i]
        return 0

    lax.fori_loop(0, ROWS, scale, 0)
    for at, x in ((par * 6, od), (6 - par * 6, ev)):
        dm = d[pl.ds(at, 2), LO:HI]
        for c in range(2):
            u[c, pl.ds(at, 2), LO:HI] = dm * x[c]
    for c in range(2):
        for n in range(4):
            u[c, 2 + n, LO - 2 : LO] = d[2 + n, LO - 2 : LO] * lo[7 * n + 3 + 2 * c : 7 * n + 5 + 2 * c]
            u[c, 2 + n, HI : HI + 2] = d[2 + n, HI : HI + 2] * hi[7 * n + 3 + 2 * c : 7 * n + 5 + 2 * c]
        for r, at in ((1, 30), (6, 34)):
            u[c, r, LO - 1 : LO] = d[r, LO - 1 : LO] * lo[at + c : at + c + 1]
            u[c, r, HI : HI + 1] = d[r, HI : HI + 1] * hi[at + c : at + c + 1]

    def first(r, _):
        vm = v[r + 1]
        fy = vm + pltpu.roll(vm, FRAME - 1, 0)
        fxp, fxm = vm + v[r + 2], vm + v[r]
        fzp, dm = fz[r], d[r]
        for c in range(2):
            x = u[c, r]
            y = fy * pltpu.roll(x, FRAME - 1, 0) + pltpu.roll(fy * x, 1, 0)
            y = y + fxp * u[c, r + 1] + fxm * u[c, r - 1]
            y = y + fzp * up_z(x) + down_z(fzp * x)
            t[c, r] = E1 * x + E2 * (dm * y)
        return 0

    lax.fori_loop(1, 7, first, 0)

    def store(c, i, y):
        out[c, i] = E0 * u[c, i + 2, LO:HI] + y

    for i in range(ROWS):
        couple(i, v, d, fz, t, lambda c, y: store(c, i, y))


def couple(i, v, d, fz, t, done):
    own_rows = slice(LO, HI)
    above = slice(LO + 1, HI + 1)
    under = slice(LO - 1, HI - 1)
    r = i + 2
    vm = v[r + 1, own_rows]
    fyp = vm + v[r + 1, above]
    fym = vm + v[r + 1, under]
    fxp, fxm = vm + v[r + 2, own_rows], vm + v[r, own_rows]
    fzp, dm = fz[r, own_rows], d[r, own_rows]
    for c in range(2):
        x = t[c, r, own_rows]
        y = fyp * t[c, r, above] + fym * t[c, r, under]
        y = y + fxp * t[c, r + 1, own_rows] + fxm * t[c, r - 1, own_rows]
        y = y + fzp * up_z(x) + down_z(fzp * x)
        done(c, dm * y)


def velocity_kernel(basis, dots, onehot, h0, ex, ez, v, d, fz, forced, vel_hbm, press, vel, t, b, bz, sems):
    sums = jnp.sum(jnp.sum(dots[...], axis=0), axis=1, keepdims=True)
    gg, gh, hh, hkh = sums[0:1], sums[1:2], sums[2:3], sums[3:4]
    alpha0 = gg / gh
    fresh = gg - 2.0 * alpha0 * gh + alpha0 * alpha0 * hh
    beta = fresh / gg
    grow = 1.0 + beta
    alpha1 = fresh / (grow * grow * gh - 2.0 * grow * alpha0 * hh + alpha0 * alpha0 * hkh)
    on_g = alpha0 + alpha1 * grow
    on_h = alpha1 * alpha0
    grad = on_g * basis[0:16] - on_h * basis[16:32]
    b[...] = grad
    bz[0:16] = up_z(grad)
    bz[16:32] = down_z(grad)
    p = on_g * basis[32:40] - on_h * basis[40:48]
    press[...] = jnp.dot(
        p, onehot[...], precision=lax.Precision.HIGHEST, preferred_element_type=jnp.float32
    )[0:4]

    def first(r, _):
        h, exi, exm, ezi = h0[r], ex[r], ex[r - 1], ez[r]
        ezm = down_z(ezi)
        for c in range(2):
            at = 8 * c + r
            y = h * b[pl.ds(at, 1)] + exi * b[pl.ds(at + 1, 1)] + exm * b[pl.ds(at - 1, 1)]
            t[c, r] = y + ezi * bz[pl.ds(at, 1)] + ezm * bz[pl.ds(16 + at, 1)]
        return 0

    lax.fori_loop(1, 7, first, 0)

    def store(c, i, y):
        own = E0 * (d[i + 2, LO:HI] * b[pl.ds(8 * c + i + 2, 1)])
        vel[c, i] = forced[c, i] - (own + y)

    saves = []
    for i in range(ROWS):
        couple(i, v, d, fz, t, lambda c, y: store(c, i, y))
        saves.append(pltpu.make_async_copy(vel.at[:, i], vel_hbm.at[:, i], sems.at[i]))
        saves[-1].start()
    for copy in saves:
        copy.wait()


VMEM = pl.BlockSpec(memory_space=pltpu.VMEM)
SMEM = pl.BlockSpec(memory_space=pltpu.SMEM)
ANY = pl.BlockSpec(memory_space=pl.ANY)
HBM = pl.BlockSpec(memory_space=pltpu.HBM)


def call(kernel, out_shape, scratch, args, in_specs, out_specs=None, micros=1.0, sems=0, mib=16, aliases={}):
    return pl.pallas_call(
        kernel,
        out_shape=out_shape,
        in_specs=in_specs,
        out_specs=out_specs or jax.tree.map(lambda _: VMEM, out_shape),
        scratch_shapes=[pltpu.VMEM(s, jnp.float32) for s in scratch]
        + ([pltpu.SemaphoreType.DMA((sems,))] if sems else []),
        input_output_aliases=aliases,
        compiler_params=pltpu.CompilerParams(vmem_limit_bytes=mib * 1024 * 1024),
        cost_estimate=pl.CostEstimate(flops=0, transcendentals=0, bytes_accessed=int(micros * 3.6e6)),
    )(*args)


def in_vmem(x):
    return pltpu.with_memory_space_constraint(x, pltpu.VMEM)


def in_hbm(x):
    return pltpu.with_memory_space_constraint(x, pltpu.HBM)


def f32(*shape):
    return jax.ShapeDtypeStruct(shape, jnp.float32)


def pairs(n, first):
    up = [(i, i + 1) for i in range(first, n - 1, 2)]
    return up + [(b, a) for a, b in up]


def shards(forcing, viscosity, owner_slot):
    slabs, cross = lax.axis_size("slab"), lax.axis_size("cross")
    slab = lax.axis_index("slab")
    par = slab % 2
    where = jnp.stack([par, slab // 2, lax.axis_index("cross") % 2, slab // 2 % 2]).astype(jnp.int32)
    mates, others = pairs(slabs, 0), pairs(slabs, 1)
    chips = slabs // 2
    first_chips = [(2 * a + c, 2 * b + c) for a, b in pairs(chips, 0) for c in range(2)]
    second_chips = [(2 * a + c, 2 * b + c) for a, b in pairs(chips, 1) for c in range(2)]

    edges, own, three, f = call(
        edge_kernel,
        (
            pltpu.VMEM((ROWS, 14, NZ), jnp.float32),
            pltpu.VMEM((ROWS, NY + 8, NZ), jnp.float32),
            pltpu.VMEM((3, NY + 8, NZ), jnp.float32),
            pltpu.VMEM(forcing.shape, jnp.float32),
        ),
        [],
        (where, in_hbm(viscosity), in_hbm(forcing)),
        in_specs=[SMEM, ANY, ANY],
        sems=3,
        mib=4,
    )
    od = lax.ppermute(three, "slab", others)
    ev = lax.ppermute(own, "slab", mates)
    layers = pltpu.VMEM((2, 2, NY, NZ), jnp.float32)
    to_od, to_ev = call(
        pack_kernel,
        (layers, layers),
        [],
        (where, in_vmem(f), in_vmem(ev)),
        in_specs=[SMEM, VMEM, VMEM],
        micros=4,
        sems=2,
        mib=2,
    )
    od_f = lax.ppermute(to_od, "slab", others)
    ev_f = lax.ppermute(to_ev, "slab", mates)
    rows = pltpu.VMEM((40, NZ), jnp.float32)
    first, second = call(
        corner_kernel,
        (rows, rows),
        [(40, NZ), (40, NZ), (ROWS, 14, NZ), (3, 14, NZ)],
        (where, in_vmem(edges), in_vmem(od), in_vmem(ev)),
        in_specs=[SMEM] + [VMEM] * 3,
        mib=4,
    )
    first = lax.ppermute(first, "cross", pairs(cross, 0))
    second = lax.ppermute(second, "cross", pairs(cross, 1))

    kept = (f32(10, FRAME, NZ), f32(8, FRAME, NZ), f32(8, FRAME, NZ)) + (f32(7, FRAME, NZ),) * 3
    part, v, d, fz, h0, ex, ez = call(
        stencil_kernel,
        (f32(10, 4, NZ), *[pltpu.VMEM(x.shape, x.dtype) for x in kept]),
        [(7, FRAME, NZ), (5, 2, 8, 8, NZ), (7, ROWS, 8, NZ)],
        (where, in_vmem(own), in_vmem(od), in_vmem(ev), in_vmem(first), in_vmem(second), in_vmem(f)),
        in_specs=[SMEM] + [VMEM] * 6,
        micros=6,
        sems=5,
        mib=8,
    )

    width = owner_slot.shape[0] // cross
    column = lax.axis_index("cross") * width + jnp.arange(width, dtype=jnp.int32)
    onehot = (owner_slot[:, None] == column[None, :]).astype(jnp.float32)

    def among(x, step):
        return [lax.ppermute(x, "cross", [(i, i ^ (n * step)) for i in range(cross)]) for n in (1, 2, 3)]

    part, onehot = lax.optimization_barrier((part, onehot))
    got = among(part, 1)
    part = part + got[0] + got[1] + got[2]
    got = among(part, 4)
    forced = call(
        forced_kernel,
        pltpu.VMEM((2, ROWS, NY, NZ), jnp.float32),
        [(2, 8, FRAME, NZ)] * 2,
        (where, in_vmem(f), in_vmem(od_f), in_vmem(ev_f), in_vmem(first), in_vmem(second), in_vmem(v), in_vmem(d), in_vmem(fz)),
        in_specs=[SMEM] + [VMEM] * 8,
        micros=5,
        mib=8,
    )
    got, forced = lax.optimization_barrier((got, forced))
    part = part + got[0] + got[1] + got[2]

    near = (lax.ppermute(part, "slab", first_chips), lax.ppermute(part, "slab", second_chips))
    crossed = lax.ppermute(jnp.stack([*near, part]), "slab", mates)
    basis, dots = call(
        krylov_kernel,
        (f32(48, NZ), f32(chips, 8, 128)),
        [(7, 24, NZ), (40, NZ)],
        (where, part, *near, crossed),
        in_specs=[SMEM] + [VMEM] * 4,
        mib=4,
    )
    groups = [[2 * z + c for z in range(chips)] for c in range(2)]
    dots = lax.all_to_all(dots, "slab", 0, 0, tiled=True, axis_index_groups=groups)

    return call(
        velocity_kernel,
        (pltpu.HBM((2, ROWS, NY, NZ), jnp.float32), f32(ROWS, width)),
        [(2, ROWS, NY, NZ), (2, 8, FRAME, NZ), (16, NZ), (32, NZ)],
        (basis, dots, onehot, *[in_vmem(x) for x in (h0, ex, ez, v, d, fz, forced)]),
        in_specs=[VMEM] * 10,
        out_specs=(HBM, VMEM),
        micros=4,
        sems=4,
        mib=8,
    )


def solution(mesh):
    in_specs = (P(None, "slab", "cross", None), P("slab", "cross", None), P())
    out_specs = (P(None, "slab", "cross", None), P("slab", "cross"))
    return jax.shard_map(shards, mesh=mesh, in_specs=in_specs, out_specs=out_specs, check_vma=False)
```
